32 devices in a mesh: dp: 4 (over x, core), seq: 8 (over z, y).
Axes of the slice: x: 2, y: 2, z: 4, core: 2. Of those that a mesh axis runs over, the one named last changes fastest.
Arguments:
- tokens: bfloat16 [2, 4096, 1024], P(None, ('dp', 'seq')), may hold values from -6 to 6
- text_states: bfloat16 [128, 1024], replicated, may hold values from -6 to 6
- image_ids: int32 [2, 4096], P(None, ('dp', 'seq')), may hold values from 0 to 7, as said below
- text_segments: int32 [128], replicated, may hold values from 0 to 7, never falling along the last dimension, each value on 1 to 32 neighbouring positions
- image_caption: int32 [2, 8], replicated, may hold values from 0 to 7
- norm_gains: bfloat16 [3, 1024], P(None, ('dp', 'seq')), may hold values from 0.099609375 to 1.8984375
- norm_shifts: bfloat16 [3, 1024], P(None, ('dp', 'seq')), may hold values from -3 to 3
- self_qkv: bfloat16 [1024, 3072], P(('dp', 'seq')), may hold values from -0.25 to 0.25
- self_out: bfloat16 [1024, 1024], P(('dp', 'seq')), may hold values from -3 to 3
- cross_query: bfloat16 [1024, 1024], P(('dp', 'seq')), may hold values from -0.25 to 0.25
- cross_keyval: bfloat16 [1024, 2048], P(('dp', 'seq')), may hold values from -0.25 to 0.25
- cross_out: bfloat16 [1024, 1024], P(('dp', 'seq')), may hold values from -0.75 to 0.75
- mlp_up: bfloat16 [1024, 4096], P(('dp', 'seq')), may hold values from -0.1875 to 0.1875
- mlp_down: bfloat16 [4096, 1024], P(('dp', 'seq')), may hold values from -0.09375 to 0.09375
- cotangent: bfloat16 [2, 4096, 1024], P(None, ('dp', 'seq')), may hold values from -6 to 6
Outputs:
- output: bfloat16 [2, 4096, 1024], P(None, ('dp', 'seq'))
- grad_tokens: float32 [2, 4096, 1024], P(None, ('dp', 'seq'))
- grad_text: float32 [128, 1024], replicated
- grad_gains: float32 [3, 1024], P(None, ('dp', 'seq'))
- grad_shifts: float32 [2, 1024], P(None, ('dp', 'seq'))
- grad_self_qkv: float32 [1024, 3072], P(('dp', 'seq'))
- grad_self_out: float32 [1024, 1024], P(('dp', 'seq'))
- grad_cross_query: float32 [1024, 1024], P(('dp', 'seq'))
- grad_cross_keyval: float32 [1024, 2048], P(('dp', 'seq'))
- grad_cross_out: float32 [1024, 1024], P(('dp', 'seq'))
- grad_mlp_up: float32 [1024, 4096], P(('dp', 'seq'))
- grad_mlp_down: float32 [4096, 1024], P(('dp', 'seq'))
- grad_mlp_shift: float32 [1024], P(('dp', 'seq'))
The draws below stay inside these ranges and needn't reach their ends.
Inputs may be any that keep to these rules, and one draw needn't show every extreme that they name: `image_ids`: within each micro-batch, the 1024 tokens of group g are blocks of 64 rows; each run of 2 blocks in a row holds one block of every image of the group, the images g * 2 to (g + 1) * 2 - 1, so each image has 512 tokens. `text_segments`: caption numbers never fall along the text rows; every caption has one or more rows.
All inputs are finite; a program needn't handle non-finite values.
Results may differ from the reference program's by a relative error of at most 0.03.
Values may be sent and summed in bfloat16 or wider, within the bound.
No kernel may reach another device: no remote copies, remote signals or barrier semaphores. Data moves between devices by JAX's collectives and lax.ppermute only.
A program may use at most 384 MiB of HBM per device.

```python
import math
import jax
import jax.numpy as jnp
import numpy as np
from jax import lax

D = 1024
H = 16
DH = 64
FF = 4096
MB = 2
TXT = 128
CAPS = 8
STRIPE = 64
GROUP = 1024
PER_GROUP = 2
ROUNDS = 8
TOKENS = 4096
IMAGES = 8
N_DP = 4


def draw_image_ids(key, part):
    key = jax.random.fold_in(key, 11)
    groups = MB * N_DP
    subkeys = jax.random.split(key, groups * (ROUNDS - 1))

    def shuffle(subkey):
        return jax.random.permutation(subkey, PER_GROUP)
    orders = jax.vmap(shuffle)(subkeys).reshape(groups, ROUNDS - 1, PER_GROUP)
    closing = orders[:, :1, ::-1]
    blocks = jnp.concatenate([orders, closing], 1).reshape(groups, ROUNDS * PER_GROUP)
    local = jnp.repeat(blocks, STRIPE, axis=1)
    offset = PER_GROUP * (jnp.arange(groups, dtype=jnp.int32) % N_DP)
    return (local + offset[:, None]).reshape(MB, N_DP * GROUP).astype(jnp.int32)


def place_ends(result, rng, low, largest):
    index_at = [jax.random.randint(jax.random.fold_in(rng, axis), (), 0, length) for axis, length in enumerate(result.shape)]
    widest = result.shape.index(max(result.shape))
    next_to = index_at[:widest] + [(index_at[widest] + 1) % result.shape[widest]] + index_at[widest + 1:]
    return result.at[tuple(index_at)].set(low).at[tuple(next_to)].set(largest)


def steps_of(rng, extent, pieces, smallest, largest):
    def one(position, shards_of):
        heights = jax.random.uniform(jax.random.fold_in(jax.random.fold_in(rng, 6), position), (shards_of,), jnp.float32, smallest / len(pieces), largest / len(pieces))
        return jnp.repeat(jnp.exp(heights), extent[position] // shards_of).reshape((-1,) + (1,) * (len(extent) - position - 1))

    level = one(*pieces[0])
    for cut in pieces[1:]:
        level = level * one(*cut)
    return level


def split_up(count, total, bound, skew):
    weights = [(1 << 20) // math.isqrt(grade ** skew) + 1 for grade in range(2, count + 1)]
    rest, given = total - bound - (count - 1), [1] * (count - 1)
    while rest > 0:
        free = [i for i in range(count - 1) if given[i] < bound]
        whole, budget = sum([weights[i] for i in free]), rest
        for i in free:
            addition = min(bound - given[i], max(1, budget * weights[i] // whole), rest)
            given[i] = given[i] + addition
            rest = rest - addition
    return np.array([bound] + given)


def ragged_sizes(rng, count, total, limit, lean):
    if count == 2:
        one = jax.random.randint(rng, (), max(1, total - limit), min(limit, total - 1) + 1)
        return jnp.stack([one, total - one])
    sizes = jnp.asarray(split_up(count, total, limit, lean), jnp.int32)
    couples = (count - 1) // 2
    giver, taker = sizes[1:1 + 2 * couples:2], sizes[2:2 + 2 * couples:2]
    margin = jnp.minimum(giver - 1, limit - taker)
    shifted = jax.random.randint(jax.random.fold_in(rng, 1), (couples,), 0, 1 << 20) % (margin + 1)
    sizes = sizes.at[1:1 + 2 * couples:2].set(giver - shifted).at[2:2 + 2 * couples:2].set(taker + shifted)
    return sizes[jax.random.permutation(jax.random.fold_in(rng, 2), count)]


def centred(stream_key, dims, width, most, cuts=(), kind=jnp.bfloat16):
    values = jax.random.normal(stream_key, dims, jnp.float32) * width
    if len(cuts) > 0:
        values = steps_of(stream_key, dims, cuts, -0.22, 0.18) * values
    return jnp.clip(values, min=-most, max=most).astype(kind)


def setup_inputs(seed: int = 0) -> dict:
    key_list = jax.random.split(jax.random.key(seed), 16)
    tokens = centred(key_list[0], (MB, TOKENS, D), 1.0, 6.0, ((1, 32),))
    text_states = centred(key_list[1], (TXT, D), 1.0, 6.0)
    image_ids = draw_image_ids(jax.random.fold_in(key_list[15], 71), 0)
    text_segments = jnp.searchsorted(jnp.cumsum(ragged_sizes(key_list[3], CAPS, TXT, 2 * TXT // CAPS, 1)), jnp.arange(TXT), side="right").astype(jnp.int32)
    image_caption = place_ends(jax.random.randint(key_list[4], (MB, IMAGES), 0, CAPS), jax.random.fold_in(key_list[4], 1), 0, CAPS - 1).astype(jnp.int32)
    norm_gains = jnp.clip(1.0 + 0.18 * jax.random.normal(key_list[5], (3, D), jnp.float32), 0.099609375, 1.8984375).astype(jnp.bfloat16)
    norm_shifts = centred(key_list[6], (3, D), 0.5, 3.0, ((1, 32),))
    self_qkv = centred(key_list[7], (D, 3 * D), (D // 2) ** -0.5, 0.25, ((0, 32),))
    self_out = centred(key_list[8], (D, D), (max(D // 256, 1)) ** -0.5, 3.0, ((0, 32),))
    cross_query = centred(key_list[9], (D, D), (D // 2) ** -0.5, 0.25, ((0, 32),))
    cross_keyval = centred(key_list[10], (D, 2 * D), (D // 2) ** -0.5, 0.25, ((0, 32),))
    cross_out = centred(key_list[11], (D, D), (max(D // 16, 1)) ** -0.5, 0.75, ((0, 32),))
    mlp_up = centred(key_list[12], (D, FF), D ** -0.5, 0.1875, ((0, 32),))
    mlp_down = centred(key_list[13], (FF, D), FF ** -0.5, 0.09375, ((0, 32),))
    cotangent = centred(key_list[14], (MB, TOKENS, D), 1.0, 6.0, ((1, 32),))
    return {"tokens": tokens, "text_states": text_states, "image_ids": image_ids, "text_segments": text_segments, "image_caption": image_caption, "norm_gains": norm_gains, "norm_shifts": norm_shifts, "self_qkv": self_qkv, "self_out": self_out, "cross_query": cross_query, "cross_keyval": cross_keyval, "cross_out": cross_out, "mlp_up": mlp_up, "mlp_down": mlp_down, "cotangent": cotangent}


EPS = 1e-05
NEG = -1e+30
GELU_C = 0.7978845608028654
HIGH = lax.Precision.HIGHEST

@jax.custom_vjp
def low(v):
    return lax.optimization_barrier(v.astype(jnp.bfloat16)).astype(jnp.float32)

@jax.custom_vjp
def low_back(v):
    return v

def low_keep(v):
    return (low(v), None)

def low_pass(kept, grad):
    return (grad,)

def back_keep(v):
    return (v, None)

def back_low(kept, grad):
    return (low(grad),)
low.defvjp(low_keep, low_pass)
low_back.defvjp(back_keep, back_low)

def matmul(left, right):
    return jnp.dot(left, right, precision=HIGH)

def layer_norm(values, gain, shift):
    center = values - lax.optimization_barrier(jnp.mean(values, -1, keepdims=True))
    spread = lax.optimization_barrier(jnp.mean(center * center, -1, keepdims=True))
    return center * lax.rsqrt(spread + EPS) * gain + shift

def gelu_tanh(values):
    return 0.5 * values * (1.0 + jnp.tanh(GELU_C * (values + 0.044715 * values * values * values)))

def masked_softmax(scores, allowed):
    scores = jnp.where(allowed, scores, NEG)
    top = lax.optimization_barrier(jnp.max(scores, -1, keepdims=True))
    raised = jnp.where(allowed, jnp.exp(scores - top), 0.0)
    return raised / lax.optimization_barrier(jnp.sum(raised, -1, keepdims=True))

def self_block(block, keys, values, ids):
    queries, block_ids, start = block
    rows = queries.shape[0]
    scores = jnp.einsum('qhd,khd->hqk', queries, keys, precision=HIGH) * DH ** (-0.5)
    scores = low_back(scores)
    query_pos = start + jnp.arange(rows, dtype=jnp.int32)
    key_pos = jnp.arange(keys.shape[0], dtype=jnp.int32)
    allowed = (key_pos[None, :] <= query_pos[:, None]) & (ids[None, :] == block_ids[:, None])
    probs = low(masked_softmax(scores, allowed[None]))
    return jnp.einsum('hqk,khd->qhd', probs, values, precision=HIGH).reshape(rows, H * DH)

def self_attention(qkv, ids):
    length = qkv.shape[0]
    queries = qkv[:, :D].reshape(length, H, DH)
    keys = qkv[:, D:2 * D].reshape(length, H, DH)
    values = qkv[:, 2 * D:].reshape(length, H, DH)
    size = math.gcd(length, 512)
    count = length // size
    blocks = (queries.reshape(count, size, H, DH), ids.reshape(count, size), jnp.arange(count, dtype=jnp.int32) * size)

    def one_block(block):
        return self_block(block, keys, values, ids)
    outs = lax.map(jax.checkpoint(one_block), blocks)
    return outs.reshape(length, D)

def cross_attention(cquery, cross_kv, caption, segments):
    length = cquery.shape[0]
    queries = cquery.reshape(length, H, DH)
    keys = cross_kv[:, :D].reshape(TXT, H, DH)
    values = cross_kv[:, D:].reshape(TXT, H, DH)
    scores = low_back(jnp.einsum('qhd,khd->hqk', queries, keys, precision=HIGH) * DH ** (-0.5))
    allowed = caption[:, None] == segments[None, :]
    probs = low(masked_softmax(scores, allowed[None]))
    return jnp.einsum('hqk,khd->qhd', probs, values, precision=HIGH).reshape(length, D)

def seq_layer(params, cross_kv, segments, inputs):
    gains, shifts, self_qkv, self_out, cross_query, cross_out, mlp_up, mlp_down = params
    resid, ids, caption = inputs
    norm_one = low(layer_norm(resid, gains[0], shifts[0]))
    qkv = low_back(low(matmul(norm_one, self_qkv)))
    attended = low_back(low(self_attention(qkv, ids)))
    hidden = resid + low_back(matmul(attended, self_out))
    norm_two = low(layer_norm(hidden, gains[1], shifts[1]))
    cquery = low_back(low(matmul(norm_two, cross_query)))
    crossed = low_back(low(cross_attention(cquery, cross_kv, caption, segments)))
    hidden = hidden + low_back(matmul(crossed, cross_out))
    norm_three = low(layer_norm(hidden, gains[2], shifts[2]))
    upward = low_back(matmul(norm_three, mlp_up))
    active = low(gelu_tanh(upward))
    return hidden + low_back(matmul(active, mlp_down))

def reference(tokens, text_states, image_ids, text_segments, image_caption, norm_gains, norm_shifts, self_qkv, self_out, cross_query, cross_keyval, cross_out, mlp_up, mlp_down, cotangent):
    ids_all = image_ids.reshape(MB * N_DP, GROUP)
    captions = jnp.take_along_axis(image_caption, image_ids, axis=1).reshape(MB * N_DP, GROUP)

    def forward(inputs, texts, gains, shifts, w_qkv, w_out, w_cq, w_ckv, w_co, w_up, w_down):
        cross_kv = low_back(low(matmul(texts, w_ckv)))
        params = (gains, shifts, w_qkv, w_out, w_cq, w_co, w_up, w_down)
        rows_in = inputs.reshape(MB * N_DP, GROUP, D)

        def step(carry, item):
            return (carry, jax.checkpoint(seq_layer)(params, cross_kv, text_segments, item))
        _, outs = lax.scan(step, None, (rows_in, ids_all, captions))
        return outs.reshape(MB, TOKENS, D)
    floats = (tokens, text_states, norm_gains, norm_shifts, self_qkv, self_out, cross_query, cross_keyval, cross_out, mlp_up, mlp_down)
    floats = tuple((item.astype(jnp.float32) for item in floats))
    primal, backward = jax.vjp(forward, *floats)
    grads = backward(cotangent.astype(jnp.float32))
    return (primal.astype(jnp.bfloat16), grads[0], grads[1], grads[2], grads[3][:2], grads[4], grads[5], grads[6], grads[7], grads[8], grads[9], grads[10], grads[3][2])
```

```python
import functools

import jax
import jax.numpy as jnp
from jax import lax
from jax.experimental import pallas as pl
from jax.experimental.pallas import tpu as pltpu
from jax.sharding import PartitionSpec as P

H = 16
STRIPE = 64
EPS = 1e-05
NEG = -1e30
GELU_C = 0.7978845608028654
BF = jnp.bfloat16
F32 = jnp.float32
AXES = ("dp", "seq")


def mm(left, right):
    return jnp.dot(left, right, preferred_element_type=F32)


def mm_rows(left, right):
    return lax.dot_general(left, right, (((0,), (0,)), ((), ())), preferred_element_type=F32)


def mm_cols(left, right):
    return lax.dot_general(left, right, (((1,), (1,)), ((), ())), preferred_element_type=F32)


def pick(array, dim, index):
    return lax.dynamic_index_in_dim(array, index, dim, keepdims=False)


class Grid:
    def __init__(self, dp, seq):
        self.dp, self.seq, self.t = dp, seq, seq // 8
        self.count = dp * seq
        me = lax.axis_index(AXES)
        part = lax.rem(me, seq)
        self.me = me
        self.x = me // (2 * seq)
        self.c = lax.rem(me // seq, 2)
        self.z = part // (2 * self.t)
        self.r = lax.rem(part // 2, self.t)
        self.y = lax.rem(part, 2)

    def coords(self, d):
        part = d % self.seq
        return (
            d // (2 * self.seq),
            d // self.seq % 2,
            part // (2 * self.t),
            part // 2 % self.t,
            part % 2,
        )

    def index(self, x, c, z, r, y):
        return (x * 2 + c) * self.seq + (z * self.t + r) * 2 + y

    def send(self, value, move):
        perm = [(d, self.index(*move(*self.coords(d)))) for d in range(self.count)]
        return lax.ppermute(value, AXES, perm)

    def over_c(self, value):
        return self.send(value, lambda x, c, z, r, y: (x, 1 - c, z, r, y))

    def over_x(self, value):
        return self.send(value, lambda x, c, z, r, y: (1 - x, c, z, r, y))

    def over_y(self, value):
        return self.send(value, lambda x, c, z, r, y: (x, c, z, r, 1 - y))

    def over_z(self, value, step):
        return self.send(value, lambda x, c, z, r, y: (x, c, (z + step) % 4, r, y))

    def xor_z(self, value, bit):
        return self.send(value, lambda x, c, z, r, y: (x, c, z ^ bit, r, y))

    def over_r(self, value, step):
        return self.send(value, lambda x, c, z, r, y: (x, c, z, (r + step) % self.t, y))

    def regroup(self, value, step):
        return self.send(value, lambda x, c, z, r, y: (x, y, (z + step) % 4, r, c))


def place(scalars, sources, shapes, copies):
    def kernel(s_ref, *refs):
        ins = refs[: len(sources)]
        outs = refs[len(sources) : len(sources) + len(shapes)]
        sems = refs[-1]
        started = []
        for i, (source, at, target, to) in enumerate(copies):
            copy = pltpu.make_async_copy(
                ins[source].at[at(s_ref)], outs[target].at[to(s_ref)], sems.at[i]
            )
            copy.start()
            started.append(copy)
        for copy in started:
            copy.wait()

    moved = sum(source.size * 2 for source in sources)
    return pl.pallas_call(
        kernel,
        out_shape=[jax.ShapeDtypeStruct(shape, BF) for shape in shapes],
        in_specs=[pl.BlockSpec(memory_space=pltpu.SMEM)]
        + [pl.BlockSpec(memory_space=pl.ANY)] * len(sources),
        out_specs=[pl.BlockSpec(memory_space=pl.ANY)] * len(shapes),
        scratch_shapes=[pltpu.SemaphoreType.DMA((len(copies),))],
        cost_estimate=pl.CostEstimate(flops=0, bytes_accessed=2 * moved, transcendentals=0),
    )(scalars, *sources)


ALL = slice(None)


def everything(s):
    return (ALL,)


def gather_xyz(g, scal, shard, widths):
    kinds, rows, _ = shard.shape
    other = g.over_x(shard)
    (pair,) = place(
        scal,
        [shard, other],
        [(2,) + shard.shape],
        [
            (0, everything, 0, lambda s: (s[0],)),
            (1, everything, 0, lambda s: (1 - s[0],)),
        ],
    )
    bufs = []
    for dy, block in ((0, pair), (1, g.over_y(pair))):
        low, high = g.over_z(block, 1), g.over_z(block, -1)
        far = g.over_z(low, 1) if dy == 0 else g.over_z(high, -1)
        bufs += [(block, 0, dy), (high, 1, dy), (far, 2, dy), (low, 3, dy)]
    shapes = [(2, kinds, 4, 2, rows, width) for width in widths]
    copies = []
    for i, (_, dz, dy) in enumerate(bufs):
        start = 0
        for o, width in enumerate(widths):
            copies.append(
                (
                    i,
                    lambda s, start=start, width=width: (ALL, ALL, ALL, pl.ds(start, width)),
                    o,
                    lambda s, dz=dz, dy=dy: (ALL, ALL, (s[2] + dz) & 3, s[3] ^ dy),
                )
            )
            start += width
    return place(scal, [b[0] for b in bufs], shapes, copies)


def gather_yxz(g, scal, shard, sections):
    _, rows, _ = shard.shape
    other = g.over_y(shard)
    (pair,) = place(
        scal,
        [shard, other],
        [(2,) + shard.shape],
        [
            (0, everything, 0, lambda s: (s[3],)),
            (1, everything, 0, lambda s: (1 - s[3],)),
        ],
    )
    bufs = []
    for dx, block in ((0, pair), (1, g.over_x(pair))):
        low, high = g.over_z(block, 1), g.over_z(block, -1)
        far = g.over_z(low, 1) if dx == 0 else g.over_z(high, -1)
        bufs += [(block, 0, dx), (high, 1, dx), (far, 2, dx), (low, 3, dx)]
    shapes = [(2, kinds, 4, 2, rows, width) for width, kinds in sections]
    copies = []
    for i, (_, dz, dx) in enumerate(bufs):
        start = 0
        for o, (width, kinds) in enumerate(sections):
            for kind in range(kinds):
                copies.append(
                    (
                        i,
                        lambda s, start=start, width=width: (ALL, 0, ALL, pl.ds(start, width)),
                        o,
                        lambda s, dz=dz, dx=dx, kind=kind: (s[0] ^ dx, kind, (s[2] + dz) & 3),
                    )
                )
                start += width
    return place(scal, [b[0] for b in bufs], shapes, copies)


def gather_z_first(g, scal, shard, order, step):
    kinds, rows, width = shard.shape
    low, high = g.over_z(shard, 1), g.over_z(shard, -1)
    far = g.over_z(low, 1) if step == 1 else g.over_z(high, -1)
    (line,) = place(
        scal,
        [shard, high, far, low],
        [(4,) + shard.shape],
        [(i, everything, 0, lambda s, i=i: ((s[2] + i) & 3,)) for i in range(4)],
    )
    bufs = []
    if order == "zxy":
        for dx, block in ((0, line), (1, g.over_x(line))):
            bufs += [(block, dx, 0), (g.over_y(block), dx, 1)]
    else:
        for dy, block in ((0, line), (1, g.over_y(line))):
            bufs += [(block, 0, dy), (g.over_x(block), 1, dy)]
    copies = []
    for i, (_, dx, dy) in enumerate(bufs):
        for kind in range(kinds):
            copies.append(
                (
                    i,
                    lambda s, kind=kind: (ALL, kind),
                    0,
                    lambda s, dx=dx, dy=dy, kind=kind: (s[0] ^ dx, kind, ALL, s[3] ^ dy),
                )
            )
    return place(scal, [b[0] for b in bufs], [(2, kinds, 4, 2, rows, width)], copies)[0]


def plus(*terms):
    total = terms[0].astype(F32)
    for term in terms[1:]:
        total = total + term.astype(F32)
    return total.astype(BF)


def reduce_z(g, part, dim, step):
    ahead = g.over_z(part((g.z + 2) & 3), step)
    near = g.over_z(plus(part((g.z + step) & 3), ahead), step)
    back = g.over_z(part((g.z - step) & 3), -step)
    return near, back


def reduce_pair(g, terms, dim, mine, over):
    gone = plus(*[pick(term, dim, 1 - mine) for term in terms])
    return [pick(term, dim, mine) for term in terms] + [over(gone)]


def scatter(g, grad, order, step):
    terms = [grad]
    dims = ["x", "k", "z", "y"]
    for axis in order:
        dim = dims.index(axis)
        if axis == "z":
            if len(terms) > 1:
                terms = [plus(*terms)]
            whole = terms[0]
            near, back = reduce_z(g, lambda i: pick(whole, dim, i), dim, step)
            terms = [pick(whole, dim, g.z), near, back]
        elif axis == "x":
            terms = reduce_pair(g, terms, dim, g.x, g.over_x)
        else:
            terms = reduce_pair(g, terms, dim, g.y, g.over_y)
        dims.pop(dim)
    return terms


def attn_fwd_kernel(z_ref, q_ref, k_ref, v_ref, o_ref, *, scale):
    z = z_ref[0]
    size = q_ref.shape[0] // 4
    starts = [pl.multiple_of(((z - h) & 3) * size, size) for h in range(4)]
    keys = jnp.concatenate([k_ref[pl.ds(s, size), :] for s in starts], 0)
    values = jnp.concatenate([v_ref[pl.ds(s, size), :] for s in starts], 0)
    first = lax.broadcasted_iota(jnp.int32, (size, 128), 1) < 64
    for j in range(4):
        span = (j + 1) * size
        q = q_ref[pl.ds(starts[j], size), :]
        row = lax.broadcasted_iota(jnp.int32, (size, span), 0) + j * size
        seen = lax.broadcasted_iota(jnp.int32, (size, span), 1) <= row
        outs = []
        for head in range(2):
            lanes = first if head == 0 else ~first
            qh = jnp.where(lanes, q, jnp.zeros_like(q))
            s = mm_cols(qh, keys[:span]) * scale
            s = jnp.where(seen, s, NEG)
            p = jnp.exp(s - jnp.max(s, -1, keepdims=True))
            total = jnp.sum(p, -1, keepdims=True)
            outs.append(mm(p.astype(BF), values[:span]) / total)
        o_ref[pl.ds(starts[j], size), :] = jnp.where(first, outs[0], outs[1]).astype(BF)


def attn_fwd(z, qkv, scale):
    rows, width = qkv.shape
    pairs = width // 3 // 128
    return pl.pallas_call(
        functools.partial(attn_fwd_kernel, scale=scale),
        grid=(pairs,),
        out_shape=jax.ShapeDtypeStruct((rows, width // 3), BF),
        in_specs=[
            pl.BlockSpec(memory_space=pltpu.SMEM),
            pl.BlockSpec((rows, 128), lambda i: (0, i)),
            pl.BlockSpec((rows, 128), lambda i: (0, pairs + i)),
            pl.BlockSpec((rows, 128), lambda i: (0, 2 * pairs + i)),
        ],
        out_specs=pl.BlockSpec((rows, 128), lambda i: (0, i)),
        compiler_params=pltpu.CompilerParams(vmem_limit_bytes=32 * 2**20),
        cost_estimate=pl.CostEstimate(
            flops=4 * rows * rows * width // 3,
            bytes_accessed=rows * width * 3,
            transcendentals=rows * rows * pairs * 2,
        ),
    )(z, qkv, qkv, qkv)


def attn_bwd_kernel(z_ref, q_ref, k_ref, v_ref, g_ref, d_ref, dk_ref, dv_ref, *, scale, pairs):
    z = z_ref[0]
    at = pl.program_id(0)
    size = q_ref.shape[0] // 4
    starts = [pl.multiple_of(((z - h) & 3) * size, size) for h in range(4)]
    keys = jnp.concatenate([k_ref[pl.ds(s, size), :] for s in starts], 0)
    values = jnp.concatenate([v_ref[pl.ds(s, size), :] for s in starts], 0)
    first = lax.broadcasted_iota(jnp.int32, (size, 128), 1) < 64
    dk_ref[...] = jnp.zeros_like(dk_ref)
    dv_ref[...] = jnp.zeros_like(dv_ref)
    for j in range(4):
        span = (j + 1) * size
        q = q_ref[pl.ds(starts[j], size), :]
        grad = g_ref[pl.ds(starts[j], size), :]
        row = lax.broadcasted_iota(jnp.int32, (size, span), 0) + j * size
        seen = lax.broadcasted_iota(jnp.int32, (size, span), 1) <= row
        outs = []
        for head in range(2):
            lanes = first if head == 0 else ~first
            qh = jnp.where(lanes, q, jnp.zeros_like(q))
            gh = jnp.where(lanes, grad, jnp.zeros_like(grad))
            s = mm_cols(qh, keys[:span]) * scale
            s = jnp.where(seen, s, NEG)
            p = jnp.exp(s - jnp.max(s, -1, keepdims=True))
            p = p / jnp.sum(p, -1, keepdims=True)
            dp = mm_cols(gh, values[:span])
            ds = (p * (dp - jnp.sum(p * dp, -1, keepdims=True))).astype(BF)
            dv_ref[0:span, :] += mm_rows(p.astype(BF), gh)
            dk_ref[0:span, :] += mm_rows(ds, qh)
            outs.append(mm(ds, keys[:span]))
        dq = jnp.where(first, outs[0], outs[1]) * scale
        d_ref[pl.ds(starts[j], size), pl.ds(pl.multiple_of(at * 128, 128), 128)] = dq.astype(BF)
    for j in range(4):
        rows = slice(j * size, (j + 1) * size)
        d_ref[pl.ds(starts[j], size), pl.ds(pl.multiple_of((at + pairs) * 128, 128), 128)] = (
            dk_ref[rows, :] * scale
        ).astype(BF)
        d_ref[pl.ds(starts[j], size), pl.ds(pl.multiple_of((at + 2 * pairs) * 128, 128), 128)] = (
            dv_ref[rows, :].astype(BF)
        )


def attn_bwd(z, qkv, grad, scale):
    rows, width = qkv.shape
    pairs = width // 3 // 128
    return pl.pallas_call(
        functools.partial(attn_bwd_kernel, scale=scale, pairs=pairs),
        grid=(pairs,),
        out_shape=jax.ShapeDtypeStruct((rows, width), BF),
        in_specs=[
            pl.BlockSpec(memory_space=pltpu.SMEM),
            pl.BlockSpec((rows, 128), lambda i: (0, i)),
            pl.BlockSpec((rows, 128), lambda i: (0, pairs + i)),
            pl.BlockSpec((rows, 128), lambda i: (0, 2 * pairs + i)),
            pl.BlockSpec((rows, 128), lambda i: (0, i)),
        ],
        out_specs=pl.BlockSpec((rows, width), lambda i: (0, 0)),
        scratch_shapes=[pltpu.VMEM((rows, 128), F32), pltpu.VMEM((rows, 128), F32)],
        compiler_params=pltpu.CompilerParams(vmem_limit_bytes=32 * 2**20),
        cost_estimate=pl.CostEstimate(
            flops=10 * rows * rows * width // 3,
            bytes_accessed=rows * width * 5,
            transcendentals=rows * rows * pairs * 2,
        ),
    )(z, qkv, qkv, qkv, grad)


def cross_probs(q, keys, lanes, seen, scale):
    qh = jnp.where(lanes, q, jnp.zeros_like(q))
    s = jnp.where(seen, mm_cols(qh, keys) * scale, NEG)
    p = jnp.where(seen, jnp.exp(s - jnp.max(s, -1, keepdims=True)), 0.0)
    return qh, p / jnp.sum(p, -1, keepdims=True)


def cross_fwd_kernel(cap_ref, seg_ref, q_ref, k_ref, v_ref, o_ref, *, scale):
    seen = seg_ref[...] == cap_ref[0]
    q, keys, values = q_ref[...], k_ref[...], v_ref[...]
    first = lax.broadcasted_iota(jnp.int32, q.shape, 1) < 64
    outs = []
    for head in range(2):
        _, p = cross_probs(q, keys, first if head == 0 else ~first, seen, scale)
        outs.append(mm(p.astype(BF), values))
    o_ref[...] = jnp.where(first, outs[0], outs[1]).astype(BF)


def cross_fwd(cap, seg, cq, ckv, scale):
    rows, width = cq.shape
    text = ckv.shape[0]
    pairs = width // 128
    return pl.pallas_call(
        functools.partial(cross_fwd_kernel, scale=scale),
        grid=(pairs,),
        out_shape=jax.ShapeDtypeStruct((rows, width), BF),
        in_specs=[
            pl.BlockSpec(memory_space=pltpu.SMEM),
            pl.BlockSpec((1, text), lambda i: (0, 0)),
            pl.BlockSpec((rows, 128), lambda i: (0, i)),
            pl.BlockSpec((text, 128), lambda i: (0, i)),
            pl.BlockSpec((text, 128), lambda i: (0, pairs + i)),
        ],
        out_specs=pl.BlockSpec((rows, 128), lambda i: (0, i)),
        compiler_params=pltpu.CompilerParams(vmem_limit_bytes=32 * 2**20),
        cost_estimate=pl.CostEstimate(
            flops=4 * rows * text * width,
            bytes_accessed=rows * width * 4,
            transcendentals=rows * text * pairs * 2,
        ),
    )(cap, seg, cq, ckv, ckv)


def cross_bwd_kernel(cap_ref, seg_ref, q_ref, k_ref, v_ref, g_ref, dq_ref, dk_ref, dv_ref, *, scale):
    seen = seg_ref[...] == cap_ref[0]
    q, keys, values, grad = q_ref[...], k_ref[...], v_ref[...], g_ref[...]
    first = lax.broadcasted_iota(jnp.int32, q.shape, 1) < 64
    outs = []
    for head in range(2):
        lanes = first if head == 0 else ~first
        qh, p = cross_probs(q, keys, lanes, seen, scale)
        gh = jnp.where(lanes, grad, jnp.zeros_like(grad))
        dp = mm_cols(gh, values)
        ds = (p * (dp - jnp.sum(p * dp, -1, keepdims=True))).astype(BF)
        dv = mm_rows(p.astype(BF), gh)
        dk = mm_rows(ds, qh) * scale
        if head == 0:
            dv_ref[...] = dv
            dk_ref[...] = dk
        else:
            dv_ref[...] += dv
            dk_ref[...] += dk
        outs.append(mm(ds, keys))
    dq_ref[...] = (jnp.where(first, outs[0], outs[1]) * scale).astype(BF)


def cross_bwd(cap, seg, cq, ckv, grad, scale):
    rows, width = cq.shape
    text = ckv.shape[0]
    pairs = width // 128
    return pl.pallas_call(
        functools.partial(cross_bwd_kernel, scale=scale),
        grid=(pairs,),
        out_shape=[
            jax.ShapeDtypeStruct((rows, width), BF),
            jax.ShapeDtypeStruct((text, width), F32),
            jax.ShapeDtypeStruct((text, width), F32),
        ],
        in_specs=[
            pl.BlockSpec(memory_space=pltpu.SMEM),
            pl.BlockSpec((1, text), lambda i: (0, 0)),
            pl.BlockSpec((rows, 128), lambda i: (0, i)),
            pl.BlockSpec((text, 128), lambda i: (0, i)),
            pl.BlockSpec((text, 128), lambda i: (0, pairs + i)),
            pl.BlockSpec((rows, 128), lambda i: (0, i)),
        ],
        out_specs=[
            pl.BlockSpec((rows, 128), lambda i: (0, i)),
            pl.BlockSpec((text, 128), lambda i: (0, i)),
            pl.BlockSpec((text, 128), lambda i: (0, i)),
        ],
        compiler_params=pltpu.CompilerParams(vmem_limit_bytes=32 * 2**20),
        cost_estimate=pl.CostEstimate(
            flops=10 * rows * text * width,
            bytes_accessed=rows * width * 6,
            transcendentals=rows * text * pairs * 2,
        ),
    )(cap, seg, cq, ckv, ckv, grad)


def long_masks(g, rows):
    slot = jnp.arange(rows, dtype=jnp.int32) // (2 * STRIPE)
    rest = jnp.arange(rows, dtype=jnp.int32) % (2 * STRIPE)

    def positions(r):
        return (((g.z - slot) % 4) * g.t + r) * (2 * STRIPE) + rest

    key_pos = jnp.concatenate([positions((g.r - q) % g.t) for q in range(g.t)])
    return key_pos[None, :] <= positions(g.r)[:, None]


def long_gather(g, value):
    return jnp.concatenate([value] + [g.over_r(value, q) for q in range(1, g.t)], 0)


def long_fwd(g, qkv, scale):
    rows, width = qkv.shape
    head = 64
    heads = width // 3 // head
    keyval = long_gather(g, qkv[:, width // 3 :])
    q = qkv[:, : width // 3].reshape(rows, heads, head)
    k = keyval[:, : width // 3].reshape(-1, heads, head)
    v = keyval[:, width // 3 :].reshape(-1, heads, head)
    seen = long_masks(g, rows)[None]
    s = jnp.einsum("qhd,khd->hqk", q, k, preferred_element_type=F32) * scale
    s = jnp.where(seen, s, NEG)
    p = jnp.exp(s - jnp.max(s, -1, keepdims=True))
    p = p / jnp.sum(p, -1, keepdims=True)
    out = jnp.einsum("hqk,khd->qhd", p.astype(BF), v, preferred_element_type=F32)
    return out.reshape(rows, width // 3).astype(BF), (q, k, v, p)


def long_bwd(g, saved, grad, scale):
    q, k, v, p = saved
    rows, heads, head = q.shape
    width = heads * head
    grad = grad.reshape(rows, heads, head)
    dv = jnp.einsum("hqk,qhd->khd", p.astype(BF), grad, preferred_element_type=F32)
    dp = jnp.einsum("qhd,khd->hqk", grad, v, preferred_element_type=F32)
    ds = (p * (dp - jnp.sum(p * dp, -1, keepdims=True))).astype(BF)
    dq = jnp.einsum("hqk,khd->qhd", ds, k, preferred_element_type=F32) * scale
    dk = jnp.einsum("hqk,qhd->khd", ds, q, preferred_element_type=F32) * scale
    both = jnp.concatenate([dk.reshape(-1, width), dv.reshape(-1, width)], 1)
    both = both.reshape(g.t, rows, 2 * width)
    total = both[0]
    for step in range(1, g.t):
        total = total + g.over_r(both[step], -step)
    return jnp.concatenate([dq.reshape(rows, width).astype(BF), total.astype(BF)], 1)


def normed(values):
    center = values - jnp.mean(values, -1, keepdims=True)
    spread = lax.rsqrt(jnp.mean(center * center, -1, keepdims=True) + EPS)
    return center * spread, spread


def norm_back(unit, spread, gain, grad):
    f = grad * gain
    added = spread * (
        f - jnp.mean(f, -1, keepdims=True) - unit * jnp.mean(f * unit, -1, keepdims=True)
    )
    return added, jnp.sum(grad * unit, 0), jnp.sum(grad, 0)


def column_halves(weight, groups, mine):
    rows, width = weight.shape
    parts = weight.reshape(rows, groups, 2, width // groups // 2)
    return (
        pick(parts, 2, mine).reshape(rows, width // 2),
        pick(parts, 2, 1 - mine).reshape(rows, width // 2),
    )


def two(g, mine, other, axis):
    first = jnp.where(g.c == 0, mine, other)
    second = jnp.where(g.c == 0, other, mine)
    return jnp.stack([first, second], axis)


def gather_fast(g, weights):
    gains, shifts, w_qkv, w_out, w_cq, w_ckv, w_co, w_up, w_down = weights
    scal = jnp.stack([g.x, g.c, g.z, g.y]).astype(jnp.int32)
    small = jnp.concatenate([gains, shifts], 0).T
    small = jnp.pad(small, ((0, 0), (0, 128 - small.shape[1])))
    mine, other = column_halves(w_qkv, 6, g.c)
    got = g.over_c(jnp.concatenate([other, small], 1))
    qkv = two(g, jnp.concatenate([mine, small], 1), got, 0)
    cq_mine, cq_other = column_halves(w_cq, 2, g.c)
    ckv_mine, ckv_other = column_halves(w_ckv, 4, g.c)
    up_mine, up_other = column_halves(w_up, 2, g.c)
    n_cq, n_ckv = cq_mine.shape[1], ckv_mine.shape[1]
    got = g.over_c(jnp.concatenate([cq_other, ckv_other, up_other], 1))
    cq = two(g, cq_mine, got[:, :n_cq], 0)
    ckv = two(g, ckv_mine, got[:, n_cq : n_cq + n_ckv], 0)
    up = two(g, up_mine, got[:, n_cq + n_ckv :], 0)
    misc = jnp.concatenate([w_out, w_co, cq[0], cq[1], ckv[0], ckv[1]], 1)[None]
    depth = w_out.shape[1]
    qkv_all, small_all = gather_xyz(g, scal, qkv, [mine.shape[1], 128])
    out_all, co_all, cq_all, ckv_all = gather_yxz(
        g, scal, misc, [(depth, 1), (depth, 1), (n_cq, 2), (n_ckv, 2)]
    )
    up_all = gather_z_first(g, scal, up, "zxy", 1)
    down_all = gather_z_first(g, scal, w_down[None], "zyx", -1)
    small_all = small_all.reshape(-1, 128)[:, :6].astype(F32).T

    def flat(array):
        return array.reshape(-1, array.shape[-1])

    return (small_all,) + tuple(
        flat(a) for a in (qkv_all, out_all, cq_all, ckv_all, co_all, up_all, down_all)
    )


def gather_plain(g, weights):
    gains, shifts, w_qkv, w_out, w_cq, w_ckv, w_co, w_up, w_down = weights
    small = lax.all_gather(jnp.concatenate([gains, shifts], 0), AXES, axis=1, tiled=True)

    def columns(weight, groups):
        whole = lax.all_gather(weight, AXES, axis=0, tiled=True)
        return column_halves(whole, groups, g.c)[0]

    def rows(weight):
        whole = lax.all_gather(weight, AXES, axis=0, tiled=True)
        parts = whole.reshape(2, 2, whole.shape[0] // 4, whole.shape[1])
        return pick(parts, 1, g.c).reshape(whole.shape[0] // 2, whole.shape[1])

    return (
        small.astype(F32),
        columns(w_qkv, 6),
        rows(w_out),
        columns(w_cq, 2),
        columns(w_ckv, 4),
        rows(w_co),
        columns(w_up, 2),
        rows(w_down),
    )


def join_columns(g, keep, got, groups):
    rows, width = keep.shape
    block = width // groups
    parts = two(g, keep.reshape(rows, groups, block), got.reshape(rows, groups, block), 2)
    return parts.reshape(rows, 2 * width)


def scatter_columns_plain(g, grad, groups):
    rows, width = grad.shape
    whole = join_columns(g, grad, jnp.zeros_like(grad), groups)
    return lax.psum_scatter(whole, AXES, scatter_dimension=0, tiled=True)


def scatter_rows_plain(g, grad):
    rows, width = grad.shape
    parts = grad.reshape(2, rows // 2, width)
    whole = two(g, parts, jnp.zeros_like(parts), 1).reshape(2 * rows, width)
    return lax.psum_scatter(whole, AXES, scatter_dimension=0, tiled=True)


def scatter_columns_fast(g, grad, rows, groups, order, step):
    width = grad.shape[1]
    terms = scatter(g, grad.astype(BF).reshape(2, 2, 4, 2, rows, width), order, step)
    gone = plus(*[pick(term, 0, 1 - g.c) for term in terms])
    got = g.over_c(gone)
    keep = sum(pick(term, 0, g.c).astype(F32) for term in terms)
    return join_columns(g, keep, got.astype(F32), groups)


def scatter_rows_fast(g, grad, rows, order, step):
    width = grad.shape[1]
    terms = scatter(g, grad.astype(BF).reshape(2, 1, 4, 2, rows, width), order, step)
    return sum(term[0].astype(F32) for term in terms)


def chip_sum(g, value):
    value = plus32(value, g.xor_z(value, 1))
    value = plus32(value, g.xor_z(value, 2))
    value = plus32(value, g.over_x(value))
    return plus32(value, g.over_y(value))


def plus32(a, b):
    return (a.astype(F32) + b.astype(F32)).astype(a.dtype)


def both_cores(g, part):
    low = part.astype(BF)
    return low.astype(F32) + g.over_c(low).astype(F32)


def local(
    tokens,
    text_states,
    image_ids,
    text_segments,
    image_caption,
    norm_gains,
    norm_shifts,
    self_qkv,
    self_out,
    cross_query,
    cross_keyval,
    cross_out,
    mlp_up,
    mlp_down,
    cotangent,
    *,
    dp,
    seq,
):
    g = Grid(dp, seq)
    fast = g.t == 1
    depth = tokens.shape[-1]
    scale = (depth // H) ** (-0.5)
    weights = (
        norm_gains,
        norm_shifts,
        self_qkv,
        self_out,
        cross_query,
        cross_keyval,
        cross_out,
        mlp_up,
        mlp_down,
    )

    start = image_ids[:, 0] & 1
    both = jnp.stack([tokens, cotangent], 2).reshape(4, STRIPE, 2 * depth)
    received = []
    for step in range(4):
        j = (g.z + step) & 3
        half = (j & 1) ^ start[j >> 1]
        received.append(g.regroup(pick(both, 0, (j >> 1) * 2 + half), step))
    mine = jnp.stack(received)
    held = two(g, mine, g.over_c(mine), 1).reshape(8 * STRIPE, 2, depth)
    resid = held[:, 0].astype(F32)
    cot = held[:, 1]

    (small, w_qkv, w_out, w_cq, w_ckv, w_co, w_up, w_down) = (
        gather_fast(g, weights) if fast else gather_plain(g, weights)
    )
    gain, shift = small[:3], small[3:]

    image = (g.x * 2 + g.y) * 2 + (g.z & 1)
    cap = image_caption[g.z >> 1, image].reshape(1)
    seg = text_segments.reshape(1, -1)
    slot = g.z.reshape(1).astype(jnp.int32)

    unit_one, spread_one = normed(resid)
    n_one = (unit_one * gain[0] + shift[0]).astype(BF)
    qkv = mm(n_one, w_qkv).astype(BF)
    if fast:
        attended = attn_fwd(slot, qkv, scale)
    else:
        attended, saved = long_fwd(g, qkv, scale)
    hidden_one = resid + both_cores(g, mm(attended, w_out))
    unit_two, spread_two = normed(hidden_one)
    n_two = (unit_two * gain[1] + shift[1]).astype(BF)
    cq = mm(n_two, w_cq).astype(BF)
    ckv = mm(text_states, w_ckv).astype(BF)
    crossed = cross_fwd(cap, seg, cq, ckv, scale)
    hidden_two = hidden_one + both_cores(g, mm(crossed, w_co))
    unit_three, spread_three = normed(hidden_two)
    n_three = (unit_three * gain[2] + shift[2]).astype(BF)
    up = mm(n_three, w_up)
    inner = jnp.tanh(GELU_C * (up + 0.044715 * up * up * up))
    act = (0.5 * up * (1.0 + inner)).astype(BF)

    def halves(value):
        parts = value.reshape(4, 2, STRIPE, value.shape[-1])
        return pick(parts, 1, g.c), pick(parts, 1, 1 - g.c)

    down = mm(act, w_down)
    keep, gone = halves(down)
    out = (halves(hidden_two)[0] + keep + g.over_c(gone.astype(BF)).astype(F32)).astype(BF)

    grad_down = mm_rows(act, cot)
    slope = 0.5 * (1.0 + inner) + 0.5 * up * (1.0 - inner * inner) * GELU_C * (
        1.0 + 3 * 0.044715 * up * up
    )
    d_up = (mm_cols(cot, w_down) * slope).astype(BF)
    grad_up = mm_rows(n_three, d_up)
    added, gain_three, shift_three = norm_back(
        unit_three, spread_three, gain[2], both_cores(g, mm_cols(d_up, w_up))
    )
    g_two = cot.astype(F32) + added
    d_cross = g_two.astype(BF)
    grad_co = mm_rows(crossed, d_cross)
    d_crossed = mm_cols(d_cross, w_co).astype(BF)
    d_cq, d_ck, d_cv = cross_bwd(cap, seg, cq, ckv, d_crossed, scale)
    grad_cq = mm_rows(n_two, d_cq)
    added, gain_two, shift_two = norm_back(
        unit_two, spread_two, gain[1], both_cores(g, mm_cols(d_cq, w_cq))
    )
    g_one = g_two + added
    d_self = g_one.astype(BF)
    grad_out = mm_rows(attended, d_self)
    d_att = mm_cols(d_self, w_out).astype(BF)
    d_qkv = attn_bwd(slot, qkv, d_att, scale) if fast else long_bwd(g, saved, d_att, scale)
    grad_qkv = mm_rows(n_one, d_qkv)
    added, gain_one, shift_one = norm_back(
        unit_one, spread_one, gain[0], both_cores(g, mm_cols(d_qkv, w_qkv))
    )
    grad_in = (g_one + added).astype(BF)

    def home(mine):
        back = jnp.stack([g.regroup(mine[step], -step) for step in range(4)])
        order = []
        for block in range(4):
            j = (block & 2) + ((block & 1) ^ start[block >> 1])
            order.append(pick(back, 0, (j - g.z) & 3))
        return jnp.stack(order).reshape(2, 2 * STRIPE, depth)

    output = home(out)
    grad_tokens = home(halves(grad_in)[0]).astype(F32)

    d_ckv = jnp.concatenate([d_ck, d_cv], 1)
    norms = jnp.stack([gain_one, gain_two, gain_three, shift_one, shift_two, shift_three])
    if fast:
        d_ckv = chip_sum(g, d_ckv.astype(BF))
        norms = chip_sum(g, norms)
        d_ckv_whole = join_columns(g, d_ckv, g.over_c(d_ckv), 4)
    else:
        whole = join_columns(g, d_ckv, jnp.zeros_like(d_ckv), 4)
        d_ckv_whole = lax.psum(whole, AXES).astype(BF)
        d_ckv = column_halves(d_ckv_whole, 4, g.c)[0]
        norms = lax.psum(norms, AXES) * 0.5
    part = mm_cols(d_ckv, w_ckv)
    grad_text = part + g.over_c(part)
    share = depth // g.count
    text_cols = lax.dynamic_slice_in_dim(text_states, g.me * share, share, 1)
    grad_ckv = mm_rows(text_cols, d_ckv_whole)
    norms = lax.dynamic_slice_in_dim(norms, g.me * share, share, 1)

    if fast:
        grad_down = scatter_rows_fast(g, grad_down, mlp_down.shape[0], "yxz", 1)
        grad_up = scatter_columns_fast(g, grad_up, share, 2, "xyz", -1)
        grad_co = scatter_rows_fast(g, grad_co, share, "zxy", 1)
        grad_cq = scatter_columns_fast(g, grad_cq, share, 2, "zxy", -1)
        grad_out = scatter_rows_fast(g, grad_out, share, "zxy", 1)
        grad_qkv = scatter_columns_fast(g, grad_qkv, share, 6, "zyx", -1)
    else:
        grad_down = scatter_rows_plain(g, grad_down)
        grad_up = scatter_columns_plain(g, grad_up, 2)
        grad_co = scatter_rows_plain(g, grad_co)
        grad_cq = scatter_columns_plain(g, grad_cq, 2)
        grad_out = scatter_rows_plain(g, grad_out)
        grad_qkv = scatter_columns_plain(g, grad_qkv, 6)
    return (
        output,
        grad_tokens,
        grad_text,
        norms[:3],
        norms[3:5],
        grad_qkv,
        grad_out,
        grad_cq,
        grad_ckv,
        grad_co,
        grad_up,
        grad_down,
        norms[5],
    )


def solution(mesh):
    both = ("dp", "seq")
    rows = P(both, None)
    in_specs = (
        P(None, both, None),
        P(),
        P(None, both),
        P(),
        P(),
        P(None, both),
        P(None, both),
        rows,
        rows,
        rows,
        rows,
        rows,
        rows,
        rows,
        P(None, both, None),
    )
    out_specs = (
        P(None, both, None),
        P(None, both, None),
        P(),
        P(None, both),
        P(None, both),
        rows,
        rows,
        rows,
        rows,
        rows,
        rows,
        rows,
        P(both),
    )
    body = functools.partial(local, dp=mesh.shape["dp"], seq=mesh.shape["seq"])
    return jax.shard_map(body, mesh=mesh, in_specs=in_specs, out_specs=out_specs, check_vma=False)
```

```python
import functools

import jax
import jax.numpy as jnp
from jax import lax
from jax.experimental import pallas as pl
from jax.experimental.pallas import tpu as pltpu
from jax.sharding import PartitionSpec as P

H = 16
STRIPE = 64
EPS = 1e-05
NEG = -1e30
GELU_C = 0.7978845608028654
BF = jnp.bfloat16
F32 = jnp.float32
AXES = ("dp", "seq")


def mm(left, right):
    return jnp.dot(left, right, preferred_element_type=F32)


def mm_rows(left, right):
    return lax.dot_general(left, right, (((0,), (0,)), ((), ())), preferred_element_type=F32)


def mm_cols(left, right):
    return lax.dot_general(left, right, (((1,), (1,)), ((), ())), preferred_element_type=F32)


def pick(array, dim, index):
    return lax.dynamic_index_in_dim(array, index, dim, keepdims=False)


class Grid:
    def __init__(self, dp, seq):
        self.dp, self.seq, self.t = dp, seq, seq // 8
        self.count = dp * seq
        me = lax.axis_index(AXES)
        part = lax.rem(me, seq)
        self.me = me
        self.x = me // (2 * seq)
        self.c = lax.rem(me // seq, 2)
        self.z = part // (2 * self.t)
        self.r = lax.rem(part // 2, self.t)
        self.y = lax.rem(part, 2)

    def coords(self, d):
        part = d % self.seq
        return (
            d // (2 * self.seq),
            d // self.seq % 2,
            part // (2 * self.t),
            part // 2 % self.t,
            part % 2,
        )

    def index(self, x, c, z, r, y):
        return (x * 2 + c) * self.seq + (z * self.t + r) * 2 + y

    def send(self, value, move):
        perm = [(d, self.index(*move(*self.coords(d)))) for d in range(self.count)]
        return lax.ppermute(value, AXES, perm)

    def over_c(self, value):
        return self.send(value, lambda x, c, z, r, y: (x, 1 - c, z, r, y))

    def over_x(self, value):
        return self.send(value, lambda x, c, z, r, y: (1 - x, c, z, r, y))

    def over_y(self, value):
        return self.send(value, lambda x, c, z, r, y: (x, c, z, r, 1 - y))

    def xor_z(self, value, bits):
        return self.send(value, lambda x, c, z, r, y: (x, c, z ^ bits, r, y))

    def over_r(self, value, step):
        return self.send(value, lambda x, c, z, r, y: (x, c, z, (r + step) % self.t, y))

    def regroup(self, value, bits):
        return self.send(value, lambda x, c, z, r, y: (x, y, z ^ bits, r, c))


def after(value, *others):
    return lax.optimization_barrier((value, others))[0]


def place(scalars, sources, shapes, copies):
    def kernel(s_ref, *refs):
        ins = refs[: len(sources)]
        outs = refs[len(sources) : len(sources) + len(shapes)]
        sems = refs[-1]
        started = []
        for i, (source, at, target, to) in enumerate(copies):
            copy = pltpu.make_async_copy(
                ins[source].at[at(s_ref)], outs[target].at[to(s_ref)], sems.at[i]
            )
            copy.start()
            started.append(copy)
        for copy in started:
            copy.wait()

    moved = sum(source.size * 2 for source in sources)
    return pl.pallas_call(
        kernel,
        out_shape=[jax.ShapeDtypeStruct(shape, BF) for shape in shapes],
        in_specs=[pl.BlockSpec(memory_space=pltpu.SMEM)]
        + [pl.BlockSpec(memory_space=pl.ANY)] * len(sources),
        out_specs=[pl.BlockSpec(memory_space=pltpu.VMEM)] * len(shapes),
        scratch_shapes=[pltpu.SemaphoreType.DMA((len(copies),))],
        compiler_params=pltpu.CompilerParams(vmem_limit_bytes=32 * 2**20),
        cost_estimate=pl.CostEstimate(flops=0, bytes_accessed=2 * moved, transcendentals=0),
    )(scalars, *sources)


ALL = slice(None)


def gather_line(scal, got):
    _, rows, width = got[0].shape
    return place(
        scal,
        got,
        [(4, rows, width)] * 2,
        [
            (k, lambda s, h=h: (h,), h, lambda s, k=k: (s[2] ^ k,))
            for k in range(4)
            for h in range(2)
        ],
    )


def gather_place(scal, pair_a, far_a, pair_b, far_b, shapes, targets):
    rows = pair_a.shape[2]
    copies = []
    for i, half in enumerate((0, 0, 1, 1)):
        far = i % 2
        for near in range(2):
            dx, dy = (near, far) if half == 0 else (far, near)
            start = 0
            for wide, out, kind, row in targets[half]:
                copies.append(
                    (
                        i,
                        lambda s, near=near, start=start, wide=wide: (
                            near,
                            ALL,
                            ALL,
                            pl.ds(start, wide),
                        ),
                        out,
                        lambda s, dx=dx, dy=dy, kind=kind, row=row, half=half: (
                            s[0] ^ dx,
                            s[1] ^ half if kind is None else kind,
                            ALL,
                            s[3] ^ dy,
                            pl.ds(row, rows),
                        ),
                    )
                )
                start += wide
    return place(scal, [pair_a, far_a, pair_b, far_b], shapes, copies)


def plus(*terms):
    total = terms[0].astype(F32)
    for term in terms[1:]:
        total = total + term.astype(F32)
    return total.astype(BF)


def by_columns(array, share):
    view = array.reshape(2, 2, 4, 2, share, array.shape[1])
    block = (None, None, None, None, share, array.shape[1])
    return [(view, block, lambda x, z, y, h: (x, h, z, y, 0, 0))]


def by_rows(array, share):
    groups, width = array.shape[0] // (16 * share), array.shape[1]
    if groups == 1:
        view = array.reshape(2, 4, 2, share, width)
        block = (None, None, None, share, width // 2)
        return [(view, block, lambda x, z, y, h: (x, z, y, 0, h))]
    view = array.reshape(2, 4, 2, groups, share, width)
    block = (None, None, None, None, share, width)
    return [
        (view, block, lambda x, z, y, h, i=i: (x, z, y, h * (groups // 2) + i, 0, 0))
        for i in range(groups // 2)
    ]


def fold(scal, slots, steps, share, places, received, outs):
    width = sum(block[-1] for _, block, _ in slots)
    arrays, specs = [], []
    for h in range(2):
        for view, block, index in slots:
            arrays.append(view)
            specs.append(
                pl.BlockSpec(
                    block, lambda i, s, h=h, index=index: index(*places[h](i, s), h)
                )
            )
        for array, at in received[h]:
            arrays.append(array)
            specs.append(
                pl.BlockSpec((None, share, width), lambda i, s, at=at: (at(i, s), 0, 0))
            )
    each = len(slots), len(received[0])

    def kernel(s_ref, *refs):
        step = pl.program_id(0)
        ins, targets = refs[: len(arrays)], refs[len(arrays) :]
        for h in range(2):
            mine = ins[h * sum(each) : (h + 1) * sum(each)]
            start = 0
            for part in mine[: each[0]]:
                wide = part.shape[-1]
                at = pl.ds(start, wide)
                value = part[...]
                if each[1]:
                    value = value.astype(F32)
                    for extra in mine[each[0] :]:
                        value = value + extra[:, at].astype(F32)
                    value = value.astype(BF)
                if outs is None:
                    targets[h][:, at] = value
                else:
                    for j in range(steps):

                        @pl.when(step == j)
                        def _():
                            targets[j][h, :, at] = value

                start += wide

    if outs is None:
        out_shape = [jax.ShapeDtypeStruct((steps, share, width), BF)] * 2
        out_specs = [pl.BlockSpec((None, share, width), lambda i, s: (i, 0, 0))] * 2
    else:
        out_shape = [jax.ShapeDtypeStruct((2, share, width), BF)] * steps
        out_specs = [pl.BlockSpec((2, share, width), lambda i, s: (0, 0, 0))] * steps
    return pl.pallas_call(
        kernel,
        grid_spec=pltpu.PrefetchScalarGridSpec(
            num_scalar_prefetch=1, grid=(steps,), in_specs=specs, out_specs=out_specs
        ),
        out_shape=out_shape,
        compiler_params=pltpu.CompilerParams(vmem_limit_bytes=32 * 2**20),
        cost_estimate=pl.CostEstimate(
            flops=0, bytes_accessed=2 * steps * share * width * 6, transcendentals=0
        ),
    )(scal, *arrays)


def spread(g, line):
    return [line[0]] + [g.xor_z(line[k], k) for k in (1, 2, 3)]


class Scatter:
    def __init__(self, g, scal, share, slots):
        self.g, self.scal, self.share, self.slots = g, scal, share, slots

    def fold(self, *rest):
        return fold(self.scal, self.slots, *rest)

    def width(self):
        return sum(block[-1] for _, block, _ in self.slots)

    def far(self, *others):
        far_a, far_b = self.fold(
            8,
            self.share,
            [
                lambda i, s: (i // 4, lax.rem(i, 4), 1 - s[3]),
                lambda i, s: (1 - s[0], i // 2, lax.rem(i, 2)),
            ],
            [[], []],
            None,
        )
        self.folded = far_a, far_b
        if others:
            far_a, far_b = after(self.folded, others)
        self.far_a, self.far_b = self.g.over_y(far_a), self.g.over_x(far_b)
        return self

    def near(self):
        near_a, near_b = self.fold(
            4,
            self.share,
            [lambda i, s: (1 - s[0], i, s[3]), lambda i, s: (s[0], i, 1 - s[3])],
            [
                [(self.far_a, lambda i, s: (1 - s[0]) * 4 + i)],
                [(self.far_b, lambda i, s: i * 2 + 1 - s[3])],
            ],
            None,
        )
        self.folded = near_a, near_b
        self.near_a, self.near_b = self.g.over_x(near_a), self.g.over_y(near_b)
        return self

    def line(self):
        line = self.fold(
            4,
            self.share,
            [lambda i, s: (s[0], s[2] ^ i, s[3])] * 2,
            [
                [
                    (self.far_a, lambda i, s: s[0] * 4 + (s[2] ^ i)),
                    (self.near_a, lambda i, s: s[2] ^ i),
                ],
                [
                    (self.far_b, lambda i, s: (s[2] ^ i) * 2 + s[3]),
                    (self.near_b, lambda i, s: s[2] ^ i),
                ],
            ],
            True,
        )
        return line


def summed(terms, *at):
    return sum(term[at].astype(F32) for term in terms)


def prep_weights(scal, sources, whole=None):
    share = sources[0][0].shape[0]
    more = 0 if whole is None else whole.shape[1]
    width = sum(array.shape[1] // (2 if groups else 1) for array, groups in sources)

    def kernel(s_ref, *refs):
        low = s_ref[1] == 0
        keep, send = refs[-2:]
        start = 0
        for ref, (_, groups) in zip(refs, sources):
            if groups == 0:
                keep[:, pl.ds(start, ref.shape[1])] = ref[...]
                send[:, pl.ds(start, ref.shape[1])] = ref[...]
                start += ref.shape[1]
                continue
            block = ref.shape[1] // groups // 2
            for i in range(groups):
                a = ref[:, pl.ds(2 * i * block, block)]
                b = ref[:, pl.ds((2 * i + 1) * block, block)]
                keep[:, pl.ds(start, block)] = jnp.where(low, a, b)
                send[:, pl.ds(start, block)] = jnp.where(low, b, a)
                start += block
        if whole is not None:
            keep[:, pl.ds(start, more)] = refs[len(sources)][...]

    vmem = pl.BlockSpec(memory_space=pltpu.VMEM)
    smem = pl.BlockSpec(memory_space=pltpu.SMEM)
    arrays = [array for array, _ in sources] + ([] if whole is None else [whole])
    return pl.pallas_call(
        kernel,
        in_specs=[smem] + [vmem] * len(arrays),
        out_specs=[vmem] * 2,
        out_shape=[
            jax.ShapeDtypeStruct((share, width + more), BF),
            jax.ShapeDtypeStruct((share, width), BF),
        ],
        compiler_params=pltpu.CompilerParams(vmem_limit_bytes=32 * 2**20),
    )(scal, *arrays)


def prep_tokens(scal, ids, tokens, cotangent):
    depth = tokens.shape[2]

    def kernel(s_ref, ids_ref, tok, cot, *blocks):
        for step in range(4):
            j = s_ref[2] ^ step
            b = j >> 1
            half = (j & 1) ^ (ids_ref[b, 0] & 1)
            rows = pl.ds(pl.multiple_of(half * STRIPE, STRIPE), STRIPE)
            blocks[step][...] = tok[b, rows, :]
            blocks[4 + step][...] = cot[b, rows, :]

    vmem = pl.BlockSpec(memory_space=pltpu.VMEM)
    smem = pl.BlockSpec(memory_space=pltpu.SMEM)
    return pl.pallas_call(
        kernel,
        in_specs=[smem, smem, vmem, vmem],
        out_specs=[vmem] * 8,
        out_shape=[jax.ShapeDtypeStruct((STRIPE, depth), BF)] * 8,
        compiler_params=pltpu.CompilerParams(vmem_limit_bytes=32 * 2**20),
    )(scal, ids, tokens, cotangent)


def join_tokens(scal, mine, other):
    _, rows, depth = other.shape

    def kernel(s_ref, a0, a1, a2, a3, o_ref, out):
        for step, ref in enumerate((a0, a1, a2, a3)):
            for part, core in ((ref, s_ref[1]), (o_ref.at[step], 1 - s_ref[1])):
                at = pl.ds(pl.multiple_of((2 * step + core) * rows, rows), rows)
                out[at, :] = part[...]

    vmem = pl.BlockSpec(memory_space=pltpu.VMEM)
    return pl.pallas_call(
        kernel,
        in_specs=[pl.BlockSpec(memory_space=pltpu.SMEM)] + [vmem] * 5,
        out_specs=vmem,
        out_shape=jax.ShapeDtypeStruct((8 * rows, depth), BF),
        compiler_params=pltpu.CompilerParams(vmem_limit_bytes=32 * 2**20),
    )(scal, *mine, other)


def place_home(scal, ids, blocks):
    rows, width = blocks[0].shape
    depth = width // 2

    def kernel(s_ref, ids_ref, a0, a1, a2, a3, out, grad):
        for step, ref in enumerate((a0, a1, a2, a3)):
            j = s_ref[2] ^ step
            b = j >> 1
            half = (j & 1) ^ (ids_ref[b, 0] & 1)
            at = pl.ds(pl.multiple_of(half * rows, rows), rows)
            out[b, at, :] = ref[:, pl.ds(0, depth)]
            grad[b, at, :] = ref[:, pl.ds(depth, depth)].astype(F32)

    vmem = pl.BlockSpec(memory_space=pltpu.VMEM)
    smem = pl.BlockSpec(memory_space=pltpu.SMEM)
    return pl.pallas_call(
        kernel,
        in_specs=[smem, smem] + [vmem] * 4,
        out_specs=[vmem] * 2,
        out_shape=[
            jax.ShapeDtypeStruct((2, 2 * rows, depth), BF),
            jax.ShapeDtypeStruct((2, 2 * rows, depth), F32),
        ],
        compiler_params=pltpu.CompilerParams(vmem_limit_bytes=32 * 2**20),
    )(scal, ids, *blocks)


def attn_fwd_kernel(z_ref, q_ref, k_ref, v_ref, o_ref, *, scale):
    z = z_ref[0]
    size = q_ref.shape[0] // 4
    starts = [pl.multiple_of((z ^ h) * size, size) for h in range(4)]
    keys = jnp.concatenate([k_ref[pl.ds(s, size), :] for s in starts], 0)
    values = jnp.concatenate([v_ref[pl.ds(s, size), :] for s in starts], 0)
    first = lax.broadcasted_iota(jnp.int32, (size, 128), 1) < 64
    for j in range(4):
        span = (j + 1) * size
        q = q_ref[pl.ds(starts[j], size), :]
        row = lax.broadcasted_iota(jnp.int32, (size, span), 0) + j * size
        seen = lax.broadcasted_iota(jnp.int32, (size, span), 1) <= row
        outs = []
        for head in range(2):
            lanes = first if head == 0 else ~first
            qh = jnp.where(lanes, q, jnp.zeros_like(q))
            s = mm_cols(qh, keys[:span]) * scale
            s = jnp.where(seen, s, NEG)
            p = jnp.exp(s - jnp.max(s, -1, keepdims=True))
            total = jnp.sum(p, -1, keepdims=True)
            outs.append(mm(p.astype(BF), values[:span]) / total)
        o_ref[pl.ds(starts[j], size), :] = jnp.where(first, outs[0], outs[1]).astype(BF)


def attn_fwd(z, qkv, scale):
    rows, width = qkv.shape
    pairs = width // 3 // 128
    return pl.pallas_call(
        functools.partial(attn_fwd_kernel, scale=scale),
        grid=(pairs,),
        out_shape=jax.ShapeDtypeStruct((rows, width // 3), BF),
        in_specs=[
            pl.BlockSpec(memory_space=pltpu.SMEM),
            pl.BlockSpec((rows, 128), lambda i: (0, i)),
            pl.BlockSpec((rows, 128), lambda i: (0, pairs + i)),
            pl.BlockSpec((rows, 128), lambda i: (0, 2 * pairs + i)),
        ],
        out_specs=pl.BlockSpec((rows, 128), lambda i: (0, i)),
        compiler_params=pltpu.CompilerParams(vmem_limit_bytes=32 * 2**20),
        cost_estimate=pl.CostEstimate(
            flops=4 * rows * rows * width // 3,
            bytes_accessed=rows * width * 3,
            transcendentals=rows * rows * pairs * 2,
        ),
    )(z, qkv, qkv, qkv)


def attn_bwd_kernel(z_ref, q_ref, k_ref, v_ref, g_ref, d_ref, dk_ref, dv_ref, *, scale, pairs):
    z = z_ref[0]
    at = pl.program_id(0)
    size = q_ref.shape[0] // 4
    starts = [pl.multiple_of((z ^ h) * size, size) for h in range(4)]
    keys = jnp.concatenate([k_ref[pl.ds(s, size), :] for s in starts], 0)
    values = jnp.concatenate([v_ref[pl.ds(s, size), :] for s in starts], 0)
    first = lax.broadcasted_iota(jnp.int32, (size, 128), 1) < 64
    dk_ref[...] = jnp.zeros_like(dk_ref)
    dv_ref[...] = jnp.zeros_like(dv_ref)
    for j in range(4):
        span = (j + 1) * size
        q = q_ref[pl.ds(starts[j], size), :]
        grad = g_ref[pl.ds(starts[j], size), :]
        row = lax.broadcasted_iota(jnp.int32, (size, span), 0) + j * size
        seen = lax.broadcasted_iota(jnp.int32, (size, span), 1) <= row
        outs = []
        for head in range(2):
            lanes = first if head == 0 else ~first
            qh = jnp.where(lanes, q, jnp.zeros_like(q))
            gh = jnp.where(lanes, grad, jnp.zeros_like(grad))
            s = mm_cols(qh, keys[:span]) * scale
            s = jnp.where(seen, s, NEG)
            p = jnp.exp(s - jnp.max(s, -1, keepdims=True))
            p = p / jnp.sum(p, -1, keepdims=True)
            dp = mm_cols(gh, values[:span])
            ds = (p * (dp - jnp.sum(p * dp, -1, keepdims=True))).astype(BF)
            dv_ref[0:span, :] += mm_rows(p.astype(BF), gh)
            dk_ref[0:span, :] += mm_rows(ds, qh)
            outs.append(mm(ds, keys[:span]))
        dq = jnp.where(first, outs[0], outs[1]) * scale
        d_ref[pl.ds(starts[j], size), pl.ds(pl.multiple_of(at * 128, 128), 128)] = dq.astype(BF)
    for j in range(4):
        rows = slice(j * size, (j + 1) * size)
        d_ref[pl.ds(starts[j], size), pl.ds(pl.multiple_of((at + pairs) * 128, 128), 128)] = (
            dk_ref[rows, :] * scale
        ).astype(BF)
        d_ref[pl.ds(starts[j], size), pl.ds(pl.multiple_of((at + 2 * pairs) * 128, 128), 128)] = (
            dv_ref[rows, :].astype(BF)
        )


def attn_bwd(z, qkv, grad, scale):
    rows, width = qkv.shape
    pairs = width // 3 // 128
    return pl.pallas_call(
        functools.partial(attn_bwd_kernel, scale=scale, pairs=pairs),
        grid=(pairs,),
        out_shape=jax.ShapeDtypeStruct((rows, width), BF),
        in_specs=[
            pl.BlockSpec(memory_space=pltpu.SMEM),
            pl.BlockSpec((rows, 128), lambda i: (0, i)),
            pl.BlockSpec((rows, 128), lambda i: (0, pairs + i)),
            pl.BlockSpec((rows, 128), lambda i: (0, 2 * pairs + i)),
            pl.BlockSpec((rows, 128), lambda i: (0, i)),
        ],
        out_specs=pl.BlockSpec((rows, width), lambda i: (0, 0)),
        scratch_shapes=[pltpu.VMEM((rows, 128), F32), pltpu.VMEM((rows, 128), F32)],
        compiler_params=pltpu.CompilerParams(vmem_limit_bytes=32 * 2**20),
        cost_estimate=pl.CostEstimate(
            flops=10 * rows * rows * width // 3,
            bytes_accessed=rows * width * 5,
            transcendentals=rows * rows * pairs * 2,
        ),
    )(z, qkv, qkv, qkv, grad)


def cross_probs(q, keys, lanes, seen, scale):
    qh = jnp.where(lanes, q, jnp.zeros_like(q))
    s = jnp.where(seen, mm_cols(qh, keys) * scale, NEG)
    p = jnp.where(seen, jnp.exp(s - jnp.max(s, -1, keepdims=True)), 0.0)
    return qh, p / jnp.sum(p, -1, keepdims=True)


def cross_fwd_kernel(cap_ref, seg_ref, q_ref, k_ref, v_ref, o_ref, *, scale):
    seen = seg_ref[...] == cap_ref[0]
    q, keys, values = q_ref[...], k_ref[...], v_ref[...]
    first = lax.broadcasted_iota(jnp.int32, q.shape, 1) < 64
    outs = []
    for head in range(2):
        _, p = cross_probs(q, keys, first if head == 0 else ~first, seen, scale)
        outs.append(mm(p.astype(BF), values))
    o_ref[...] = jnp.where(first, outs[0], outs[1]).astype(BF)


def cross_fwd(cap, seg, cq, ckv, scale):
    rows, width = cq.shape
    text = ckv.shape[0]
    pairs = width // 128
    return pl.pallas_call(
        functools.partial(cross_fwd_kernel, scale=scale),
        grid=(pairs,),
        out_shape=jax.ShapeDtypeStruct((rows, width), BF),
        in_specs=[
            pl.BlockSpec(memory_space=pltpu.SMEM),
            pl.BlockSpec((1, text), lambda i: (0, 0)),
            pl.BlockSpec((rows, 128), lambda i: (0, i)),
            pl.BlockSpec((text, 128), lambda i: (0, i)),
            pl.BlockSpec((text, 128), lambda i: (0, pairs + i)),
        ],
        out_specs=pl.BlockSpec((rows, 128), lambda i: (0, i)),
        compiler_params=pltpu.CompilerParams(vmem_limit_bytes=32 * 2**20),
        cost_estimate=pl.CostEstimate(
            flops=4 * rows * text * width,
            bytes_accessed=rows * width * 4,
            transcendentals=rows * text * pairs * 2,
        ),
    )(cap, seg, cq, ckv, ckv)


def cross_bwd_kernel(cap_ref, seg_ref, q_ref, k_ref, v_ref, g_ref, dq_ref, dk_ref, dv_ref, *, scale):
    seen = seg_ref[...] == cap_ref[0]
    q, keys, values, grad = q_ref[...], k_ref[...], v_ref[...], g_ref[...]
    first = lax.broadcasted_iota(jnp.int32, q.shape, 1) < 64
    outs = []
    for head in range(2):
        lanes = first if head == 0 else ~first
        qh, p = cross_probs(q, keys, lanes, seen, scale)
        gh = jnp.where(lanes, grad, jnp.zeros_like(grad))
        dp = mm_cols(gh, values)
        ds = (p * (dp - jnp.sum(p * dp, -1, keepdims=True))).astype(BF)
        dv = mm_rows(p.astype(BF), gh)
        dk = mm_rows(ds, qh) * scale
        if head == 0:
            dv_ref[...] = dv
            dk_ref[...] = dk
        else:
            dv_ref[...] += dv
            dk_ref[...] += dk
        outs.append(mm(ds, keys))
    dq_ref[...] = (jnp.where(first, outs[0], outs[1]) * scale).astype(BF)


def cross_bwd(cap, seg, cq, ckv, grad, scale):
    rows, width = cq.shape
    text = ckv.shape[0]
    pairs = width // 128
    return pl.pallas_call(
        functools.partial(cross_bwd_kernel, scale=scale),
        grid=(pairs,),
        out_shape=[
            jax.ShapeDtypeStruct((rows, width), BF),
            jax.ShapeDtypeStruct((text, width), F32),
            jax.ShapeDtypeStruct((text, width), F32),
        ],
        in_specs=[
            pl.BlockSpec(memory_space=pltpu.SMEM),
            pl.BlockSpec((1, text), lambda i: (0, 0)),
            pl.BlockSpec((rows, 128), lambda i: (0, i)),
            pl.BlockSpec((text, 128), lambda i: (0, i)),
            pl.BlockSpec((text, 128), lambda i: (0, pairs + i)),
            pl.BlockSpec((rows, 128), lambda i: (0, i)),
        ],
        out_specs=[
            pl.BlockSpec((rows, 128), lambda i: (0, i)),
            pl.BlockSpec((text, 128), lambda i: (0, i)),
            pl.BlockSpec((text, 128), lambda i: (0, i)),
        ],
        compiler_params=pltpu.CompilerParams(vmem_limit_bytes=32 * 2**20),
        cost_estimate=pl.CostEstimate(
            flops=10 * rows * text * width,
            bytes_accessed=rows * width * 6,
            transcendentals=rows * text * pairs * 2,
        ),
    )(cap, seg, cq, ckv, ckv, grad)


def long_masks(g, rows):
    slot = jnp.arange(rows, dtype=jnp.int32) // (2 * STRIPE)
    rest = jnp.arange(rows, dtype=jnp.int32) % (2 * STRIPE)

    def positions(r):
        return ((g.z ^ slot) * g.t + r) * (2 * STRIPE) + rest

    key_pos = jnp.concatenate([positions((g.r - q) % g.t) for q in range(g.t)])
    return key_pos[None, :] <= positions(g.r)[:, None]


def long_gather(g, value):
    return jnp.concatenate([value] + [g.over_r(value, q) for q in range(1, g.t)], 0)


def long_fwd(g, qkv, scale):
    rows, width = qkv.shape
    head = 64
    heads = width // 3 // head
    keyval = long_gather(g, qkv[:, width // 3 :])
    q = qkv[:, : width // 3].reshape(rows, heads, head)
    k = keyval[:, : width // 3].reshape(-1, heads, head)
    v = keyval[:, width // 3 :].reshape(-1, heads, head)
    seen = long_masks(g, rows)[None]
    s = jnp.einsum("qhd,khd->hqk", q, k, preferred_element_type=F32) * scale
    s = jnp.where(seen, s, NEG)
    p = jnp.exp(s - jnp.max(s, -1, keepdims=True))
    p = p / jnp.sum(p, -1, keepdims=True)
    out = jnp.einsum("hqk,khd->qhd", p.astype(BF), v, preferred_element_type=F32)
    return out.reshape(rows, width // 3).astype(BF), (q, k, v, p)


def long_bwd(g, saved, grad, scale):
    q, k, v, p = saved
    rows, heads, head = q.shape
    width = heads * head
    grad = grad.reshape(rows, heads, head)
    dv = jnp.einsum("hqk,qhd->khd", p.astype(BF), grad, preferred_element_type=F32)
    dp = jnp.einsum("qhd,khd->hqk", grad, v, preferred_element_type=F32)
    ds = (p * (dp - jnp.sum(p * dp, -1, keepdims=True))).astype(BF)
    dq = jnp.einsum("hqk,khd->qhd", ds, k, preferred_element_type=F32) * scale
    dk = jnp.einsum("hqk,qhd->khd", ds, q, preferred_element_type=F32) * scale
    both = jnp.concatenate([dk.reshape(-1, width), dv.reshape(-1, width)], 1)
    both = both.reshape(g.t, rows, 2 * width)
    total = both[0]
    for step in range(1, g.t):
        total = total + g.over_r(both[step], -step)
    return jnp.concatenate([dq.reshape(rows, width).astype(BF), total.astype(BF)], 1)


def normed(values):
    center = values - jnp.mean(values, -1, keepdims=True)
    spread = lax.rsqrt(jnp.mean(center * center, -1, keepdims=True) + EPS)
    return center * spread, spread


def norm_back(unit, spread, gain, grad):
    f = grad * gain
    added = spread * (
        f - jnp.mean(f, -1, keepdims=True) - unit * jnp.mean(f * unit, -1, keepdims=True)
    )
    return added, jnp.sum(grad * unit, 0), jnp.sum(grad, 0)


def column_halves(weight, groups, mine):
    rows, width = weight.shape
    parts = weight.reshape(rows, groups, 2, width // groups // 2)
    return (
        pick(parts, 2, mine).reshape(rows, width // 2),
        pick(parts, 2, 1 - mine).reshape(rows, width // 2),
    )


def two(g, mine, other, axis):
    first = jnp.where(g.c == 0, mine, other)
    second = jnp.where(g.c == 0, other, mine)
    return jnp.stack([first, second], axis)


def gather_fast(g, scal, weights, ids, tokens, cotangent):
    gains, shifts, w_qkv, w_out, w_cq, w_ckv, w_co, w_up, w_down = weights
    share, depth = w_co.shape
    tall = w_down.shape[0]
    small = jnp.concatenate([gains, shifts], 0).T
    small = jnp.pad(small, ((0, 0), (0, 128 - small.shape[1])))
    keep1, send1 = prep_weights(scal, [(w_qkv, 6), (small, 0), (w_cq, 2)])
    keep2, send2 = prep_weights(scal, [(w_ckv, 4)], w_out)
    keep3, send3 = prep_weights(scal, [(w_up, 2)])
    blocks = prep_tokens(scal, ids, tokens, cotangent)
    got1 = g.over_c(send1)
    got2 = g.over_c(jnp.concatenate([send2, send3], 1))

    def shape(kinds, rows, width):
        return (2, kinds, 4, 2, rows, width)

    n_qkv, n_cq, n_ckv, n_up = (w.shape[1] // 2 for w in (w_qkv, w_cq, w_ckv, w_up))
    groups = tall // share // 2
    low, high = (
        list(half.reshape(groups, share, depth))
        for half in (w_down[: tall // 2], w_down[tall // 2 :])
    )
    second = jnp.stack([keep2, jnp.concatenate([got2[:, :n_ckv], w_co], 1)])
    third = jnp.stack(
        [jnp.concatenate([keep3] + low, 1), jnp.concatenate([got2[:, n_ckv:]] + high, 1)]
    )
    first = after(jnp.stack([keep1, got1]), second, third)
    tok, cot = list(blocks[:4]), list(blocks[4:])

    def near(lines):
        return g.over_x(lines[0]), g.over_y(lines[1])

    def far(lines, got):
        pair_a, pair_b = jnp.stack([lines[0], got[0]]), jnp.stack([lines[1], got[1]])
        return pair_a, g.over_y(pair_a), pair_b, g.over_x(pair_b)

    got_a = [first] + [g.xor_z(first, k) for k in (1, 2, 3)]
    tok = [g.regroup(tok[0], 0)] + tok[1:]
    line_a = gather_line(scal, got_a)
    near_a = near(line_a)
    tok[1:] = after(tok[1:], got_a)
    tok[1:] = [g.regroup(tok[k], k) for k in (1, 2, 3)]
    second = after(second, near_a, tok)
    far_a = far(line_a, after(near_a, tok))
    got_b = [second] + [g.xor_z(second, k) for k in (1, 2, 3)]
    tok = after(tok, near_a)
    resid = join_tokens(scal, tok, g.over_c(jnp.stack(tok)))
    line_b = gather_line(scal, after(got_b, far_a))
    near_b = near(line_b)
    third = after(third, got_b, far_a)
    got_c1 = g.xor_z(third, 1)
    far_b = far(line_b, after(near_b, got_c1))
    third_late = after(third, near_b, got_c1)
    got_c = [third, got_c1] + [g.xor_z(third_late, k) for k in (2, 3)]
    line_c = gather_line(scal, after(got_c, far_b))
    near_c = near(line_c)
    cot = [g.regroup(block, k) for k, block in enumerate(after(cot, got_c, far_b))]
    far_c = far(line_c, after(near_c, cot))
    cot = after(cot, near_c)
    cot = join_tokens(scal, cot, g.over_c(jnp.stack(cot)))

    qkv, small, cq = gather_place(
        scal,
        *far_a,
        [shape(2, share, n_qkv), shape(2, share, 128), shape(2, share, n_cq)],
        [[(n_qkv, 0, None, 0), (128, 1, None, 0), (n_cq, 2, None, 0)]] * 2,
    )
    ckv, out, co = gather_place(
        scal,
        *far_b,
        [shape(2, share, n_ckv), shape(1, share, depth), shape(1, share, depth)],
        [[(n_ckv, 0, None, 0), (depth, 1 + half, 0, 0)] for half in range(2)],
    )
    up, down = gather_place(
        scal,
        *far_c,
        [shape(2, share, n_up), shape(1, tall, depth)],
        [
            [(n_up, 0, None, 0)]
            + [(depth, 1, 0, (half * groups + i) * share) for i in range(groups)]
            for half in range(2)
        ],
    )

    def flat(array):
        return array.reshape(-1, array.shape[-1])

    return (
        resid,
        cot,
        flat(small)[:, :6].astype(F32).T,
    ) + tuple(flat(array) for array in (qkv, out, cq, ckv, co, up, down))


def gather_plain(g, weights):
    gains, shifts, w_qkv, w_out, w_cq, w_ckv, w_co, w_up, w_down = weights
    small = lax.all_gather(jnp.concatenate([gains, shifts], 0), AXES, axis=1, tiled=True)

    def columns(weight, groups):
        whole = lax.all_gather(weight, AXES, axis=0, tiled=True)
        return column_halves(whole, groups, g.c)[0]

    def rows(weight):
        whole = lax.all_gather(weight, AXES, axis=0, tiled=True)
        parts = whole.reshape(2, 2, whole.shape[0] // 4, whole.shape[1])
        return pick(parts, 1, g.c).reshape(whole.shape[0] // 2, whole.shape[1])

    return (
        small.astype(F32),
        columns(w_qkv, 6),
        rows(w_out),
        columns(w_cq, 2),
        columns(w_ckv, 4),
        rows(w_co),
        columns(w_up, 2),
        rows(w_down),
    )


def join_columns(g, keep, got, groups):
    rows, width = keep.shape
    block = width // groups
    parts = two(g, keep.reshape(rows, groups, block), got.reshape(rows, groups, block), 2)
    return parts.reshape(rows, 2 * width)


def scatter_columns_plain(g, grad, groups):
    rows, width = grad.shape
    whole = join_columns(g, grad, jnp.zeros_like(grad), groups)
    return lax.psum_scatter(whole, AXES, scatter_dimension=0, tiled=True)


def scatter_rows_plain(g, grad):
    rows, width = grad.shape
    parts = grad.reshape(2, rows // 2, width)
    whole = two(g, parts, jnp.zeros_like(parts), 1).reshape(2 * rows, width)
    return lax.psum_scatter(whole, AXES, scatter_dimension=0, tiled=True)


def both_cores(g, part):
    low = part.astype(BF)
    return low.astype(F32) + g.over_c(low).astype(F32)


def local(
    tokens,
    text_states,
    image_ids,
    text_segments,
    image_caption,
    norm_gains,
    norm_shifts,
    self_qkv,
    self_out,
    cross_query,
    cross_keyval,
    cross_out,
    mlp_up,
    mlp_down,
    cotangent,
    *,
    dp,
    seq,
):
    g = Grid(dp, seq)
    fast = g.t == 1
    depth = tokens.shape[-1]
    scale = (depth // H) ** (-0.5)
    weights = (
        norm_gains,
        norm_shifts,
        self_qkv,
        self_out,
        cross_query,
        cross_keyval,
        cross_out,
        mlp_up,
        mlp_down,
    )

    scal = jnp.stack([g.x, g.c, g.z, g.y]).astype(jnp.int32)
    start = image_ids[:, 0] & 1
    if fast:
        (resid, cot, small, w_qkv, w_out, w_cq, w_ckv, w_co, w_up, w_down) = gather_fast(
            g, scal, weights, image_ids, tokens, cotangent
        )
    else:
        (small, w_qkv, w_out, w_cq, w_ckv, w_co, w_up, w_down) = gather_plain(g, weights)
        both = jnp.stack([tokens, cotangent], 2).reshape(4, STRIPE, 2 * depth)
        received = []
        for step in range(4):
            j = g.z ^ step
            half = (j & 1) ^ start[j >> 1]
            received.append(g.regroup(pick(both, 0, (j >> 1) * 2 + half), step))
        mine = jnp.stack(received)
        held = two(g, mine, g.over_c(mine), 1).reshape(8 * STRIPE, 2, depth)
        resid, cot = held[:, 0], held[:, 1]
    resid = resid.astype(F32)
    gain, shift = small[:3], small[3:]

    image = (g.x * 2 + g.y) * 2 + (g.z & 1)
    cap = image_caption[g.z >> 1, image].reshape(1)
    seg = text_segments.reshape(1, -1)
    slot = g.z.reshape(1).astype(jnp.int32)

    unit_one, spread_one = normed(resid)
    n_one = (unit_one * gain[0] + shift[0]).astype(BF)
    qkv = mm(n_one, w_qkv).astype(BF)
    if fast:
        attended = attn_fwd(slot, qkv, scale)
    else:
        attended, saved = long_fwd(g, qkv, scale)
    hidden_one = resid + both_cores(g, mm(attended, w_out))
    unit_two, spread_two = normed(hidden_one)
    n_two = (unit_two * gain[1] + shift[1]).astype(BF)
    cq = mm(n_two, w_cq).astype(BF)
    ckv = mm(text_states, w_ckv).astype(BF)
    crossed = cross_fwd(cap, seg, cq, ckv, scale)
    hidden_two = hidden_one + both_cores(g, mm(crossed, w_co))
    unit_three, spread_three = normed(hidden_two)
    n_three = (unit_three * gain[2] + shift[2]).astype(BF)
    up = mm(n_three, w_up)
    inner = jnp.tanh(GELU_C * (up + 0.044715 * up * up * up))
    act = (0.5 * up * (1.0 + inner)).astype(BF)

    def halves(value):
        parts = value.reshape(4, 2, STRIPE, value.shape[-1])
        return pick(parts, 1, g.c), pick(parts, 1, 1 - g.c)

    down = mm(act, w_down)
    keep, gone = halves(down)
    out = (halves(hidden_two)[0] + keep + g.over_c(gone.astype(BF)).astype(F32)).astype(BF)

    grad_down = mm_rows(act, cot)
    slope = 0.5 * (1.0 + inner) + 0.5 * up * (1.0 - inner * inner) * GELU_C * (
        1.0 + 3 * 0.044715 * up * up
    )
    d_up = (mm_cols(cot, w_down) * slope).astype(BF)
    grad_up = mm_rows(n_three, d_up)
    share = depth // g.count
    if fast:
        grad_down, grad_up = grad_down.astype(BF), grad_up.astype(BF)
        mlp = Scatter(g, scal, share, by_rows(grad_down, share) + by_columns(grad_up, share)).far()
    added, gain_three, shift_three = norm_back(
        unit_three, spread_three, gain[2], both_cores(g, mm_cols(d_up, w_up))
    )
    g_two = cot.astype(F32) + added
    d_cross = g_two.astype(BF)
    grad_co = mm_rows(crossed, d_cross)
    d_crossed = mm_cols(d_cross, w_co).astype(BF)
    d_cq, d_ck, d_cv = cross_bwd(cap, seg, cq, ckv, d_crossed, scale)
    grad_cq = mm_rows(n_two, d_cq)
    added, gain_two, shift_two = norm_back(
        unit_two, spread_two, gain[1], both_cores(g, mm_cols(d_cq, w_cq))
    )
    g_one = g_two + added
    d_self = g_one.astype(BF)
    grad_out = mm_rows(attended, d_self)
    d_att = mm_cols(d_self, w_out).astype(BF)
    if fast:
        grad_co, grad_cq = grad_co.astype(BF), grad_cq.astype(BF)
        cross = Scatter(g, scal, share, by_rows(grad_co, share) + by_columns(grad_cq, share))
        d_ckv = jnp.concatenate([d_ck, d_cv], 1).astype(BF)
        swapped = g.xor_z(d_ckv, 1)
        mlp.near()
        d_att, swapped = after((d_att, swapped), mlp.folded)
        d_ckv = plus(d_ckv, swapped)
        swapped = g.xor_z(d_ckv, 2)
        d_qkv = attn_bwd(slot, qkv, d_att, scale)
        mlp_line = mlp.line()
        cross.far()
        d_qkv, swapped = after((d_qkv, swapped), mlp_line, cross.folded)
        mlp_terms = spread(g, mlp_line)
        d_ckv = plus(d_ckv, swapped)
    else:
        d_qkv = long_bwd(g, saved, d_att, scale)
    grad_qkv = mm_rows(n_one, d_qkv)
    added, gain_one, shift_one = norm_back(
        unit_one, spread_one, gain[0], both_cores(g, mm_cols(d_qkv, w_qkv))
    )
    grad_in = (g_one + added).astype(BF)

    norms = jnp.stack([gain_one, gain_two, gain_three, shift_one, shift_two, shift_three])
    back = jnp.concatenate([out, halves(grad_in)[0]], 2)
    if fast:
        grad_out, grad_qkv = grad_out.astype(BF), grad_qkv.astype(BF)
        cross.near()
        last = Scatter(
            g, scal, share, by_rows(grad_out, share) + by_columns(grad_qkv, share)
        )
        last.far(cross.near_a, cross.near_b)
        back, mlp_terms = after((back, mlp_terms), last.folded, last.far_a, last.far_b)
        last.near()
        back = [g.regroup(back[step], step) for step in range(4)]
        mlp_terms = after(mlp_terms, last.folded)
        lines = [jnp.concatenate(pair, 2) for pair in zip(cross.line(), last.line())]
        last_terms = spread(g, after(lines, back))
        d_ckv, norms, mlp_terms = after(
            (d_ckv, norms, mlp_terms), lines, last.near_a, last.near_b
        )
        d_ckv = plus(d_ckv, g.over_x(d_ckv))
        norms = norms + g.over_y(norms)
        d_ckv = plus(d_ckv, g.over_y(d_ckv))
        norms = norms + g.over_x(norms)
        norms = norms + g.xor_z(norms, 1)
        norms = norms + g.xor_z(norms, 2)
        norms = lax.dynamic_slice_in_dim(norms, g.me * share, share, 1)
        output, grad_tokens = place_home(scal, image_ids, back)
        n_cross = cross.width()
        cross_terms = [term[:, :, : n_cross] for term in last_terms]
        last_terms = [term[:, :, n_cross:] for term in last_terms]
        d_ckv_whole = join_columns(g, d_ckv, g.over_c(d_ckv), 4)
    else:
        back = jnp.stack([g.regroup(back[step], step) for step in range(4)])
        order = []
        for block in range(4):
            j = (block & 2) + ((block & 1) ^ start[block >> 1])
            order.append(pick(back, 0, j ^ g.z))
        back = jnp.stack(order).reshape(2, 2 * STRIPE, 2 * depth)
        output, grad_tokens = back[:, :, :depth], back[:, :, depth:].astype(F32)
        d_ckv = jnp.concatenate([d_ck, d_cv], 1)
        whole = join_columns(g, d_ckv, jnp.zeros_like(d_ckv), 4)
        d_ckv_whole = lax.psum(whole, AXES).astype(BF)
        d_ckv = column_halves(d_ckv_whole, 4, g.c)[0]
        norms = lax.psum(norms, AXES) * 0.5
        norms = lax.dynamic_slice_in_dim(norms, g.me * (depth // g.count), depth // g.count, 1)
    part = mm_cols(d_ckv, w_ckv)
    grad_text = part + g.over_c(part)
    text_cols = lax.dynamic_slice_in_dim(text_states, g.me * share, share, 1)
    grad_ckv = mm_rows(text_cols, d_ckv_whole)
    if fast:
        tall = mlp_down.shape[0]

        def columns(terms, low, high, groups):
            got = g.over_c(plus(*[pick(term, 0, 1 - g.c)[:, low:high] for term in terms]))
            keep = sum(pick(term, 0, g.c)[:, low:high].astype(F32) for term in terms)
            return join_columns(g, keep, got.astype(F32), groups)

        terms = mlp_terms
        n_down = tall // share // 2 * depth
        grad_down = summed(terms, ALL, ALL, slice(0, n_down))
        grad_down = grad_down.reshape(2, share, tall // share // 2, depth)
        grad_down = grad_down.transpose(0, 2, 1, 3).reshape(tall, depth)
        grad_up = columns(terms, n_down, None, 2)
        terms = cross_terms
        half = depth // 2
        co = summed(terms, ALL, ALL, slice(0, half))
        grad_co = jnp.concatenate([co[0], co[1]], 1)
        grad_cq = columns(terms, half, None, 2)
        terms = last_terms
        out_sum = summed(terms, ALL, ALL, slice(0, half))
        grad_out = jnp.concatenate([out_sum[0], out_sum[1]], 1)
        grad_qkv = columns(terms, half, None, 6)
    else:
        grad_down = scatter_rows_plain(g, grad_down)
        grad_up = scatter_columns_plain(g, grad_up, 2)
        grad_co = scatter_rows_plain(g, grad_co)
        grad_cq = scatter_columns_plain(g, grad_cq, 2)
        grad_out = scatter_rows_plain(g, grad_out)
        grad_qkv = scatter_columns_plain(g, grad_qkv, 6)
    return (
        output,
        grad_tokens,
        grad_text,
        norms[:3],
        norms[3:5],
        grad_qkv,
        grad_out,
        grad_cq,
        grad_ckv,
        grad_co,
        grad_up,
        grad_down,
        norms[5],
    )


def solution(mesh):
    both = ("dp", "seq")
    rows = P(both, None)
    in_specs = (
        P(None, both, None),
        P(),
        P(None, both),
        P(),
        P(),
        P(None, both),
        P(None, both),
        rows,
        rows,
        rows,
        rows,
        rows,
        rows,
        rows,
        P(None, both, None),
    )
    out_specs = (
        P(None, both, None),
        P(None, both, None),
        P(),
        P(None, both),
        P(None, both),
        rows,
        rows,
        rows,
        rows,
        rows,
        rows,
        rows,
        P(both),
    )
    body = functools.partial(local, dp=mesh.shape["dp"], seq=mesh.shape["seq"])
    return jax.shard_map(body, mesh=mesh, in_specs=in_specs, out_specs=out_specs, check_vma=False)
```

```python
import functools

import jax
import jax.numpy as jnp
from jax import lax
from jax.experimental import pallas as pl
from jax.experimental.pallas import tpu as pltpu
from jax.sharding import PartitionSpec as P

H = 16
STRIPE = 64
EPS = 1e-05
NEG = -1e30
GELU_C = 0.7978845608028654
BF = jnp.bfloat16
F32 = jnp.float32
AXES = ("dp", "seq")


def mm(left, right):
    return jnp.dot(left, right, preferred_element_type=F32)


def mm_rows(left, right):
    return lax.dot_general(left, right, (((0,), (0,)), ((), ())), preferred_element_type=F32)


def mm_cols(left, right):
    return lax.dot_general(left, right, (((1,), (1,)), ((), ())), preferred_element_type=F32)


def pick(array, dim, index):
    return lax.dynamic_index_in_dim(array, index, dim, keepdims=False)


class Grid:
    def __init__(self, dp, seq):
        self.dp, self.seq, self.t = dp, seq, seq // 8
        self.count = dp * seq
        me = lax.axis_index(AXES)
        part = lax.rem(me, seq)
        self.me = me
        self.x = me // (2 * seq)
        self.c = lax.rem(me // seq, 2)
        self.z = part // (2 * self.t)
        self.r = lax.rem(part // 2, self.t)
        self.y = lax.rem(part, 2)

    def coords(self, d):
        part = d % self.seq
        return (
            d // (2 * self.seq),
            d // self.seq % 2,
            part // (2 * self.t),
            part // 2 % self.t,
            part % 2,
        )

    def index(self, x, c, z, r, y):
        return (x * 2 + c) * self.seq + (z * self.t + r) * 2 + y

    def send(self, value, move):
        perm = [(d, self.index(*move(*self.coords(d)))) for d in range(self.count)]
        return lax.ppermute(value, AXES, perm)

    def over_c(self, value):
        return self.send(value, lambda x, c, z, r, y: (x, 1 - c, z, r, y))

    def over_x(self, value):
        return self.send(value, lambda x, c, z, r, y: (1 - x, c, z, r, y))

    def over_y(self, value):
        return self.send(value, lambda x, c, z, r, y: (x, c, z, r, 1 - y))

    def xor_z(self, value, bits):
        return self.send(value, lambda x, c, z, r, y: (x, c, z ^ bits, r, y))

    def over_r(self, value, step):
        return self.send(value, lambda x, c, z, r, y: (x, c, z, (r + step) % self.t, y))

    def regroup(self, value, bits):
        return self.send(value, lambda x, c, z, r, y: (x, y, z ^ bits, r, c))


def after(value, *others):
    return lax.optimization_barrier((value, others))[0]


def place(scalars, sources, shapes, copies):
    def kernel(s_ref, *refs):
        ins = refs[: len(sources)]
        outs = refs[len(sources) : len(sources) + len(shapes)]
        sems = refs[-1]
        started = []
        for i, (source, at, target, to) in enumerate(copies):
            copy = pltpu.make_async_copy(
                ins[source].at[at(s_ref)], outs[target].at[to(s_ref)], sems.at[i]
            )
            copy.start()
            started.append(copy)
        for copy in started:
            copy.wait()

    moved = sum(source.size * 2 for source in sources)
    return pl.pallas_call(
        kernel,
        out_shape=[jax.ShapeDtypeStruct(shape, BF) for shape in shapes],
        in_specs=[pl.BlockSpec(memory_space=pltpu.SMEM)]
        + [pl.BlockSpec(memory_space=pl.ANY)] * len(sources),
        out_specs=[pl.BlockSpec(memory_space=pltpu.VMEM)] * len(shapes),
        scratch_shapes=[pltpu.SemaphoreType.DMA((len(copies),))],
        compiler_params=pltpu.CompilerParams(vmem_limit_bytes=32 * 2**20),
        cost_estimate=pl.CostEstimate(flops=0, bytes_accessed=2 * moved, transcendentals=0),
    )(scalars, *sources)


ALL = slice(None)


def gather_line(scal, got):
    _, rows, width = got[0].shape
    return place(
        scal,
        got,
        [(4, rows, width)] * 2,
        [
            (k, lambda s, h=h: (h,), h, lambda s, k=k: (s[2] ^ k,))
            for k in range(4)
            for h in range(2)
        ],
    )


def gather_place(scal, pair_a, far_a, pair_b, far_b, shapes, targets):
    rows = pair_a.shape[2]
    copies = []
    for i, half in enumerate((0, 0, 1, 1)):
        far = i % 2
        for near in range(2):
            dx, dy = (near, far) if half == 0 else (far, near)
            start = 0
            for wide, out, kind, row in targets[half]:
                copies.append(
                    (
                        i,
                        lambda s, near=near, start=start, wide=wide: (
                            near,
                            ALL,
                            ALL,
                            pl.ds(start, wide),
                        ),
                        out,
                        lambda s, dx=dx, dy=dy, kind=kind, row=row, half=half: (
                            s[0] ^ dx,
                            s[1] ^ half if kind is None else kind,
                            ALL,
                            s[3] ^ dy,
                            pl.ds(row, rows),
                        ),
                    )
                )
                start += wide
    return place(scal, [pair_a, far_a, pair_b, far_b], shapes, copies)


def plus(*terms):
    total = terms[0].astype(F32)
    for term in terms[1:]:
        total = total + term.astype(F32)
    return total.astype(BF)


def by_columns(array, share):
    view = array.reshape(2, 2, 4, 2, share, array.shape[1])
    block = (None, None, None, None, share, array.shape[1])
    return [(view, block, lambda x, z, y, h: (x, h, z, y, 0, 0))]


def by_rows(array, share):
    groups, width = array.shape[0] // (16 * share), array.shape[1]
    if groups == 1:
        view = array.reshape(2, 4, 2, share, width)
        block = (None, None, None, share, width // 2)
        return [(view, block, lambda x, z, y, h: (x, z, y, 0, h))]
    view = array.reshape(2, 4, 2, groups, share, width)
    block = (None, None, None, None, share, width)
    return [
        (view, block, lambda x, z, y, h, i=i: (x, z, y, h * (groups // 2) + i, 0, 0))
        for i in range(groups // 2)
    ]


def fold(scal, slots, steps, share, places, received, outs):
    width = sum(block[-1] for _, block, _ in slots)
    arrays, specs = [], []
    for h in range(2):
        for view, block, index in slots:
            arrays.append(view)
            specs.append(
                pl.BlockSpec(
                    block, lambda i, s, h=h, index=index: index(*places[h](i, s), h)
                )
            )
        for array, at in received[h]:
            arrays.append(array)
            specs.append(
                pl.BlockSpec((None, share, width), lambda i, s, at=at: (at(i, s), 0, 0))
            )
    each = len(slots), len(received[0])

    def kernel(s_ref, *refs):
        step = pl.program_id(0)
        ins, targets = refs[: len(arrays)], refs[len(arrays) :]
        for h in range(2):
            mine = ins[h * sum(each) : (h + 1) * sum(each)]
            start = 0
            for part in mine[: each[0]]:
                wide = part.shape[-1]
                at = pl.ds(start, wide)
                value = part[...]
                if each[1]:
                    value = value.astype(F32)
                    for extra in mine[each[0] :]:
                        value = value + extra[:, at].astype(F32)
                    value = value.astype(BF)
                if outs is None:
                    targets[h][:, at] = value
                else:
                    for j in range(steps):

                        @pl.when(step == j)
                        def _():
                            targets[j][h, :, at] = value

                start += wide

    if outs is None:
        out_shape = [jax.ShapeDtypeStruct((steps, share, width), BF)] * 2
        out_specs = [pl.BlockSpec((None, share, width), lambda i, s: (i, 0, 0))] * 2
    else:
        out_shape = [jax.ShapeDtypeStruct((2, share, width), BF)] * steps
        out_specs = [pl.BlockSpec((2, share, width), lambda i, s: (0, 0, 0))] * steps
    return pl.pallas_call(
        kernel,
        grid_spec=pltpu.PrefetchScalarGridSpec(
            num_scalar_prefetch=1, grid=(steps,), in_specs=specs, out_specs=out_specs
        ),
        out_shape=out_shape,
        compiler_params=pltpu.CompilerParams(vmem_limit_bytes=32 * 2**20),
        cost_estimate=pl.CostEstimate(
            flops=0, bytes_accessed=2 * steps * share * width * 6, transcendentals=0
        ),
    )(scal, *arrays)


def spread(g, line):
    return [line[0]] + [g.xor_z(line[k], k) for k in (1, 2, 3)]


class Scatter:
    def __init__(self, g, scal, share, slots):
        self.g, self.scal, self.share, self.slots = g, scal, share, slots

    def fold(self, *rest):
        return fold(self.scal, self.slots, *rest)

    def width(self):
        return sum(block[-1] for _, block, _ in self.slots)

    def fold_far(self):
        return self.fold(
            8,
            self.share,
            [
                lambda i, s: (i // 4, lax.rem(i, 4), 1 - s[3]),
                lambda i, s: (1 - s[0], i // 2, lax.rem(i, 2)),
            ],
            [[], []],
            None,
        )

    def send_far(self, folded):
        self.far_a, self.far_b = self.g.over_y(folded[0]), self.g.over_x(folded[1])
        return self.far_a, self.far_b

    def fold_near(self):
        return self.fold(
            4,
            self.share,
            [lambda i, s: (1 - s[0], i, s[3]), lambda i, s: (s[0], i, 1 - s[3])],
            [
                [(self.far_a, lambda i, s: (1 - s[0]) * 4 + i)],
                [(self.far_b, lambda i, s: i * 2 + 1 - s[3])],
            ],
            None,
        )

    def send_near(self, folded):
        self.near_a, self.near_b = self.g.over_x(folded[0]), self.g.over_y(folded[1])
        return self.near_a, self.near_b

    def line(self):
        line = self.fold(
            4,
            self.share,
            [lambda i, s: (s[0], s[2] ^ i, s[3])] * 2,
            [
                [
                    (self.far_a, lambda i, s: s[0] * 4 + (s[2] ^ i)),
                    (self.near_a, lambda i, s: s[2] ^ i),
                ],
                [
                    (self.far_b, lambda i, s: (s[2] ^ i) * 2 + s[3]),
                    (self.near_b, lambda i, s: s[2] ^ i),
                ],
            ],
            True,
        )
        return line


def summed(terms, *at):
    return sum(term[at].astype(F32) for term in terms)


def prep_weights(scal, sources, whole=None):
    share = sources[0][0].shape[0]
    more = 0 if whole is None else whole.shape[1]
    width = sum(array.shape[1] // (2 if groups else 1) for array, groups in sources)

    def kernel(s_ref, *refs):
        low = s_ref[1] == 0
        keep, send = refs[-2:]
        start = 0
        for ref, (_, groups) in zip(refs, sources):
            if groups == 0:
                keep[:, pl.ds(start, ref.shape[1])] = ref[...]
                send[:, pl.ds(start, ref.shape[1])] = ref[...]
                start += ref.shape[1]
                continue
            block = ref.shape[1] // groups // 2
            for i in range(groups):
                a = ref[:, pl.ds(2 * i * block, block)]
                b = ref[:, pl.ds((2 * i + 1) * block, block)]
                keep[:, pl.ds(start, block)] = jnp.where(low, a, b)
                send[:, pl.ds(start, block)] = jnp.where(low, b, a)
                start += block
        if whole is not None:
            keep[:, pl.ds(start, more)] = refs[len(sources)][...]

    vmem = pl.BlockSpec(memory_space=pltpu.VMEM)
    smem = pl.BlockSpec(memory_space=pltpu.SMEM)
    arrays = [array for array, _ in sources] + ([] if whole is None else [whole])
    return pl.pallas_call(
        kernel,
        in_specs=[smem] + [vmem] * len(arrays),
        out_specs=[vmem] * 2,
        out_shape=[
            jax.ShapeDtypeStruct((share, width + more), BF),
            jax.ShapeDtypeStruct((share, width), BF),
        ],
        compiler_params=pltpu.CompilerParams(vmem_limit_bytes=32 * 2**20),
    )(scal, *arrays)


def prep_tokens(scal, ids, tokens, cotangent):
    depth = tokens.shape[2]

    def kernel(s_ref, ids_ref, tok, cot, *blocks):
        for step in range(4):
            j = s_ref[2] ^ step
            b = j >> 1
            half = (j & 1) ^ (ids_ref[b, 0] & 1)
            rows = pl.ds(pl.multiple_of(half * STRIPE, STRIPE), STRIPE)
            blocks[step][...] = tok[b, rows, :]
            blocks[4 + step][...] = cot[b, rows, :]

    vmem = pl.BlockSpec(memory_space=pltpu.VMEM)
    smem = pl.BlockSpec(memory_space=pltpu.SMEM)
    return pl.pallas_call(
        kernel,
        in_specs=[smem, smem, vmem, vmem],
        out_specs=[vmem] * 8,
        out_shape=[jax.ShapeDtypeStruct((STRIPE, depth), BF)] * 8,
        compiler_params=pltpu.CompilerParams(vmem_limit_bytes=32 * 2**20),
    )(scal, ids, tokens, cotangent)


def join_tokens(scal, mine, other):
    _, rows, depth = other.shape

    def kernel(s_ref, a0, a1, a2, a3, o_ref, out):
        for step, ref in enumerate((a0, a1, a2, a3)):
            for part, core in ((ref, s_ref[1]), (o_ref.at[step], 1 - s_ref[1])):
                at = pl.ds(pl.multiple_of((2 * step + core) * rows, rows), rows)
                out[at, :] = part[...]

    vmem = pl.BlockSpec(memory_space=pltpu.VMEM)
    return pl.pallas_call(
        kernel,
        in_specs=[pl.BlockSpec(memory_space=pltpu.SMEM)] + [vmem] * 5,
        out_specs=vmem,
        out_shape=jax.ShapeDtypeStruct((8 * rows, depth), BF),
        compiler_params=pltpu.CompilerParams(vmem_limit_bytes=32 * 2**20),
    )(scal, *mine, other)


def place_home(scal, ids, outs, grads):
    rows, depth = outs[0].shape

    def kernel(s_ref, ids_ref, *refs):
        out, grad = refs[8:]
        for step in range(4):
            j = s_ref[2] ^ step
            b = j >> 1
            half = (j & 1) ^ (ids_ref[b, 0] & 1)
            at = pl.ds(pl.multiple_of(half * rows, rows), rows)
            out[b, at, :] = refs[step][...]
            grad[b, at, :] = refs[4 + step][...].astype(F32)

    vmem = pl.BlockSpec(memory_space=pltpu.VMEM)
    smem = pl.BlockSpec(memory_space=pltpu.SMEM)
    return pl.pallas_call(
        kernel,
        in_specs=[smem, smem] + [vmem] * 8,
        out_specs=[vmem] * 2,
        out_shape=[
            jax.ShapeDtypeStruct((2, 2 * rows, depth), BF),
            jax.ShapeDtypeStruct((2, 2 * rows, depth), F32),
        ],
        compiler_params=pltpu.CompilerParams(vmem_limit_bytes=32 * 2**20),
    )(scal, ids, *outs, *grads)


def attn_fwd_kernel(z_ref, q_ref, k_ref, v_ref, o_ref, *, scale):
    z = z_ref[0]
    size = q_ref.shape[0] // 4
    starts = [pl.multiple_of((z ^ h) * size, size) for h in range(4)]
    keys = jnp.concatenate([k_ref[pl.ds(s, size), :] for s in starts], 0)
    values = jnp.concatenate([v_ref[pl.ds(s, size), :] for s in starts], 0)
    first = lax.broadcasted_iota(jnp.int32, (size, 128), 1) < 64
    for j in range(4):
        span = (j + 1) * size
        q = q_ref[pl.ds(starts[j], size), :]
        row = lax.broadcasted_iota(jnp.int32, (size, span), 0) + j * size
        seen = lax.broadcasted_iota(jnp.int32, (size, span), 1) <= row
        outs = []
        for head in range(2):
            lanes = first if head == 0 else ~first
            qh = jnp.where(lanes, q, jnp.zeros_like(q))
            s = mm_cols(qh, keys[:span]) * scale
            s = jnp.where(seen, s, NEG)
            p = jnp.exp(s - jnp.max(s, -1, keepdims=True))
            total = jnp.sum(p, -1, keepdims=True)
            outs.append(mm(p.astype(BF), values[:span]) / total)
        o_ref[pl.ds(starts[j], size), :] = jnp.where(first, outs[0], outs[1]).astype(BF)


def attn_fwd(z, qkv, scale):
    rows, width = qkv.shape
    pairs = width // 3 // 128
    return pl.pallas_call(
        functools.partial(attn_fwd_kernel, scale=scale),
        grid=(pairs,),
        out_shape=jax.ShapeDtypeStruct((rows, width // 3), BF),
        in_specs=[
            pl.BlockSpec(memory_space=pltpu.SMEM),
            pl.BlockSpec((rows, 128), lambda i: (0, i)),
            pl.BlockSpec((rows, 128), lambda i: (0, pairs + i)),
            pl.BlockSpec((rows, 128), lambda i: (0, 2 * pairs + i)),
        ],
        out_specs=pl.BlockSpec((rows, 128), lambda i: (0, i)),
        compiler_params=pltpu.CompilerParams(vmem_limit_bytes=32 * 2**20),
        cost_estimate=pl.CostEstimate(
            flops=4 * rows * rows * width // 3,
            bytes_accessed=rows * width * 3,
            transcendentals=rows * rows * pairs * 2,
        ),
    )(z, qkv, qkv, qkv)


def attn_bwd_kernel(z_ref, q_ref, k_ref, v_ref, g_ref, d_ref, dk_ref, dv_ref, *, scale, pairs):
    z = z_ref[0]
    at = pl.program_id(0)
    size = q_ref.shape[0] // 4
    starts = [pl.multiple_of((z ^ h) * size, size) for h in range(4)]
    keys = jnp.concatenate([k_ref[pl.ds(s, size), :] for s in starts], 0)
    values = jnp.concatenate([v_ref[pl.ds(s, size), :] for s in starts], 0)
    first = lax.broadcasted_iota(jnp.int32, (size, 128), 1) < 64
    dk_ref[...] = jnp.zeros_like(dk_ref)
    dv_ref[...] = jnp.zeros_like(dv_ref)
    for j in range(4):
        span = (j + 1) * size
        q = q_ref[pl.ds(starts[j], size), :]
        grad = g_ref[pl.ds(starts[j], size), :]
        row = lax.broadcasted_iota(jnp.int32, (size, span), 0) + j * size
        seen = lax.broadcasted_iota(jnp.int32, (size, span), 1) <= row
        outs = []
        for head in range(2):
            lanes = first if head == 0 else ~first
            qh = jnp.where(lanes, q, jnp.zeros_like(q))
            gh = jnp.where(lanes, grad, jnp.zeros_like(grad))
            s = mm_cols(qh, keys[:span]) * scale
            s = jnp.where(seen, s, NEG)
            p = jnp.exp(s - jnp.max(s, -1, keepdims=True))
            p = p / jnp.sum(p, -1, keepdims=True)
            dp = mm_cols(gh, values[:span])
            ds = (p * (dp - jnp.sum(p * dp, -1, keepdims=True))).astype(BF)
            dv_ref[0:span, :] += mm_rows(p.astype(BF), gh)
            dk_ref[0:span, :] += mm_rows(ds, qh)
            outs.append(mm(ds, keys[:span]))
        dq = jnp.where(first, outs[0], outs[1]) * scale
        d_ref[pl.ds(starts[j], size), pl.ds(pl.multiple_of(at * 128, 128), 128)] = dq.astype(BF)
    for j in range(4):
        rows = slice(j * size, (j + 1) * size)
        d_ref[pl.ds(starts[j], size), pl.ds(pl.multiple_of((at + pairs) * 128, 128), 128)] = (
            dk_ref[rows, :] * scale
        ).astype(BF)
        d_ref[pl.ds(starts[j], size), pl.ds(pl.multiple_of((at + 2 * pairs) * 128, 128), 128)] = (
            dv_ref[rows, :].astype(BF)
        )


def attn_bwd(z, qkv, grad, scale):
    rows, width = qkv.shape
    pairs = width // 3 // 128
    return pl.pallas_call(
        functools.partial(attn_bwd_kernel, scale=scale, pairs=pairs),
        grid=(pairs,),
        out_shape=jax.ShapeDtypeStruct((rows, width), BF),
        in_specs=[
            pl.BlockSpec(memory_space=pltpu.SMEM),
            pl.BlockSpec((rows, 128), lambda i: (0, i)),
            pl.BlockSpec((rows, 128), lambda i: (0, pairs + i)),
            pl.BlockSpec((rows, 128), lambda i: (0, 2 * pairs + i)),
            pl.BlockSpec((rows, 128), lambda i: (0, i)),
        ],
        out_specs=pl.BlockSpec((rows, width), lambda i: (0, 0)),
        scratch_shapes=[pltpu.VMEM((rows, 128), F32), pltpu.VMEM((rows, 128), F32)],
        compiler_params=pltpu.CompilerParams(vmem_limit_bytes=32 * 2**20),
        cost_estimate=pl.CostEstimate(
            flops=10 * rows * rows * width // 3,
            bytes_accessed=rows * width * 5,
            transcendentals=rows * rows * pairs * 2,
        ),
    )(z, qkv, qkv, qkv, grad)


def cross_probs(q, keys, lanes, seen, scale):
    qh = jnp.where(lanes, q, jnp.zeros_like(q))
    s = jnp.where(seen, mm_cols(qh, keys) * scale, NEG)
    p = jnp.where(seen, jnp.exp(s - jnp.max(s, -1, keepdims=True)), 0.0)
    return qh, p / jnp.sum(p, -1, keepdims=True)


def cross_fwd_kernel(cap_ref, seg_ref, q_ref, k_ref, v_ref, o_ref, *, scale):
    seen = seg_ref[...] == cap_ref[0]
    q, keys, values = q_ref[...], k_ref[...], v_ref[...]
    first = lax.broadcasted_iota(jnp.int32, q.shape, 1) < 64
    outs = []
    for head in range(2):
        _, p = cross_probs(q, keys, first if head == 0 else ~first, seen, scale)
        outs.append(mm(p.astype(BF), values))
    o_ref[...] = jnp.where(first, outs[0], outs[1]).astype(BF)


def cross_fwd(cap, seg, cq, ckv, scale):
    rows, width = cq.shape
    text = ckv.shape[0]
    pairs = width // 128
    return pl.pallas_call(
        functools.partial(cross_fwd_kernel, scale=scale),
        grid=(pairs,),
        out_shape=jax.ShapeDtypeStruct((rows, width), BF),
        in_specs=[
            pl.BlockSpec(memory_space=pltpu.SMEM),
            pl.BlockSpec((1, text), lambda i: (0, 0)),
            pl.BlockSpec((rows, 128), lambda i: (0, i)),
            pl.BlockSpec((text, 128), lambda i: (0, i)),
            pl.BlockSpec((text, 128), lambda i: (0, pairs + i)),
        ],
        out_specs=pl.BlockSpec((rows, 128), lambda i: (0, i)),
        compiler_params=pltpu.CompilerParams(vmem_limit_bytes=32 * 2**20),
        cost_estimate=pl.CostEstimate(
            flops=4 * rows * text * width,
            bytes_accessed=rows * width * 4,
            transcendentals=rows * text * pairs * 2,
        ),
    )(cap, seg, cq, ckv, ckv)


def cross_bwd_kernel(cap_ref, seg_ref, q_ref, k_ref, v_ref, g_ref, dq_ref, dk_ref, dv_ref, *, scale):
    seen = seg_ref[...] == cap_ref[0]
    q, keys, values, grad = q_ref[...], k_ref[...], v_ref[...], g_ref[...]
    first = lax.broadcasted_iota(jnp.int32, q.shape, 1) < 64
    outs = []
    for head in range(2):
        lanes = first if head == 0 else ~first
        qh, p = cross_probs(q, keys, lanes, seen, scale)
        gh = jnp.where(lanes, grad, jnp.zeros_like(grad))
        dp = mm_cols(gh, values)
        ds = (p * (dp - jnp.sum(p * dp, -1, keepdims=True))).astype(BF)
        dv = mm_rows(p.astype(BF), gh)
        dk = mm_rows(ds, qh) * scale
        if head == 0:
            dv_ref[...] = dv
            dk_ref[...] = dk
        else:
            dv_ref[...] += dv
            dk_ref[...] += dk
        outs.append(mm(ds, keys))
    dq_ref[...] = (jnp.where(first, outs[0], outs[1]) * scale).astype(BF)


def cross_bwd(cap, seg, cq, ckv, grad, scale):
    rows, width = cq.shape
    text = ckv.shape[0]
    pairs = width // 128
    return pl.pallas_call(
        functools.partial(cross_bwd_kernel, scale=scale),
        grid=(pairs,),
        out_shape=[
            jax.ShapeDtypeStruct((rows, width), BF),
            jax.ShapeDtypeStruct((text, width), F32),
            jax.ShapeDtypeStruct((text, width), F32),
        ],
        in_specs=[
            pl.BlockSpec(memory_space=pltpu.SMEM),
            pl.BlockSpec((1, text), lambda i: (0, 0)),
            pl.BlockSpec((rows, 128), lambda i: (0, i)),
            pl.BlockSpec((text, 128), lambda i: (0, i)),
            pl.BlockSpec((text, 128), lambda i: (0, pairs + i)),
            pl.BlockSpec((rows, 128), lambda i: (0, i)),
        ],
        out_specs=[
            pl.BlockSpec((rows, 128), lambda i: (0, i)),
            pl.BlockSpec((text, 128), lambda i: (0, i)),
            pl.BlockSpec((text, 128), lambda i: (0, i)),
        ],
        compiler_params=pltpu.CompilerParams(vmem_limit_bytes=32 * 2**20),
        cost_estimate=pl.CostEstimate(
            flops=10 * rows * text * width,
            bytes_accessed=rows * width * 6,
            transcendentals=rows * text * pairs * 2,
        ),
    )(cap, seg, cq, ckv, ckv, grad)


def long_masks(g, rows):
    slot = jnp.arange(rows, dtype=jnp.int32) // (2 * STRIPE)
    rest = jnp.arange(rows, dtype=jnp.int32) % (2 * STRIPE)

    def positions(r):
        return ((g.z ^ slot) * g.t + r) * (2 * STRIPE) + rest

    key_pos = jnp.concatenate([positions((g.r - q) % g.t) for q in range(g.t)])
    return key_pos[None, :] <= positions(g.r)[:, None]


def long_gather(g, value):
    return jnp.concatenate([value] + [g.over_r(value, q) for q in range(1, g.t)], 0)


def long_fwd(g, qkv, scale):
    rows, width = qkv.shape
    head = 64
    heads = width // 3 // head
    keyval = long_gather(g, qkv[:, width // 3 :])
    q = qkv[:, : width // 3].reshape(rows, heads, head)
    k = keyval[:, : width // 3].reshape(-1, heads, head)
    v = keyval[:, width // 3 :].reshape(-1, heads, head)
    seen = long_masks(g, rows)[None]
    s = jnp.einsum("qhd,khd->hqk", q, k, preferred_element_type=F32) * scale
    s = jnp.where(seen, s, NEG)
    p = jnp.exp(s - jnp.max(s, -1, keepdims=True))
    p = p / jnp.sum(p, -1, keepdims=True)
    out = jnp.einsum("hqk,khd->qhd", p.astype(BF), v, preferred_element_type=F32)
    return out.reshape(rows, width // 3).astype(BF), (q, k, v, p)


def long_bwd(g, saved, grad, scale):
    q, k, v, p = saved
    rows, heads, head = q.shape
    width = heads * head
    grad = grad.reshape(rows, heads, head)
    dv = jnp.einsum("hqk,qhd->khd", p.astype(BF), grad, preferred_element_type=F32)
    dp = jnp.einsum("qhd,khd->hqk", grad, v, preferred_element_type=F32)
    ds = (p * (dp - jnp.sum(p * dp, -1, keepdims=True))).astype(BF)
    dq = jnp.einsum("hqk,khd->qhd", ds, k, preferred_element_type=F32) * scale
    dk = jnp.einsum("hqk,qhd->khd", ds, q, preferred_element_type=F32) * scale
    both = jnp.concatenate([dk.reshape(-1, width), dv.reshape(-1, width)], 1)
    both = both.reshape(g.t, rows, 2 * width)
    total = both[0]
    for step in range(1, g.t):
        total = total + g.over_r(both[step], -step)
    return jnp.concatenate([dq.reshape(rows, width).astype(BF), total.astype(BF)], 1)


def normed(values):
    center = values - jnp.mean(values, -1, keepdims=True)
    spread = lax.rsqrt(jnp.mean(center * center, -1, keepdims=True) + EPS)
    return center * spread, spread


def norm_back(unit, spread, gain, grad):
    f = grad * gain
    added = spread * (
        f - jnp.mean(f, -1, keepdims=True) - unit * jnp.mean(f * unit, -1, keepdims=True)
    )
    return added, jnp.sum(grad * unit, 0), jnp.sum(grad, 0)


def column_halves(weight, groups, mine):
    rows, width = weight.shape
    parts = weight.reshape(rows, groups, 2, width // groups // 2)
    return (
        pick(parts, 2, mine).reshape(rows, width // 2),
        pick(parts, 2, 1 - mine).reshape(rows, width // 2),
    )


def two(g, mine, other, axis):
    first = jnp.where(g.c == 0, mine, other)
    second = jnp.where(g.c == 0, other, mine)
    return jnp.stack([first, second], axis)


def gather_fast(g, scal, weights, ids, tokens, cotangent):
    gains, shifts, w_qkv, w_out, w_cq, w_ckv, w_co, w_up, w_down = weights
    share, depth = w_co.shape
    tall = w_down.shape[0]
    small = jnp.concatenate([gains, shifts], 0).T
    small = jnp.pad(small, ((0, 0), (0, 128 - small.shape[1])))
    keep1, send1 = prep_weights(scal, [(w_qkv, 6), (small, 0), (w_cq, 2)])
    keep2, send2 = prep_weights(scal, [(w_ckv, 4)], w_out)
    keep3, send3 = prep_weights(scal, [(w_up, 2)])
    blocks = prep_tokens(scal, ids, tokens, cotangent)
    got1 = g.over_c(send1)
    got2 = g.over_c(jnp.concatenate([send2, send3], 1))

    def shape(kinds, rows, width):
        return (2, kinds, 4, 2, rows, width)

    n_qkv, n_cq, n_ckv, n_up = (w.shape[1] // 2 for w in (w_qkv, w_cq, w_ckv, w_up))
    groups = tall // share // 2
    low, high = (
        list(half.reshape(groups, share, depth))
        for half in (w_down[: tall // 2], w_down[tall // 2 :])
    )
    second = jnp.stack([keep2, jnp.concatenate([got2[:, :n_ckv], w_co], 1)])
    third = jnp.stack(
        [jnp.concatenate([keep3] + low, 1), jnp.concatenate([got2[:, n_ckv:]] + high, 1)]
    )
    first = after(jnp.stack([keep1, got1]), second, third)
    third_low, third_high = third[:1], third[1:]
    tok, cot = list(blocks[:4]), list(blocks[4:])

    def near(lines):
        return g.over_x(lines[0]), g.over_y(lines[1])

    def far(lines, got):
        pair_a, pair_b = jnp.stack([lines[0], got[0]]), jnp.stack([lines[1], got[1]])
        return pair_a, g.over_y(pair_a), pair_b, g.over_x(pair_b)

    got_a = [first] + [g.xor_z(first, k) for k in (1, 2, 3)]
    tok[0], cot[0] = g.regroup(tok[0], 0), g.regroup(cot[0], 0)
    line_a = gather_line(scal, got_a)

    line_a, second = after((line_a, second), got_a, tok[0], cot[0])
    near_a = near(line_a)
    got_b = [second] + [g.xor_z(second, k) for k in (1, 2)]

    near_a, second, third, third_low = after((near_a, second, third, third_low), got_b)
    far_a = far(line_a, near_a)
    got_b.append(g.xor_z(second, 3))
    got_c1 = g.xor_z(third, 1)
    got_c2 = g.xor_z(third_low, 2)
    line_b = gather_line(scal, got_b)

    line_b, third_high = after((line_b, third_high), far_a, got_c1, got_c2)
    near_b = near(line_b)
    got_c2 = jnp.concatenate([got_c2, g.xor_z(third_high, 2)], 0)

    near_b, third = after((near_b, third), got_c2)
    far_b = far(line_b, near_b)
    got_c = [third, got_c1, got_c2, g.xor_z(third, 3)]
    line_c = gather_line(scal, got_c)

    line_c, *late = after((line_c, *tok[1:]), far_b)
    near_c = near(line_c)
    tok = [tok[0]] + [g.regroup(late[k - 1], k) for k in (1, 2, 3)]

    near_c, *late = after((near_c, *cot[1:]), tok)
    far_c = far(line_c, near_c)
    resid = join_tokens(scal, tok, g.over_c(jnp.stack(tok)))
    cot = [cot[0]] + [g.regroup(late[k - 1], k) for k in (1, 2, 3)]
    cot = join_tokens(scal, cot, g.over_c(jnp.stack(cot)))

    qkv, small, cq = gather_place(
        scal,
        *far_a,
        [shape(2, share, n_qkv), shape(2, share, 128), shape(2, share, n_cq)],
        [[(n_qkv, 0, None, 0), (128, 1, None, 0), (n_cq, 2, None, 0)]] * 2,
    )
    ckv, out, co = gather_place(
        scal,
        *far_b,
        [shape(2, share, n_ckv), shape(1, share, depth), shape(1, share, depth)],
        [[(n_ckv, 0, None, 0), (depth, 1 + half, 0, 0)] for half in range(2)],
    )
    up, down = gather_place(
        scal,
        *far_c,
        [shape(2, share, n_up), shape(1, tall, depth)],
        [
            [(n_up, 0, None, 0)]
            + [(depth, 1, 0, (half * groups + i) * share) for i in range(groups)]
            for half in range(2)
        ],
    )

    def flat(array):
        return array.reshape(-1, array.shape[-1])

    return (
        resid,
        cot,
        flat(small)[:, :6].astype(F32).T,
    ) + tuple(flat(array) for array in (qkv, out, cq, ckv, co, up, down))


def gather_plain(g, weights):
    gains, shifts, w_qkv, w_out, w_cq, w_ckv, w_co, w_up, w_down = weights
    small = lax.all_gather(jnp.concatenate([gains, shifts], 0), AXES, axis=1, tiled=True)

    def columns(weight, groups):
        whole = lax.all_gather(weight, AXES, axis=0, tiled=True)
        return column_halves(whole, groups, g.c)[0]

    def rows(weight):
        whole = lax.all_gather(weight, AXES, axis=0, tiled=True)
        parts = whole.reshape(2, 2, whole.shape[0] // 4, whole.shape[1])
        return pick(parts, 1, g.c).reshape(whole.shape[0] // 2, whole.shape[1])

    return (
        small.astype(F32),
        columns(w_qkv, 6),
        rows(w_out),
        columns(w_cq, 2),
        columns(w_ckv, 4),
        rows(w_co),
        columns(w_up, 2),
        rows(w_down),
    )


def join_columns(g, keep, got, groups):
    rows, width = keep.shape
    block = width // groups
    parts = two(g, keep.reshape(rows, groups, block), got.reshape(rows, groups, block), 2)
    return parts.reshape(rows, 2 * width)


def scatter_columns_plain(g, grad, groups):
    rows, width = grad.shape
    whole = join_columns(g, grad, jnp.zeros_like(grad), groups)
    return lax.psum_scatter(whole, AXES, scatter_dimension=0, tiled=True)


def scatter_rows_plain(g, grad):
    rows, width = grad.shape
    parts = grad.reshape(2, rows // 2, width)
    whole = two(g, parts, jnp.zeros_like(parts), 1).reshape(2 * rows, width)
    return lax.psum_scatter(whole, AXES, scatter_dimension=0, tiled=True)


def both_cores(g, part):
    low = part.astype(BF)
    return low.astype(F32) + g.over_c(low).astype(F32)


def local(
    tokens,
    text_states,
    image_ids,
    text_segments,
    image_caption,
    norm_gains,
    norm_shifts,
    self_qkv,
    self_out,
    cross_query,
    cross_keyval,
    cross_out,
    mlp_up,
    mlp_down,
    cotangent,
    *,
    dp,
    seq,
):
    g = Grid(dp, seq)
    fast = g.t == 1
    depth = tokens.shape[-1]
    scale = (depth // H) ** (-0.5)
    weights = (
        norm_gains,
        norm_shifts,
        self_qkv,
        self_out,
        cross_query,
        cross_keyval,
        cross_out,
        mlp_up,
        mlp_down,
    )

    scal = jnp.stack([g.x, g.c, g.z, g.y]).astype(jnp.int32)
    start = image_ids[:, 0] & 1
    if fast:
        (resid, cot, small, w_qkv, w_out, w_cq, w_ckv, w_co, w_up, w_down) = gather_fast(
            g, scal, weights, image_ids, tokens, cotangent
        )
    else:
        (small, w_qkv, w_out, w_cq, w_ckv, w_co, w_up, w_down) = gather_plain(g, weights)
        both = jnp.stack([tokens, cotangent], 2).reshape(4, STRIPE, 2 * depth)
        received = []
        for step in range(4):
            j = g.z ^ step
            half = (j & 1) ^ start[j >> 1]
            received.append(g.regroup(pick(both, 0, (j >> 1) * 2 + half), step))
        mine = jnp.stack(received)
        held = two(g, mine, g.over_c(mine), 1).reshape(8 * STRIPE, 2, depth)
        resid, cot = held[:, 0], held[:, 1]
    resid = resid.astype(F32)
    gain, shift = small[:3], small[3:]

    image = (g.x * 2 + g.y) * 2 + (g.z & 1)
    cap = image_caption[g.z >> 1, image].reshape(1)
    seg = text_segments.reshape(1, -1)
    slot = g.z.reshape(1).astype(jnp.int32)

    unit_one, spread_one = normed(resid)
    n_one = (unit_one * gain[0] + shift[0]).astype(BF)
    qkv = mm(n_one, w_qkv).astype(BF)
    if fast:
        attended = attn_fwd(slot, qkv, scale)
    else:
        attended, saved = long_fwd(g, qkv, scale)
    hidden_one = resid + both_cores(g, mm(attended, w_out))
    unit_two, spread_two = normed(hidden_one)
    n_two = (unit_two * gain[1] + shift[1]).astype(BF)
    cq = mm(n_two, w_cq).astype(BF)
    ckv = mm(text_states, w_ckv).astype(BF)
    crossed = cross_fwd(cap, seg, cq, ckv, scale)
    hidden_two = hidden_one + both_cores(g, mm(crossed, w_co))
    unit_three, spread_three = normed(hidden_two)
    n_three = (unit_three * gain[2] + shift[2]).astype(BF)
    up = mm(n_three, w_up)
    inner = jnp.tanh(GELU_C * (up + 0.044715 * up * up * up))
    act = (0.5 * up * (1.0 + inner)).astype(BF)

    def halves(value):
        parts = value.reshape(4, 2, STRIPE, value.shape[-1])
        return pick(parts, 1, g.c), pick(parts, 1, 1 - g.c)

    down = mm(act, w_down)
    keep, gone = halves(down)
    out = (halves(hidden_two)[0] + keep + g.over_c(gone.astype(BF)).astype(F32)).astype(BF)

    grad_down = mm_rows(act, cot)
    slope = 0.5 * (1.0 + inner) + 0.5 * up * (1.0 - inner * inner) * GELU_C * (
        1.0 + 3 * 0.044715 * up * up
    )
    d_up = (mm_cols(cot, w_down) * slope).astype(BF)
    grad_up = mm_rows(n_three, d_up)
    share = depth // g.count
    if fast:
        grad_down, grad_up = grad_down.astype(BF), grad_up.astype(BF)
        mlp = Scatter(g, scal, share, by_rows(grad_down, share) + by_columns(grad_up, share))
        folded, out = after((mlp.fold_far(), out))
        done = mlp.send_far(folded)
        out_home = [g.regroup(out[step], step) for step in range(4)]
    added, gain_three, shift_three = norm_back(
        unit_three, spread_three, gain[2], both_cores(g, mm_cols(d_up, w_up))
    )
    g_two = cot.astype(F32) + added
    d_cross = g_two.astype(BF)
    grad_co = mm_rows(crossed, d_cross)
    d_crossed = mm_cols(d_cross, w_co).astype(BF)
    d_cq, d_ck, d_cv = cross_bwd(cap, seg, cq, ckv, d_crossed, scale)
    grad_cq = mm_rows(n_two, d_cq)
    added, gain_two, shift_two = norm_back(
        unit_two, spread_two, gain[1], both_cores(g, mm_cols(d_cq, w_cq))
    )
    g_one = g_two + added
    d_self = g_one.astype(BF)
    grad_out = mm_rows(attended, d_self)
    d_att = mm_cols(d_self, w_out).astype(BF)
    if fast:
        grad_co, grad_cq = grad_co.astype(BF), grad_cq.astype(BF)
        cross = Scatter(g, scal, share, by_rows(grad_co, share) + by_columns(grad_cq, share))
        d_ckv = jnp.concatenate([d_ck, d_cv], 1).astype(BF)
        folded, swapped = after((mlp.fold_near(), d_ckv), done, out_home)
        done = mlp.send_near(folded), g.xor_z(swapped, 1)
        d_qkv = attn_bwd(slot, qkv, after(d_att, folded), scale)
        d_ckv = plus(d_ckv, done[1])
        folded, swapped = after((cross.fold_far(), d_ckv), done)
        mlp_line = mlp.line()
        done = cross.send_far(folded), g.xor_z(swapped, 2)
        d_ckv = plus(d_ckv, done[1])
    else:
        d_qkv = long_bwd(g, saved, d_att, scale)
    grad_qkv = mm_rows(n_one, d_qkv)
    added, gain_one, shift_one = norm_back(
        unit_one, spread_one, gain[0], both_cores(g, mm_cols(d_qkv, w_qkv))
    )
    grad_in = (g_one + added).astype(BF)

    norms = jnp.stack([gain_one, gain_two, gain_three, shift_one, shift_two, shift_three])
    back = halves(grad_in)[0]
    if fast:
        grad_out, grad_qkv = grad_out.astype(BF), grad_qkv.astype(BF)
        last = Scatter(
            g, scal, share, by_rows(grad_out, share) + by_columns(grad_qkv, share)
        )
        folded, mlp_line = after((last.fold_far(), mlp_line), done)
        mlp_terms = [mlp_line[0]] + [g.xor_z(mlp_line[k], k) for k in (1, 2)]
        done = last.send_far(folded), mlp_terms[1:]
        folded = last.fold_near(), cross.fold_near()
        folded, mlp_line = after((folded, mlp_line), done)
        mlp_terms.append(g.xor_z(mlp_line[3], 3))
        done = last.send_near(folded[0]), cross.send_near(folded[1]), mlp_terms[3]
        lines = [jnp.concatenate(pair, 2) for pair in zip(cross.line(), last.line())]
        lines, back, d_ckv, norms = after((lines, back, d_ckv, norms), done)
        last_terms = spread(g, lines)
        back = [g.regroup(back[step], step) for step in range(4)]
        mlp_terms = after(mlp_terms, lines)
        d_ckv = plus(d_ckv, g.over_x(d_ckv))
        norms = norms + g.over_y(norms)
        d_ckv = plus(d_ckv, g.over_y(d_ckv))
        norms = norms + g.over_x(norms)
        norms = norms + g.xor_z(norms, 1)
        norms = norms + g.xor_z(norms, 2)
        norms = lax.dynamic_slice_in_dim(norms, g.me * share, share, 1)
        output, grad_tokens = place_home(scal, image_ids, out_home, back)
        n_cross = cross.width()
        cross_terms = [term[:, :, : n_cross] for term in last_terms]
        last_terms = [term[:, :, n_cross:] for term in last_terms]
        d_ckv_whole = join_columns(g, d_ckv, g.over_c(d_ckv), 4)
    else:
        back = jnp.concatenate([out, back], 2)
        back = jnp.stack([g.regroup(back[step], step) for step in range(4)])
        order = []
        for block in range(4):
            j = (block & 2) + ((block & 1) ^ start[block >> 1])
            order.append(pick(back, 0, j ^ g.z))
        back = jnp.stack(order).reshape(2, 2 * STRIPE, 2 * depth)
        output, grad_tokens = back[:, :, :depth], back[:, :, depth:].astype(F32)
        d_ckv = jnp.concatenate([d_ck, d_cv], 1)
        whole = join_columns(g, d_ckv, jnp.zeros_like(d_ckv), 4)
        d_ckv_whole = lax.psum(whole, AXES).astype(BF)
        d_ckv = column_halves(d_ckv_whole, 4, g.c)[0]
        norms = lax.psum(norms, AXES) * 0.5
        norms = lax.dynamic_slice_in_dim(norms, g.me * (depth // g.count), depth // g.count, 1)
    part = mm_cols(d_ckv, w_ckv)
    grad_text = part + g.over_c(part)
    text_cols = lax.dynamic_slice_in_dim(text_states, g.me * share, share, 1)
    grad_ckv = mm_rows(text_cols, d_ckv_whole)
    if fast:
        tall = mlp_down.shape[0]

        def columns(terms, low, high, groups):
            got = g.over_c(plus(*[pick(term, 0, 1 - g.c)[:, low:high] for term in terms]))
            keep = sum(pick(term, 0, g.c)[:, low:high].astype(F32) for term in terms)
            return join_columns(g, keep, got.astype(F32), groups)

        terms = mlp_terms
        n_down = tall // share // 2 * depth
        grad_down = summed(terms, ALL, ALL, slice(0, n_down))
        grad_down = grad_down.reshape(2, share, tall // share // 2, depth)
        grad_down = grad_down.transpose(0, 2, 1, 3).reshape(tall, depth)
        grad_up = columns(terms, n_down, None, 2)
        terms = cross_terms
        half = depth // 2
        co = summed(terms, ALL, ALL, slice(0, half))
        grad_co = jnp.concatenate([co[0], co[1]], 1)
        grad_cq = columns(terms, half, None, 2)
        terms = last_terms
        out_sum = summed(terms, ALL, ALL, slice(0, half))
        grad_out = jnp.concatenate([out_sum[0], out_sum[1]], 1)
        grad_qkv = columns(terms, half, None, 6)
    else:
        grad_down = scatter_rows_plain(g, grad_down)
        grad_up = scatter_columns_plain(g, grad_up, 2)
        grad_co = scatter_rows_plain(g, grad_co)
        grad_cq = scatter_columns_plain(g, grad_cq, 2)
        grad_out = scatter_rows_plain(g, grad_out)
        grad_qkv = scatter_columns_plain(g, grad_qkv, 6)
    return (
        output,
        grad_tokens,
        grad_text,
        norms[:3],
        norms[3:5],
        grad_qkv,
        grad_out,
        grad_cq,
        grad_ckv,
        grad_co,
        grad_up,
        grad_down,
        norms[5],
    )


def solution(mesh):
    both = ("dp", "seq")
    rows = P(both, None)
    in_specs = (
        P(None, both, None),
        P(),
        P(None, both),
        P(),
        P(),
        P(None, both),
        P(None, both),
        rows,
        rows,
        rows,
        rows,
        rows,
        rows,
        rows,
        P(None, both, None),
    )
    out_specs = (
        P(None, both, None),
        P(None, both, None),
        P(),
        P(None, both),
        P(None, both),
        rows,
        rows,
        rows,
        rows,
        rows,
        rows,
        rows,
        P(both),
    )
    body = functools.partial(local, dp=mesh.shape["dp"], seq=mesh.shape["seq"])
    return jax.shard_map(body, mesh=mesh, in_specs=in_specs, out_specs=out_specs, check_vma=False)
```

```python
import functools

import jax
import jax.numpy as jnp
from jax import lax
from jax.experimental import pallas as pl
from jax.experimental.pallas import tpu as pltpu
from jax.sharding import PartitionSpec as P

H = 16
STRIPE = 64
EPS = 1e-05
NEG = -1e30
GELU_C = 0.7978845608028654
BF = jnp.bfloat16
F32 = jnp.float32
AXES = ("dp", "seq")


def mm(left, right):
    return jnp.dot(left, right, preferred_element_type=F32)


def mm_rows(left, right):
    return lax.dot_general(left, right, (((0,), (0,)), ((), ())), preferred_element_type=F32)


def mm_cols(left, right):
    return lax.dot_general(left, right, (((1,), (1,)), ((), ())), preferred_element_type=F32)


def pick(array, dim, index):
    return lax.dynamic_index_in_dim(array, index, dim, keepdims=False)


class Grid:
    def __init__(self, dp, seq):
        self.dp, self.seq, self.t = dp, seq, seq // 8
        self.count = dp * seq
        me = lax.axis_index(AXES)
        part = lax.rem(me, seq)
        self.me = me
        self.x = me // (2 * seq)
        self.c = lax.rem(me // seq, 2)
        self.z = part // (2 * self.t)
        self.r = lax.rem(part // 2, self.t)
        self.y = lax.rem(part, 2)

    def coords(self, d):
        part = d % self.seq
        return (
            d // (2 * self.seq),
            d // self.seq % 2,
            part // (2 * self.t),
            part // 2 % self.t,
            part % 2,
        )

    def index(self, x, c, z, r, y):
        return (x * 2 + c) * self.seq + (z * self.t + r) * 2 + y

    def send(self, value, move):
        perm = [(d, self.index(*move(*self.coords(d)))) for d in range(self.count)]
        return lax.ppermute(value, AXES, perm)

    def over_c(self, value):
        return self.send(value, lambda x, c, z, r, y: (x, 1 - c, z, r, y))

    def over_x(self, value):
        return self.send(value, lambda x, c, z, r, y: (1 - x, c, z, r, y))

    def over_y(self, value):
        return self.send(value, lambda x, c, z, r, y: (x, c, z, r, 1 - y))

    def xor_z(self, value, bits):
        return self.send(value, lambda x, c, z, r, y: (x, c, z ^ bits, r, y))

    def over_r(self, value, step):
        return self.send(value, lambda x, c, z, r, y: (x, c, z, (r + step) % self.t, y))

    def regroup(self, value, bits):
        return self.send(value, lambda x, c, z, r, y: (x, y, z ^ bits, r, c))

    def gather_near(self, lines):
        return self.over_x(lines[0]), self.over_y(lines[1])

    def gather_far(self, lines, got):
        pair_a, pair_b = jnp.stack([lines[0], got[0]]), jnp.stack([lines[1], got[1]])
        return pair_a, self.over_y(pair_a), pair_b, self.over_x(pair_b)

    def swap(self, value):
        return self.send(value, lambda x, c, z, r, y: (x, y, z, r, c))


def after(value, *others):
    return lax.optimization_barrier((value, others))[0]


def place(scalars, sources, shapes, copies):
    def kernel(s_ref, *refs):
        ins = refs[: len(sources)]
        outs = refs[len(sources) : len(sources) + len(shapes)]
        sems = refs[-1]
        started = []
        for i, (source, at, target, to) in enumerate(copies):
            copy = pltpu.make_async_copy(
                ins[source].at[at(s_ref)], outs[target].at[to(s_ref)], sems.at[i]
            )
            copy.start()
            started.append(copy)
        for copy in started:
            copy.wait()

    moved = sum(source.size * 2 for source in sources)
    return pl.pallas_call(
        kernel,
        out_shape=[jax.ShapeDtypeStruct(shape, BF) for shape in shapes],
        in_specs=[pl.BlockSpec(memory_space=pltpu.SMEM)]
        + [pl.BlockSpec(memory_space=pl.ANY)] * len(sources),
        out_specs=[pl.BlockSpec(memory_space=pltpu.VMEM)] * len(shapes),
        scratch_shapes=[pltpu.SemaphoreType.DMA((len(copies),))],
        compiler_params=pltpu.CompilerParams(vmem_limit_bytes=32 * 2**20),
        cost_estimate=pl.CostEstimate(flops=0, bytes_accessed=2 * moved, transcendentals=0),
    )(scalars, *sources)


ALL = slice(None)


def gather_line(scal, got):
    _, rows, width = got[0].shape
    return place(
        scal,
        got,
        [(4, rows, width)] * 2,
        [
            (k, lambda s, h=h: (h,), h, lambda s, k=k: (s[2] ^ k,))
            for k in range(4)
            for h in range(2)
        ],
    )


def gather_place(scal, pair_a, far_a, pair_b, far_b, shapes, targets):
    rows = pair_a.shape[2]
    copies = []
    for i, half in enumerate((0, 0, 1, 1)):
        far = i % 2
        for near in range(2):
            dx, dy = (near, far) if half == 0 else (far, near)
            start = 0
            for wide, out, kind, row in targets[half]:
                copies.append(
                    (
                        i,
                        lambda s, near=near, start=start, wide=wide: (
                            near,
                            ALL,
                            ALL,
                            pl.ds(start, wide),
                        ),
                        out,
                        lambda s, dx=dx, dy=dy, kind=kind, row=row, half=half: (
                            s[0] ^ dx,
                            s[1] ^ half if kind is None else kind,
                            ALL,
                            s[3] ^ dy,
                            pl.ds(row, rows),
                        ),
                    )
                )
                start += wide
    return place(scal, [pair_a, far_a, pair_b, far_b], shapes, copies)


def plus(*terms):
    total = terms[0].astype(F32)
    for term in terms[1:]:
        total = total + term.astype(F32)
    return total.astype(BF)


def by_columns(array, share):
    view = array.reshape(2, 2, 4, 2, share, array.shape[1])
    block = (None, None, None, None, share, array.shape[1])
    return [(view, block, lambda x, z, y, h, i: (x, h, z, y, 0, 0))]


def by_rows(array, share):
    groups, width = array.shape[0] // (16 * share), array.shape[1]
    if groups == 1:
        view = array.reshape(2, 4, 2, share, width)
        block = (None, None, None, share, width // 2)
        return [(view, block, lambda x, z, y, h, i: (x, z, y, 0, h))]
    view = array.reshape(2, 4, 2, groups, share, width)
    block = (None, None, None, None, share, width)
    return [
        (view, block, lambda x, z, y, h, i, j=j: (x, z, y, h * (groups // 2) + j, 0, 0))
        for j in range(groups // 2)
    ]


def by_steps(array):
    return [(array, (None, None) + array.shape[2:], lambda x, z, y, h, i: (i, h, 0, 0))]


def fold(scal, groups, steps, share, places, outs):
    arrays, specs, parts, width = [], [], [], 0
    for slots, received in groups:
        wide = sum(block[-1] for _, block, _ in slots)
        for h in range(2):
            extras, at = [], 0
            for array, at_step in received[h]:
                extras.append(len(arrays))
                arrays.append(array)
                specs.append(
                    pl.BlockSpec(
                        (None, share, wide),
                        lambda i, s, f=at_step: (f(i, s), 0, 0),
                    )
                )
            for view, block, index in slots:
                parts.append((h, len(arrays), extras, at, width + at, block[-1]))
                arrays.append(view)
                specs.append(
                    pl.BlockSpec(block, lambda i, s, h=h, f=index: f(*places[h](i, s), h, i))
                )
                at += block[-1]
        width += wide

    def kernel(s_ref, *refs):
        step = pl.program_id(0)
        ins, targets = refs[: len(arrays)], refs[len(arrays) :]
        for h, own, extras, at, to, wide in parts:
            value = ins[own][...]
            if extras:
                value = value.astype(F32)
                for extra in extras:
                    value = value + ins[extra][:, pl.ds(at, wide)].astype(F32)
                value = value.astype(BF)
            if outs is None:
                targets[h][:, pl.ds(to, wide)] = value
            else:
                for j in range(steps):

                    @pl.when(step == j)
                    def _():
                        targets[j][h, :, pl.ds(to, wide)] = value

    if outs is None:
        out_shape = [jax.ShapeDtypeStruct((steps, share, width), BF)] * 2
        out_specs = [pl.BlockSpec((None, share, width), lambda i, s: (i, 0, 0))] * 2
    else:
        out_shape = [jax.ShapeDtypeStruct((2, share, width), BF)] * steps
        out_specs = [pl.BlockSpec((2, share, width), lambda i, s: (0, 0, 0))] * steps
    return pl.pallas_call(
        kernel,
        grid_spec=pltpu.PrefetchScalarGridSpec(
            num_scalar_prefetch=1, grid=(steps,), in_specs=specs, out_specs=out_specs
        ),
        out_shape=out_shape,
        compiler_params=pltpu.CompilerParams(vmem_limit_bytes=32 * 2**20),
        cost_estimate=pl.CostEstimate(
            flops=0, bytes_accessed=2 * steps * share * width * 6, transcendentals=0
        ),
    )(scal, *arrays)


def fold_far(scal, share, slots):
    return fold(
        scal,
        [(slots, [[], []])],
        8,
        share,
        [
            lambda i, s: (i // 4, lax.rem(i, 4), 1 - s[3]),
            lambda i, s: (1 - s[0], i // 2, lax.rem(i, 2)),
        ],
        None,
    )


def fold_near(scal, share, chunks):
    return fold(
        scal,
        [
            (
                slots,
                [
                    [(far[0], lambda i, s: (1 - s[0]) * 4 + i)],
                    [(far[1], lambda i, s: i * 2 + 1 - s[3])],
                ],
            )
            for slots, far in chunks
        ],
        4,
        share,
        [lambda i, s: (1 - s[0], i, s[3]), lambda i, s: (s[0], i, 1 - s[3])],
        None,
    )


def fold_line(scal, share, chunks, more=()):
    groups = []
    for slots, far, near in chunks:
        groups.append(
            (
                slots,
                [
                    [
                        (far[0], lambda i, s: s[0] * 4 + (s[2] ^ i)),
                        (near[0], lambda i, s: s[2] ^ i),
                    ],
                    [
                        (far[1], lambda i, s: (s[2] ^ i) * 2 + s[3]),
                        (near[1], lambda i, s: s[2] ^ i),
                    ],
                ],
            )
        )
    if more:
        groups.append((list(more), [[], []]))
    return fold(
        scal, groups, 4, share, [lambda i, s: (s[0], s[2] ^ i, s[3])] * 2, True
    )


def summed(terms, *at):
    return sum(term[at].astype(F32) for term in terms)


def prep_weights(scal, sources, whole=None):
    share = sources[0][0].shape[0]
    more = 0 if whole is None else whole.shape[1]
    width = sum(array.shape[1] // (2 if groups else 1) for array, groups in sources)

    def kernel(s_ref, *refs):
        low = s_ref[1] == 0
        keep, send = refs[-2:]
        start = 0
        for ref, (_, groups) in zip(refs, sources):
            if groups == 0:
                keep[:, pl.ds(start, ref.shape[1])] = ref[...]
                send[:, pl.ds(start, ref.shape[1])] = ref[...]
                start += ref.shape[1]
                continue
            block = ref.shape[1] // groups // 2
            for i in range(groups):
                a = ref[:, pl.ds(2 * i * block, block)]
                b = ref[:, pl.ds((2 * i + 1) * block, block)]
                keep[:, pl.ds(start, block)] = jnp.where(low, a, b)
                send[:, pl.ds(start, block)] = jnp.where(low, b, a)
                start += block
        if whole is not None:
            keep[:, pl.ds(start, more)] = refs[len(sources)][...]

    vmem = pl.BlockSpec(memory_space=pltpu.VMEM)
    smem = pl.BlockSpec(memory_space=pltpu.SMEM)
    arrays = [array for array, _ in sources] + ([] if whole is None else [whole])
    return pl.pallas_call(
        kernel,
        in_specs=[smem] + [vmem] * len(arrays),
        out_specs=[vmem] * 2,
        out_shape=[
            jax.ShapeDtypeStruct((share, width + more), BF),
            jax.ShapeDtypeStruct((share, width), BF),
        ],
        compiler_params=pltpu.CompilerParams(vmem_limit_bytes=32 * 2**20),
    )(scal, *arrays)


def prep_tokens(scal, ids, tokens, cotangent):
    depth = tokens.shape[2]

    def kernel(s_ref, ids_ref, tok, cot, *blocks):
        for step in range(4):
            j = s_ref[2] ^ step
            b = j >> 1
            half = (j & 1) ^ (ids_ref[b, 0] & 1)
            rows = pl.ds(pl.multiple_of(half * STRIPE, STRIPE), STRIPE)
            blocks[step][...] = tok[b, rows, :]
            blocks[4 + step][...] = cot[b, rows, :]

    vmem = pl.BlockSpec(memory_space=pltpu.VMEM)
    smem = pl.BlockSpec(memory_space=pltpu.SMEM)
    return pl.pallas_call(
        kernel,
        in_specs=[smem, smem, vmem, vmem],
        out_specs=[vmem] * 8,
        out_shape=[jax.ShapeDtypeStruct((STRIPE, depth), BF)] * 8,
        compiler_params=pltpu.CompilerParams(vmem_limit_bytes=32 * 2**20),
    )(scal, ids, tokens, cotangent)


def join_tokens(scal, mine, other):
    _, rows, depth = other.shape

    def kernel(s_ref, a0, a1, a2, a3, o_ref, out):
        for step, ref in enumerate((a0, a1, a2, a3)):
            for part, core in ((ref, s_ref[1]), (o_ref.at[step], 1 - s_ref[1])):
                at = pl.ds(pl.multiple_of((2 * step + core) * rows, rows), rows)
                out[at, :] = part[...]

    vmem = pl.BlockSpec(memory_space=pltpu.VMEM)
    return pl.pallas_call(
        kernel,
        in_specs=[pl.BlockSpec(memory_space=pltpu.SMEM)] + [vmem] * 5,
        out_specs=vmem,
        out_shape=jax.ShapeDtypeStruct((8 * rows, depth), BF),
        compiler_params=pltpu.CompilerParams(vmem_limit_bytes=32 * 2**20),
    )(scal, *mine, other)


def place_home(scal, ids, outs, grads):
    rows, depth = outs[0].shape

    def kernel(s_ref, ids_ref, *refs):
        out, grad = refs[8:]
        for step in range(4):
            j = s_ref[2] ^ step
            b = j >> 1
            half = (j & 1) ^ (ids_ref[b, 0] & 1)
            at = pl.ds(pl.multiple_of(half * rows, rows), rows)
            out[b, at, :] = refs[step][...]
            grad[b, at, :] = refs[4 + step][...].astype(F32)

    vmem = pl.BlockSpec(memory_space=pltpu.VMEM)
    smem = pl.BlockSpec(memory_space=pltpu.SMEM)
    return pl.pallas_call(
        kernel,
        in_specs=[smem, smem] + [vmem] * 8,
        out_specs=[vmem] * 2,
        out_shape=[
            jax.ShapeDtypeStruct((2, 2 * rows, depth), BF),
            jax.ShapeDtypeStruct((2, 2 * rows, depth), F32),
        ],
        compiler_params=pltpu.CompilerParams(vmem_limit_bytes=32 * 2**20),
    )(scal, ids, *outs, *grads)


def attn_fwd_kernel(z_ref, q_ref, k_ref, v_ref, o_ref, *, scale):
    z = z_ref[0]
    size = q_ref.shape[0] // 4
    starts = [pl.multiple_of((z ^ h) * size, size) for h in range(4)]
    keys = jnp.concatenate([k_ref[pl.ds(s, size), :] for s in starts], 0)
    values = jnp.concatenate([v_ref[pl.ds(s, size), :] for s in starts], 0)
    first = lax.broadcasted_iota(jnp.int32, (size, 128), 1) < 64
    for j in range(4):
        span = (j + 1) * size
        q = q_ref[pl.ds(starts[j], size), :]
        row = lax.broadcasted_iota(jnp.int32, (size, span), 0) + j * size
        seen = lax.broadcasted_iota(jnp.int32, (size, span), 1) <= row
        outs = []
        for head in range(2):
            lanes = first if head == 0 else ~first
            qh = jnp.where(lanes, q, jnp.zeros_like(q))
            s = mm_cols(qh, keys[:span]) * scale
            s = jnp.where(seen, s, NEG)
            p = jnp.exp(s - jnp.max(s, -1, keepdims=True))
            total = jnp.sum(p, -1, keepdims=True)
            outs.append(mm(p.astype(BF), values[:span]) / total)
        o_ref[pl.ds(starts[j], size), :] = jnp.where(first, outs[0], outs[1]).astype(BF)


def attn_fwd(z, qkv, scale):
    rows, width = qkv.shape
    pairs = width // 3 // 128
    return pl.pallas_call(
        functools.partial(attn_fwd_kernel, scale=scale),
        grid=(pairs,),
        out_shape=jax.ShapeDtypeStruct((rows, width // 3), BF),
        in_specs=[
            pl.BlockSpec(memory_space=pltpu.SMEM),
            pl.BlockSpec((rows, 128), lambda i: (0, i)),
            pl.BlockSpec((rows, 128), lambda i: (0, pairs + i)),
            pl.BlockSpec((rows, 128), lambda i: (0, 2 * pairs + i)),
        ],
        out_specs=pl.BlockSpec((rows, 128), lambda i: (0, i)),
        compiler_params=pltpu.CompilerParams(vmem_limit_bytes=32 * 2**20),
        cost_estimate=pl.CostEstimate(
            flops=4 * rows * rows * width // 3,
            bytes_accessed=rows * width * 3,
            transcendentals=rows * rows * pairs * 2,
        ),
    )(z, qkv, qkv, qkv)


def attn_bwd_kernel(z_ref, q_ref, k_ref, v_ref, g_ref, d_ref, dk_ref, dv_ref, *, scale, pairs):
    z = z_ref[0]
    at = pl.program_id(0)
    size = q_ref.shape[0] // 4
    starts = [pl.multiple_of((z ^ h) * size, size) for h in range(4)]
    keys = jnp.concatenate([k_ref[pl.ds(s, size), :] for s in starts], 0)
    values = jnp.concatenate([v_ref[pl.ds(s, size), :] for s in starts], 0)
    first = lax.broadcasted_iota(jnp.int32, (size, 128), 1) < 64
    dk_ref[...] = jnp.zeros_like(dk_ref)
    dv_ref[...] = jnp.zeros_like(dv_ref)
    for j in range(4):
        span = (j + 1) * size
        q = q_ref[pl.ds(starts[j], size), :]
        grad = g_ref[pl.ds(starts[j], size), :]
        row = lax.broadcasted_iota(jnp.int32, (size, span), 0) + j * size
        seen = lax.broadcasted_iota(jnp.int32, (size, span), 1) <= row
        outs = []
        for head in range(2):
            lanes = first if head == 0 else ~first
            qh = jnp.where(lanes, q, jnp.zeros_like(q))
            gh = jnp.where(lanes, grad, jnp.zeros_like(grad))
            s = mm_cols(qh, keys[:span]) * scale
            s = jnp.where(seen, s, NEG)
            p = jnp.exp(s - jnp.max(s, -1, keepdims=True))
            p = p / jnp.sum(p, -1, keepdims=True)
            dp = mm_cols(gh, values[:span])
            ds = (p * (dp - jnp.sum(p * dp, -1, keepdims=True))).astype(BF)
            dv_ref[0:span, :] += mm_rows(p.astype(BF), gh)
            dk_ref[0:span, :] += mm_rows(ds, qh)
            outs.append(mm(ds, keys[:span]))
        dq = jnp.where(first, outs[0], outs[1]) * scale
        d_ref[pl.ds(starts[j], size), pl.ds(pl.multiple_of(at * 128, 128), 128)] = dq.astype(BF)
    for j in range(4):
        rows = slice(j * size, (j + 1) * size)
        d_ref[pl.ds(starts[j], size), pl.ds(pl.multiple_of((at + pairs) * 128, 128), 128)] = (
            dk_ref[rows, :] * scale
        ).astype(BF)
        d_ref[pl.ds(starts[j], size), pl.ds(pl.multiple_of((at + 2 * pairs) * 128, 128), 128)] = (
            dv_ref[rows, :].astype(BF)
        )


def attn_bwd(z, qkv, grad, scale):
    rows, width = qkv.shape
    pairs = width // 3 // 128
    return pl.pallas_call(
        functools.partial(attn_bwd_kernel, scale=scale, pairs=pairs),
        grid=(pairs,),
        out_shape=jax.ShapeDtypeStruct((rows, width), BF),
        in_specs=[
            pl.BlockSpec(memory_space=pltpu.SMEM),
            pl.BlockSpec((rows, 128), lambda i: (0, i)),
            pl.BlockSpec((rows, 128), lambda i: (0, pairs + i)),
            pl.BlockSpec((rows, 128), lambda i: (0, 2 * pairs + i)),
            pl.BlockSpec((rows, 128), lambda i: (0, i)),
        ],
        out_specs=pl.BlockSpec((rows, width), lambda i: (0, 0)),
        scratch_shapes=[pltpu.VMEM((rows, 128), F32), pltpu.VMEM((rows, 128), F32)],
        compiler_params=pltpu.CompilerParams(vmem_limit_bytes=32 * 2**20),
        cost_estimate=pl.CostEstimate(
            flops=10 * rows * rows * width // 3,
            bytes_accessed=rows * width * 5,
            transcendentals=rows * rows * pairs * 2,
        ),
    )(z, qkv, qkv, qkv, grad)


def cross_probs(q, keys, lanes, seen, scale):
    qh = jnp.where(lanes, q, jnp.zeros_like(q))
    s = jnp.where(seen, mm_cols(qh, keys) * scale, NEG)
    p = jnp.where(seen, jnp.exp(s - jnp.max(s, -1, keepdims=True)), 0.0)
    return qh, p / jnp.sum(p, -1, keepdims=True)


def cross_fwd_kernel(cap_ref, seg_ref, q_ref, k_ref, v_ref, o_ref, *, scale):
    seen = seg_ref[...] == cap_ref[0]
    q, keys, values = q_ref[...], k_ref[...], v_ref[...]
    first = lax.broadcasted_iota(jnp.int32, q.shape, 1) < 64
    outs = []
    for head in range(2):
        _, p = cross_probs(q, keys, first if head == 0 else ~first, seen, scale)
        outs.append(mm(p.astype(BF), values))
    o_ref[...] = jnp.where(first, outs[0], outs[1]).astype(BF)


def cross_fwd(cap, seg, cq, ckv, scale):
    rows, width = cq.shape
    text = ckv.shape[0]
    pairs = width // 128
    return pl.pallas_call(
        functools.partial(cross_fwd_kernel, scale=scale),
        grid=(pairs,),
        out_shape=jax.ShapeDtypeStruct((rows, width), BF),
        in_specs=[
            pl.BlockSpec(memory_space=pltpu.SMEM),
            pl.BlockSpec((1, text), lambda i: (0, 0)),
            pl.BlockSpec((rows, 128), lambda i: (0, i)),
            pl.BlockSpec((text, 128), lambda i: (0, i)),
            pl.BlockSpec((text, 128), lambda i: (0, pairs + i)),
        ],
        out_specs=pl.BlockSpec((rows, 128), lambda i: (0, i)),
        compiler_params=pltpu.CompilerParams(vmem_limit_bytes=32 * 2**20),
        cost_estimate=pl.CostEstimate(
            flops=4 * rows * text * width,
            bytes_accessed=rows * width * 4,
            transcendentals=rows * text * pairs * 2,
        ),
    )(cap, seg, cq, ckv, ckv)


def cross_bwd_kernel(cap_ref, seg_ref, q_ref, k_ref, v_ref, g_ref, dq_ref, dk_ref, dv_ref, *, scale):
    seen = seg_ref[...] == cap_ref[0]
    q, keys, values, grad = q_ref[...], k_ref[...], v_ref[...], g_ref[...]
    first = lax.broadcasted_iota(jnp.int32, q.shape, 1) < 64
    outs = []
    for head in range(2):
        lanes = first if head == 0 else ~first
        qh, p = cross_probs(q, keys, lanes, seen, scale)
        gh = jnp.where(lanes, grad, jnp.zeros_like(grad))
        dp = mm_cols(gh, values)
        ds = (p * (dp - jnp.sum(p * dp, -1, keepdims=True))).astype(BF)
        dv = mm_rows(p.astype(BF), gh)
        dk = mm_rows(ds, qh) * scale
        if head == 0:
            dv_ref[...] = dv
            dk_ref[...] = dk
        else:
            dv_ref[...] += dv
            dk_ref[...] += dk
        outs.append(mm(ds, keys))
    dq_ref[...] = (jnp.where(first, outs[0], outs[1]) * scale).astype(BF)


def cross_bwd(cap, seg, cq, ckv, grad, scale):
    rows, width = cq.shape
    text = ckv.shape[0]
    pairs = width // 128
    return pl.pallas_call(
        functools.partial(cross_bwd_kernel, scale=scale),
        grid=(pairs,),
        out_shape=[
            jax.ShapeDtypeStruct((rows, width), BF),
            jax.ShapeDtypeStruct((text, width), F32),
            jax.ShapeDtypeStruct((text, width), F32),
        ],
        in_specs=[
            pl.BlockSpec(memory_space=pltpu.SMEM),
            pl.BlockSpec((1, text), lambda i: (0, 0)),
            pl.BlockSpec((rows, 128), lambda i: (0, i)),
            pl.BlockSpec((text, 128), lambda i: (0, i)),
            pl.BlockSpec((text, 128), lambda i: (0, pairs + i)),
            pl.BlockSpec((rows, 128), lambda i: (0, i)),
        ],
        out_specs=[
            pl.BlockSpec((rows, 128), lambda i: (0, i)),
            pl.BlockSpec((text, 128), lambda i: (0, i)),
            pl.BlockSpec((text, 128), lambda i: (0, i)),
        ],
        compiler_params=pltpu.CompilerParams(vmem_limit_bytes=32 * 2**20),
        cost_estimate=pl.CostEstimate(
            flops=10 * rows * text * width,
            bytes_accessed=rows * width * 6,
            transcendentals=rows * text * pairs * 2,
        ),
    )(cap, seg, cq, ckv, ckv, grad)


def long_masks(g, rows):
    slot = jnp.arange(rows, dtype=jnp.int32) // (2 * STRIPE)
    rest = jnp.arange(rows, dtype=jnp.int32) % (2 * STRIPE)

    def positions(r):
        return ((g.z ^ slot) * g.t + r) * (2 * STRIPE) + rest

    key_pos = jnp.concatenate([positions((g.r - q) % g.t) for q in range(g.t)])
    return key_pos[None, :] <= positions(g.r)[:, None]


def long_gather(g, value):
    return jnp.concatenate([value] + [g.over_r(value, q) for q in range(1, g.t)], 0)


def long_fwd(g, qkv, scale):
    rows, width = qkv.shape
    head = 64
    heads = width // 3 // head
    keyval = long_gather(g, qkv[:, width // 3 :])
    q = qkv[:, : width // 3].reshape(rows, heads, head)
    k = keyval[:, : width // 3].reshape(-1, heads, head)
    v = keyval[:, width // 3 :].reshape(-1, heads, head)
    seen = long_masks(g, rows)[None]
    s = jnp.einsum("qhd,khd->hqk", q, k, preferred_element_type=F32) * scale
    s = jnp.where(seen, s, NEG)
    p = jnp.exp(s - jnp.max(s, -1, keepdims=True))
    p = p / jnp.sum(p, -1, keepdims=True)
    out = jnp.einsum("hqk,khd->qhd", p.astype(BF), v, preferred_element_type=F32)
    return out.reshape(rows, width // 3).astype(BF), (q, k, v, p)


def long_bwd(g, saved, grad, scale):
    q, k, v, p = saved
    rows, heads, head = q.shape
    width = heads * head
    grad = grad.reshape(rows, heads, head)
    dv = jnp.einsum("hqk,qhd->khd", p.astype(BF), grad, preferred_element_type=F32)
    dp = jnp.einsum("qhd,khd->hqk", grad, v, preferred_element_type=F32)
    ds = (p * (dp - jnp.sum(p * dp, -1, keepdims=True))).astype(BF)
    dq = jnp.einsum("hqk,khd->qhd", ds, k, preferred_element_type=F32) * scale
    dk = jnp.einsum("hqk,qhd->khd", ds, q, preferred_element_type=F32) * scale
    both = jnp.concatenate([dk.reshape(-1, width), dv.reshape(-1, width)], 1)
    both = both.reshape(g.t, rows, 2 * width)
    total = both[0]
    for step in range(1, g.t):
        total = total + g.over_r(both[step], -step)
    return jnp.concatenate([dq.reshape(rows, width).astype(BF), total.astype(BF)], 1)


def normed(values):
    center = values - jnp.mean(values, -1, keepdims=True)
    spread = lax.rsqrt(jnp.mean(center * center, -1, keepdims=True) + EPS)
    return center * spread, spread


def norm_back(unit, spread, gain, grad):
    f = grad * gain
    added = spread * (
        f - jnp.mean(f, -1, keepdims=True) - unit * jnp.mean(f * unit, -1, keepdims=True)
    )
    return added, jnp.sum(grad * unit, 0), jnp.sum(grad, 0)


def column_halves(weight, groups, mine):
    rows, width = weight.shape
    parts = weight.reshape(rows, groups, 2, width // groups // 2)
    return (
        pick(parts, 2, mine).reshape(rows, width // 2),
        pick(parts, 2, 1 - mine).reshape(rows, width // 2),
    )


def two(g, mine, other, axis):
    first = jnp.where(g.c == 0, mine, other)
    second = jnp.where(g.c == 0, other, mine)
    return jnp.stack([first, second], axis)


def gather_fast(g, scal, weights, ids, tokens, cotangent):
    gains, shifts, w_qkv, w_out, w_cq, w_ckv, w_co, w_up, w_down = weights
    share, depth = w_co.shape
    tall = w_down.shape[0]
    small = jnp.concatenate([gains, shifts], 0).T
    small = jnp.pad(small, ((0, 0), (0, 128 - small.shape[1])))
    keep1, send1 = prep_weights(scal, [(w_qkv, 6), (small, 0), (w_cq, 2)])
    keep2, send2 = prep_weights(scal, [(w_ckv, 4)], w_out)
    keep3, send3 = prep_weights(scal, [(w_up, 2)])
    blocks = prep_tokens(scal, ids, tokens, cotangent)
    got1 = g.over_c(send1)
    got2 = g.over_c(jnp.concatenate([send2, send3], 1))

    def shape(kinds, rows, width):
        return (2, kinds, 4, 2, rows, width)

    n_qkv, n_cq, n_ckv, n_up = (w.shape[1] // 2 for w in (w_qkv, w_cq, w_ckv, w_up))
    groups = tall // share // 2
    low, high = (
        list(half.reshape(groups, share, depth))
        for half in (w_down[: tall // 2], w_down[tall // 2 :])
    )
    second = jnp.stack([keep2, jnp.concatenate([got2[:, :n_ckv], w_co], 1)])
    third = jnp.stack(
        [jnp.concatenate([keep3] + low, 1), jnp.concatenate([got2[:, n_ckv:]] + high, 1)]
    )
    first = after(jnp.stack([keep1, got1]), second, third)
    third_low, third_high = third[:1], third[1:]
    tok, cot = list(blocks[:4]), list(blocks[4:])

    near, far = g.gather_near, g.gather_far

    got_a = [first] + [g.xor_z(first, k) for k in (1, 2, 3)]
    tok[0], cot[0] = g.regroup(tok[0], 0), g.regroup(cot[0], 0)
    line_a = gather_line(scal, got_a)

    line_a, second, late = after((line_a, second, tok[3]), got_a, tok[0], cot[0])
    near_a = near(line_a)
    got_b = [second] + [g.xor_z(second, k) for k in (1, 2)]
    tok[3] = g.regroup(late, 3)

    near_a, second, third, third_low = after((near_a, second, third, third_low), got_b, tok[3])
    far_a = far(line_a, near_a)
    got_b.append(g.xor_z(second, 3))
    got_c1 = g.xor_z(third, 1)
    got_c2 = g.xor_z(third_low, 2)
    line_b = gather_line(scal, got_b)

    line_b, third_high, *late = after((line_b, third_high, *tok[1:3]), far_a, got_c1, got_c2)
    near_b = near(line_b)
    got_c2 = jnp.concatenate([got_c2, g.xor_z(third_high, 2)], 0)
    tok[1:3] = [g.regroup(late[k - 1], k) for k in (1, 2)]

    near_b, third, tok = after((near_b, third, tok), got_c2)
    far_b = far(line_b, near_b)
    got_c = [third, got_c1, got_c2, g.xor_z(third, 3)]
    resid = join_tokens(scal, tok, g.over_c(jnp.stack(tok)))
    line_c = gather_line(scal, got_c)

    line_c, *late = after((line_c, *cot[1:]), far_b)
    near_c = near(line_c)
    cot[1:] = [g.regroup(late[k - 1], k) for k in (1, 2, 3)]

    near_c, cot = after((near_c, cot))
    far_c = far(line_c, near_c)
    cot = join_tokens(scal, cot, g.over_c(jnp.stack(cot)))

    qkv, small, cq = gather_place(
        scal,
        *far_a,
        [shape(2, share, n_qkv), shape(2, share, 128), shape(2, share, n_cq)],
        [[(n_qkv, 0, None, 0), (128, 1, None, 0), (n_cq, 2, None, 0)]] * 2,
    )
    ckv, out, co = gather_place(
        scal,
        *far_b,
        [shape(2, share, n_ckv), shape(1, share, depth), shape(1, share, depth)],
        [[(n_ckv, 0, None, 0), (depth, 1 + half, 0, 0)] for half in range(2)],
    )

    def flat(array):
        return array.reshape(-1, array.shape[-1])

    def last(far_c):
        up, down = gather_place(
            scal,
            *far_c,
            [shape(2, share, n_up), shape(1, tall, depth)],
            [
                [(n_up, 0, None, 0)]
                + [(depth, 1, 0, (half * groups + i) * share) for i in range(groups)]
                for half in range(2)
            ],
        )
        return flat(up), flat(down)

    return (
        (resid, cot, far_c),
        last,
        flat(small)[:, :6].astype(F32).T,
    ) + tuple(flat(array) for array in (qkv, out, cq, ckv, co))


def gather_plain(g, weights):
    gains, shifts, w_qkv, w_out, w_cq, w_ckv, w_co, w_up, w_down = weights
    small = lax.all_gather(jnp.concatenate([gains, shifts], 0), AXES, axis=1, tiled=True)

    def columns(weight, groups):
        whole = lax.all_gather(weight, AXES, axis=0, tiled=True)
        return column_halves(whole, groups, g.c)[0]

    def rows(weight):
        whole = lax.all_gather(weight, AXES, axis=0, tiled=True)
        parts = whole.reshape(2, 2, whole.shape[0] // 4, whole.shape[1])
        return pick(parts, 1, g.c).reshape(whole.shape[0] // 2, whole.shape[1])

    return (
        small.astype(F32),
        columns(w_qkv, 6),
        rows(w_out),
        columns(w_cq, 2),
        columns(w_ckv, 4),
        rows(w_co),
        columns(w_up, 2),
        rows(w_down),
    )


def join_columns(g, keep, got, groups):
    rows, width = keep.shape
    block = width // groups
    parts = two(g, keep.reshape(rows, groups, block), got.reshape(rows, groups, block), 2)
    return parts.reshape(rows, 2 * width)


def scatter_columns_plain(g, grad, groups):
    rows, width = grad.shape
    whole = join_columns(g, grad, jnp.zeros_like(grad), groups)
    return lax.psum_scatter(whole, AXES, scatter_dimension=0, tiled=True)


def scatter_rows_plain(g, grad):
    rows, width = grad.shape
    parts = grad.reshape(2, rows // 2, width)
    whole = two(g, parts, jnp.zeros_like(parts), 1).reshape(2 * rows, width)
    return lax.psum_scatter(whole, AXES, scatter_dimension=0, tiled=True)


def both_cores(g, part):
    low = part.astype(BF)
    return low.astype(F32) + g.over_c(low).astype(F32)


def local(
    tokens,
    text_states,
    image_ids,
    text_segments,
    image_caption,
    norm_gains,
    norm_shifts,
    self_qkv,
    self_out,
    cross_query,
    cross_keyval,
    cross_out,
    mlp_up,
    mlp_down,
    cotangent,
    *,
    dp,
    seq,
):
    g = Grid(dp, seq)
    fast = g.t == 1
    depth = tokens.shape[-1]
    scale = (depth // H) ** (-0.5)
    weights = (
        norm_gains,
        norm_shifts,
        self_qkv,
        self_out,
        cross_query,
        cross_keyval,
        cross_out,
        mlp_up,
        mlp_down,
    )

    scal = jnp.stack([g.x, g.c, g.z, g.y]).astype(jnp.int32)
    start = image_ids[:, 0] & 1
    if fast:
        ((resid, cot, far_c), place_last, small, w_qkv, w_out, w_cq, w_ckv, w_co) = gather_fast(
            g, scal, weights, image_ids, tokens, cotangent
        )
    else:
        (small, w_qkv, w_out, w_cq, w_ckv, w_co, w_up, w_down) = gather_plain(g, weights)
        both = jnp.stack([tokens, cotangent], 2).reshape(4, STRIPE, 2 * depth)
        received = []
        for step in range(4):
            j = g.z ^ step
            half = (j & 1) ^ start[j >> 1]
            received.append(g.regroup(pick(both, 0, (j >> 1) * 2 + half), step))
        mine = jnp.stack(received)
        held = two(g, mine, g.over_c(mine), 1).reshape(8 * STRIPE, 2, depth)
        resid, cot = held[:, 0], held[:, 1]
    resid = resid.astype(F32)
    gain, shift = small[:3], small[3:]

    image = (g.x * 2 + g.y) * 2 + (g.z & 1)
    cap = image_caption[g.z >> 1, image].reshape(1)
    seg = text_segments.reshape(1, -1)
    slot = g.z.reshape(1).astype(jnp.int32)

    unit_one, spread_one = normed(resid)
    n_one = (unit_one * gain[0] + shift[0]).astype(BF)
    qkv = mm(n_one, w_qkv).astype(BF)
    if fast:
        attended = attn_fwd(slot, qkv, scale)
    else:
        attended, saved = long_fwd(g, qkv, scale)
    hidden_one = resid + both_cores(g, mm(attended, w_out))
    unit_two, spread_two = normed(hidden_one)
    n_two = (unit_two * gain[1] + shift[1]).astype(BF)
    cq = mm(n_two, w_cq).astype(BF)
    ckv = mm(text_states, w_ckv).astype(BF)
    crossed = cross_fwd(cap, seg, cq, ckv, scale)
    hidden_two = hidden_one + both_cores(g, mm(crossed, w_co))
    unit_three, spread_three = normed(hidden_two)
    n_three = (unit_three * gain[2] + shift[2]).astype(BF)
    if fast:
        w_up, w_down = place_last(far_c)
    up = mm(n_three, w_up)
    inner = jnp.tanh(GELU_C * (up + 0.044715 * up * up * up))
    act = (0.5 * up * (1.0 + inner)).astype(BF)

    def halves(value):
        parts = value.reshape(4, 2, STRIPE, value.shape[-1])
        return pick(parts, 1, g.c), pick(parts, 1, 1 - g.c)

    down = mm(act, w_down)
    keep, gone = halves(down)

    def finish(gone):
        return (halves(hidden_two)[0] + keep + g.over_c(gone).astype(F32)).astype(BF)

    grad_down = mm_rows(act, cot)
    slope = 0.5 * (1.0 + inner) + 0.5 * up * (1.0 - inner * inner) * GELU_C * (
        1.0 + 3 * 0.044715 * up * up
    )
    d_up = (mm_cols(cot, w_down) * slope).astype(BF)
    grad_up = mm_rows(n_three, d_up)
    share = depth // g.count
    if fast:
        mlp = by_rows(grad_down.astype(BF), share) + by_columns(grad_up.astype(BF), share)
        mlp_far, gone = after((fold_far(scal, share, mlp), gone.astype(BF)))
        mlp_far = g.over_y(mlp_far[0]), g.over_x(mlp_far[1])
        out = finish(gone)
        out_home = [g.regroup(out[k], k) for k in range(4)]
    else:
        out = finish(gone.astype(BF))
    added, gain_three, shift_three = norm_back(
        unit_three, spread_three, gain[2], both_cores(g, mm_cols(d_up, w_up))
    )
    g_two = cot.astype(F32) + added
    d_cross = g_two.astype(BF)
    grad_co = mm_rows(crossed, d_cross)
    d_crossed = mm_cols(d_cross, w_co).astype(BF)
    d_cq, d_ck, d_cv = cross_bwd(cap, seg, cq, ckv, d_crossed, scale)
    grad_cq = mm_rows(n_two, d_cq)
    if fast:
        cross = by_rows(grad_co.astype(BF), share) + by_columns(grad_cq.astype(BF), share)
        d_ckv = jnp.concatenate([d_ck, d_cv], 1).astype(BF)
    added, gain_two, shift_two = norm_back(
        unit_two, spread_two, gain[1], both_cores(g, mm_cols(d_cq, w_cq))
    )
    g_one = g_two + added
    d_self = g_one.astype(BF)
    grad_out = mm_rows(attended, d_self)
    d_att = mm_cols(d_self, w_out).astype(BF)
    if fast:
        near_ready, swapped = after(
            (fold_near(scal, share, [(mlp, mlp_far)]), d_ckv), mlp_far, out_home
        )
        mlp_near = g.over_x(near_ready[0]), g.over_y(near_ready[1])
        swapped = g.xor_z(swapped, 1)
        d_qkv = attn_bwd(slot, qkv, after(d_att, near_ready), scale)
        d_ckv = plus(d_ckv, swapped)
        cross_far, d_ckv = after((fold_far(scal, share, cross), d_ckv), mlp_near, swapped)
        mlp_line = fold_line(scal, share, [(mlp, mlp_far, mlp_near)])
        cross_far = g.over_y(cross_far[0]), g.over_x(cross_far[1])
        swapped = g.xor_z(d_ckv, 2)
    else:
        d_qkv = long_bwd(g, saved, d_att, scale)
    grad_qkv = mm_rows(n_one, d_qkv)
    added, gain_one, shift_one = norm_back(
        unit_one, spread_one, gain[0], both_cores(g, mm_cols(d_qkv, w_qkv))
    )
    grad_in = (g_one + added).astype(BF)

    norms = jnp.stack([gain_one, gain_two, gain_three, shift_one, shift_two, shift_three])
    back = halves(grad_in)[0]
    if fast:
        last = by_rows(grad_out.astype(BF), share) + by_columns(grad_qkv.astype(BF), share)
        d_ckv = plus(d_ckv, swapped)
        last_far, mlp_line = after(
            (fold_far(scal, share, last), mlp_line), cross_far, swapped
        )
        last_far = g.over_y(last_far[0]), g.over_x(last_far[1])
        mlp_terms = [mlp_line[0]] + [g.xor_z(mlp_line[k], k) for k in (1, 2)]

        near_last = fold_near(scal, share, [(last, last_far)])
        near_cross = fold_near(scal, share, [(cross, cross_far)])
        near_last, near_cross, mlp_line, d_ckv, norms = after(
            (near_last, near_cross, mlp_line, d_ckv, norms), last_far, mlp_terms[1:]
        )
        near_last = g.over_x(near_last[0]), g.over_y(near_last[1])
        near_cross = g.over_x(near_cross[0]), g.over_y(near_cross[1])
        mlp_terms.append(g.xor_z(mlp_line[3], 3))
        d_ckv = plus(d_ckv, g.over_x(d_ckv))
        norms = norms + g.over_y(norms)

        line = fold_line(
            scal, share, [(last, last_far, near_last), (cross, cross_far, near_cross)]
        )
        line, back, mlp_terms, d_ckv, norms = after((line, back, mlp_terms, d_ckv, norms))
        terms = [line[0]] + [g.xor_z(line[k], k) for k in (1, 2, 3)]
        back = [g.regroup(back[k], k) for k in range(4)]
        mlp_terms = after(mlp_terms, back)
        d_ckv = plus(d_ckv, g.over_y(d_ckv))
        norms = after(norms + g.over_x(norms), terms)
        norms = norms + g.xor_z(norms, 1)
        norms = norms + g.xor_z(norms, 2)
        norms = lax.dynamic_slice_in_dim(norms, g.me * share, share, 1)
        output, grad_tokens = place_home(scal, image_ids, out_home, back)
        d_ckv_whole = join_columns(g, d_ckv, g.over_c(d_ckv), 4)
    else:
        back = jnp.concatenate([out, back], 2)
        back = jnp.stack([g.regroup(back[step], step) for step in range(4)])
        order = []
        for block in range(4):
            j = (block & 2) + ((block & 1) ^ start[block >> 1])
            order.append(pick(back, 0, j ^ g.z))
        back = jnp.stack(order).reshape(2, 2 * STRIPE, 2 * depth)
        output, grad_tokens = back[:, :, :depth], back[:, :, depth:].astype(F32)
        d_ckv = jnp.concatenate([d_ck, d_cv], 1)
        whole = join_columns(g, d_ckv, jnp.zeros_like(d_ckv), 4)
        d_ckv_whole = lax.psum(whole, AXES).astype(BF)
        d_ckv = column_halves(d_ckv_whole, 4, g.c)[0]
        norms = lax.psum(norms, AXES) * 0.5
        norms = lax.dynamic_slice_in_dim(norms, g.me * (depth // g.count), depth // g.count, 1)
    part = mm_cols(d_ckv, w_ckv)
    grad_text = part + g.over_c(part)
    text_cols = lax.dynamic_slice_in_dim(text_states, g.me * share, share, 1)
    grad_ckv = mm_rows(text_cols, d_ckv_whole)
    if fast:
        tall = mlp_down.shape[0]

        def columns(terms, low, high, groups):
            got = g.over_c(plus(*[pick(term, 0, 1 - g.c)[:, low:high] for term in terms]))
            keep = sum(pick(term, 0, g.c)[:, low:high].astype(F32) for term in terms)
            return join_columns(g, keep, got.astype(F32), groups)

        n_down = tall // share // 2 * depth
        grad_down = summed(mlp_terms, ALL, ALL, slice(0, n_down))
        grad_down = grad_down.reshape(2, share, tall // share // 2, depth)
        grad_down = grad_down.transpose(0, 2, 1, 3).reshape(tall, depth)
        grad_up = columns(mlp_terms, n_down, None, 2)
        half = depth // 2
        to_qkv = half + grad_qkv.shape[1]

        def halves_of(start):
            total = summed(terms, ALL, ALL, slice(start, start + half))
            return jnp.concatenate([total[0], total[1]], 1)

        grad_out = halves_of(0)
        grad_qkv = columns(terms, half, to_qkv, 6)
        grad_co = halves_of(to_qkv)
        grad_cq = columns(terms, to_qkv + half, None, 2)
    else:
        grad_down = scatter_rows_plain(g, grad_down)
        grad_up = scatter_columns_plain(g, grad_up, 2)
        grad_co = scatter_rows_plain(g, grad_co)
        grad_cq = scatter_columns_plain(g, grad_cq, 2)
        grad_out = scatter_rows_plain(g, grad_out)
        grad_qkv = scatter_columns_plain(g, grad_qkv, 6)
    return (
        output,
        grad_tokens,
        grad_text,
        norms[:3],
        norms[3:5],
        grad_qkv,
        grad_out,
        grad_cq,
        grad_ckv,
        grad_co,
        grad_up,
        grad_down,
        norms[5],
    )


def solution(mesh):
    both = ("dp", "seq")
    rows = P(both, None)
    in_specs = (
        P(None, both, None),
        P(),
        P(None, both),
        P(),
        P(),
        P(None, both),
        P(None, both),
        rows,
        rows,
        rows,
        rows,
        rows,
        rows,
        rows,
        P(None, both, None),
    )
    out_specs = (
        P(None, both, None),
        P(None, both, None),
        P(),
        P(None, both),
        P(None, both),
        rows,
        rows,
        rows,
        rows,
        rows,
        rows,
        rows,
        P(both),
    )
    body = functools.partial(local, dp=mesh.shape["dp"], seq=mesh.shape["seq"])
    return jax.shard_map(body, mesh=mesh, in_specs=in_specs, out_specs=out_specs, check_vma=False)
```

```python
import functools

import jax
import jax.numpy as jnp
from jax import lax
from jax.experimental import pallas as pl
from jax.experimental.pallas import tpu as pltpu
from jax.sharding import PartitionSpec as P

H = 16
STRIPE = 64
EPS = 1e-05
NEG = -1e30
GELU_C = 0.7978845608028654
BF = jnp.bfloat16
F32 = jnp.float32
AXES = ("dp", "seq")


def mm(left, right):
    return jnp.dot(left, right, preferred_element_type=F32)


def mm_rows(left, right):
    return lax.dot_general(left, right, (((0,), (0,)), ((), ())), preferred_element_type=F32)


def mm_cols(left, right):
    return lax.dot_general(left, right, (((1,), (1,)), ((), ())), preferred_element_type=F32)


def pick(array, dim, index):
    return lax.dynamic_index_in_dim(array, index, dim, keepdims=False)


class Grid:
    def __init__(self, dp, seq):
        self.dp, self.seq, self.t = dp, seq, seq // 8
        self.count = dp * seq
        me = lax.axis_index(AXES)
        part = lax.rem(me, seq)
        self.me = me
        self.x = me // (2 * seq)
        self.c = lax.rem(me // seq, 2)
        self.z = part // (2 * self.t)
        self.r = lax.rem(part // 2, self.t)
        self.y = lax.rem(part, 2)

    def coords(self, d):
        part = d % self.seq
        return (
            d // (2 * self.seq),
            d // self.seq % 2,
            part // (2 * self.t),
            part // 2 % self.t,
            part % 2,
        )

    def index(self, x, c, z, r, y):
        return (x * 2 + c) * self.seq + (z * self.t + r) * 2 + y

    def send(self, value, move):
        perm = [(d, self.index(*move(*self.coords(d)))) for d in range(self.count)]
        return lax.ppermute(value, AXES, perm)

    def over_c(self, value):
        return self.send(value, lambda x, c, z, r, y: (x, 1 - c, z, r, y))

    def over_x(self, value):
        return self.send(value, lambda x, c, z, r, y: (1 - x, c, z, r, y))

    def over_y(self, value):
        return self.send(value, lambda x, c, z, r, y: (x, c, z, r, 1 - y))

    def xor_z(self, value, bits):
        return self.send(value, lambda x, c, z, r, y: (x, c, z ^ bits, r, y))

    def over_r(self, value, step):
        return self.send(value, lambda x, c, z, r, y: (x, c, z, (r + step) % self.t, y))

    def regroup(self, value, bits):
        return self.send(value, lambda x, c, z, r, y: (x, y, z ^ bits, r, c))

    def gather_near(self, lines):
        return self.over_x(lines[0]), self.over_y(lines[1])

    def gather_far(self, lines, got):
        pair_a, pair_b = jnp.stack([lines[0], got[0]]), jnp.stack([lines[1], got[1]])
        return pair_a, self.over_y(pair_a), pair_b, self.over_x(pair_b)

    def swap(self, value):
        return self.send(value, lambda x, c, z, r, y: (x, y, z, r, c))


def after(value, *others):
    return lax.optimization_barrier((value, others))[0]


def place(scalars, sources, shapes, copies):
    def kernel(s_ref, *refs):
        ins = refs[: len(sources)]
        outs = refs[len(sources) : len(sources) + len(shapes)]
        sems = refs[-1]
        started = []
        for i, (source, at, target, to) in enumerate(copies):
            copy = pltpu.make_async_copy(
                ins[source].at[at(s_ref)], outs[target].at[to(s_ref)], sems.at[i]
            )
            copy.start()
            started.append(copy)
        for copy in started:
            copy.wait()

    moved = sum(source.size * 2 for source in sources)
    return pl.pallas_call(
        kernel,
        out_shape=[jax.ShapeDtypeStruct(shape, BF) for shape in shapes],
        in_specs=[pl.BlockSpec(memory_space=pltpu.SMEM)]
        + [pl.BlockSpec(memory_space=pl.ANY)] * len(sources),
        out_specs=[pl.BlockSpec(memory_space=pltpu.VMEM)] * len(shapes),
        scratch_shapes=[pltpu.SemaphoreType.DMA((len(copies),))],
        compiler_params=pltpu.CompilerParams(vmem_limit_bytes=32 * 2**20),
        cost_estimate=pl.CostEstimate(flops=0, bytes_accessed=2 * moved, transcendentals=0),
    )(scalars, *sources)


ALL = slice(None)


def gather_line(scal, got):
    _, rows, width = got[0].shape
    return place(
        scal,
        got,
        [(4, rows, width)] * 2,
        [
            (k, lambda s, h=h: (h,), h, lambda s, k=k: (s[2] ^ k,))
            for k in range(4)
            for h in range(2)
        ],
    )


def gather_place(scal, pair_a, far_a, pair_b, far_b, shapes, targets):
    rows = pair_a.shape[2]
    copies = []
    for i, half in enumerate((0, 0, 1, 1)):
        far = i % 2
        for near in range(2):
            dx, dy = (near, far) if half == 0 else (far, near)
            start = 0
            for wide, out, kind, row in targets[half]:
                copies.append(
                    (
                        i,
                        lambda s, near=near, start=start, wide=wide: (
                            near,
                            ALL,
                            ALL,
                            pl.ds(start, wide),
                        ),
                        out,
                        lambda s, dx=dx, dy=dy, kind=kind, row=row, half=half: (
                            s[0] ^ dx,
                            s[1] ^ half if kind is None else kind,
                            ALL,
                            s[3] ^ dy,
                            pl.ds(row, rows),
                        ),
                    )
                )
                start += wide
    return place(scal, [pair_a, far_a, pair_b, far_b], shapes, copies)


def plus(*terms):
    total = terms[0].astype(F32)
    for term in terms[1:]:
        total = total + term.astype(F32)
    return total.astype(BF)


def by_columns(array, share):
    view = array.reshape(2, 2, 4, 2, share, array.shape[1])
    block = (None, None, None, None, share, array.shape[1])
    return [(view, block, lambda x, z, y, h, i: (x, h, z, y, 0, 0))]


def by_rows(array, share):
    groups, width = array.shape[0] // (16 * share), array.shape[1]
    if groups == 1:
        view = array.reshape(2, 4, 2, share, width)
        block = (None, None, None, share, width // 2)
        return [(view, block, lambda x, z, y, h, i: (x, z, y, 0, h))]
    view = array.reshape(2, 4, 2, groups, share, width)
    block = (None, None, None, None, share, width)
    return [
        (view, block, lambda x, z, y, h, i, j=j: (x, z, y, h * (groups // 2) + j, 0, 0))
        for j in range(groups // 2)
    ]


def by_steps(array):
    return [(array, (None, None) + array.shape[2:], lambda x, z, y, h, i: (i, h, 0, 0))]


def fold(scal, groups, steps, share, places, outs):
    arrays, specs, parts, width = [], [], [], 0
    for slots, received in groups:
        wide = sum(block[-1] for _, block, _ in slots)
        for h in range(2):
            extras, at = [], 0
            for array, at_step in received[h]:
                extras.append(len(arrays))
                arrays.append(array)
                specs.append(
                    pl.BlockSpec(
                        (None, share, wide),
                        lambda i, s, f=at_step: (f(i, s), 0, 0),
                    )
                )
            for view, block, index in slots:
                parts.append((h, len(arrays), extras, at, width + at, block[-1]))
                arrays.append(view)
                specs.append(
                    pl.BlockSpec(block, lambda i, s, h=h, f=index: f(*places[h](i, s), h, i))
                )
                at += block[-1]
        width += wide

    def kernel(s_ref, *refs):
        step = pl.program_id(0)
        ins, targets = refs[: len(arrays)], refs[len(arrays) :]
        for h, own, extras, at, to, wide in parts:
            value = ins[own][...]
            if extras:
                value = value.astype(F32)
                for extra in extras:
                    value = value + ins[extra][:, pl.ds(at, wide)].astype(F32)
                value = value.astype(BF)
            if outs is None:
                targets[h][:, pl.ds(to, wide)] = value
            else:
                for j in range(steps):

                    @pl.when(step == j)
                    def _():
                        targets[j][h, :, pl.ds(to, wide)] = value

    if outs is None:
        out_shape = [jax.ShapeDtypeStruct((steps, share, width), BF)] * 2
        out_specs = [pl.BlockSpec((None, share, width), lambda i, s: (i, 0, 0))] * 2
    else:
        out_shape = [jax.ShapeDtypeStruct((2, share, width), BF)] * steps
        out_specs = [pl.BlockSpec((2, share, width), lambda i, s: (0, 0, 0))] * steps
    return pl.pallas_call(
        kernel,
        grid_spec=pltpu.PrefetchScalarGridSpec(
            num_scalar_prefetch=1, grid=(steps,), in_specs=specs, out_specs=out_specs
        ),
        out_shape=out_shape,
        compiler_params=pltpu.CompilerParams(vmem_limit_bytes=32 * 2**20),
        cost_estimate=pl.CostEstimate(
            flops=0, bytes_accessed=2 * steps * share * width * 6, transcendentals=0
        ),
    )(scal, *arrays)


def fold_far(scal, share, slots):
    return fold(
        scal,
        [(slots, [[], []])],
        8,
        share,
        [
            lambda i, s: (i // 4, lax.rem(i, 4), 1 - s[3]),
            lambda i, s: (1 - s[0], i // 2, lax.rem(i, 2)),
        ],
        None,
    )


def fold_near(scal, share, chunks):
    return fold(
        scal,
        [
            (
                slots,
                [
                    [(far[0], lambda i, s: (1 - s[0]) * 4 + i)],
                    [(far[1], lambda i, s: i * 2 + 1 - s[3])],
                ],
            )
            for slots, far in chunks
        ],
        4,
        share,
        [lambda i, s: (1 - s[0], i, s[3]), lambda i, s: (s[0], i, 1 - s[3])],
        None,
    )


def fold_line(scal, share, chunks, more=()):
    groups = []
    for slots, far, near in chunks:
        groups.append(
            (
                slots,
                [
                    [
                        (far[0], lambda i, s: s[0] * 4 + (s[2] ^ i)),
                        (near[0], lambda i, s: s[2] ^ i),
                    ],
                    [
                        (far[1], lambda i, s: (s[2] ^ i) * 2 + s[3]),
                        (near[1], lambda i, s: s[2] ^ i),
                    ],
                ],
            )
        )
    if more:
        groups.append((list(more), [[], []]))
    return fold(
        scal, groups, 4, share, [lambda i, s: (s[0], s[2] ^ i, s[3])] * 2, True
    )


def summed(terms, *at):
    return sum(term[at].astype(F32) for term in terms)


def prep_weights(scal, sources, whole=None):
    share = sources[0][0].shape[0]
    more = 0 if whole is None else whole.shape[1]
    width = sum(array.shape[1] // (2 if groups else 1) for array, groups in sources)

    def kernel(s_ref, *refs):
        low = s_ref[1] == 0
        keep, send = refs[-2:]
        start = 0
        for ref, (_, groups) in zip(refs, sources):
            if groups == 0:
                keep[:, pl.ds(start, ref.shape[1])] = ref[...]
                send[:, pl.ds(start, ref.shape[1])] = ref[...]
                start += ref.shape[1]
                continue
            block = ref.shape[1] // groups // 2
            for i in range(groups):
                a = ref[:, pl.ds(2 * i * block, block)]
                b = ref[:, pl.ds((2 * i + 1) * block, block)]
                keep[:, pl.ds(start, block)] = jnp.where(low, a, b)
                send[:, pl.ds(start, block)] = jnp.where(low, b, a)
                start += block
        if whole is not None:
            keep[:, pl.ds(start, more)] = refs[len(sources)][...]

    vmem = pl.BlockSpec(memory_space=pltpu.VMEM)
    smem = pl.BlockSpec(memory_space=pltpu.SMEM)
    arrays = [array for array, _ in sources] + ([] if whole is None else [whole])
    return pl.pallas_call(
        kernel,
        in_specs=[smem] + [vmem] * len(arrays),
        out_specs=[vmem] * 2,
        out_shape=[
            jax.ShapeDtypeStruct((share, width + more), BF),
            jax.ShapeDtypeStruct((share, width), BF),
        ],
        compiler_params=pltpu.CompilerParams(vmem_limit_bytes=32 * 2**20),
    )(scal, *arrays)


def prep_tokens(scal, ids, tokens, cotangent):
    depth = tokens.shape[2]

    def kernel(s_ref, ids_ref, tok, cot, *blocks):
        for step in range(4):
            j = s_ref[2] ^ step
            b = j >> 1
            half = (j & 1) ^ (ids_ref[b, 0] & 1)
            rows = pl.ds(pl.multiple_of(half * STRIPE, STRIPE), STRIPE)
            blocks[step][...] = tok[b, rows, :]
            blocks[4 + step][...] = cot[b, rows, :]

    vmem = pl.BlockSpec(memory_space=pltpu.VMEM)
    smem = pl.BlockSpec(memory_space=pltpu.SMEM)
    return pl.pallas_call(
        kernel,
        in_specs=[smem, smem, vmem, vmem],
        out_specs=[vmem] * 8,
        out_shape=[jax.ShapeDtypeStruct((STRIPE, depth), BF)] * 8,
        compiler_params=pltpu.CompilerParams(vmem_limit_bytes=32 * 2**20),
    )(scal, ids, tokens, cotangent)


def join_tokens(scal, mine, other):
    _, rows, depth = other.shape

    def kernel(s_ref, a0, a1, a2, a3, o_ref, out):
        for step, ref in enumerate((a0, a1, a2, a3)):
            for part, core in ((ref, s_ref[1]), (o_ref.at[step], 1 - s_ref[1])):
                at = pl.ds(pl.multiple_of((2 * step + core) * rows, rows), rows)
                out[at, :] = part[...]

    vmem = pl.BlockSpec(memory_space=pltpu.VMEM)
    return pl.pallas_call(
        kernel,
        in_specs=[pl.BlockSpec(memory_space=pltpu.SMEM)] + [vmem] * 5,
        out_specs=vmem,
        out_shape=jax.ShapeDtypeStruct((8 * rows, depth), BF),
        compiler_params=pltpu.CompilerParams(vmem_limit_bytes=32 * 2**20),
    )(scal, *mine, other)


def place_home(scal, ids, outs, grads):
    rows, depth = outs[0].shape

    def kernel(s_ref, ids_ref, *refs):
        out, grad = refs[8:]
        for step in range(4):
            j = s_ref[2] ^ step
            b = j >> 1
            half = (j & 1) ^ (ids_ref[b, 0] & 1)
            at = pl.ds(pl.multiple_of(half * rows, rows), rows)
            out[b, at, :] = refs[step][...]
            grad[b, at, :] = refs[4 + step][...].astype(F32)

    vmem = pl.BlockSpec(memory_space=pltpu.VMEM)
    smem = pl.BlockSpec(memory_space=pltpu.SMEM)
    return pl.pallas_call(
        kernel,
        in_specs=[smem, smem] + [vmem] * 8,
        out_specs=[vmem] * 2,
        out_shape=[
            jax.ShapeDtypeStruct((2, 2 * rows, depth), BF),
            jax.ShapeDtypeStruct((2, 2 * rows, depth), F32),
        ],
        compiler_params=pltpu.CompilerParams(vmem_limit_bytes=32 * 2**20),
    )(scal, ids, *outs, *grads)


def attn_fwd_kernel(z_ref, q_ref, k_ref, v_ref, o_ref, *, scale):
    z = z_ref[0]
    size = q_ref.shape[0] // 4
    starts = [pl.multiple_of((z ^ h) * size, size) for h in range(4)]
    keys = jnp.concatenate([k_ref[pl.ds(s, size), :] for s in starts], 0)
    values = jnp.concatenate([v_ref[pl.ds(s, size), :] for s in starts], 0)
    first = lax.broadcasted_iota(jnp.int32, (size, 128), 1) < 64
    for j in range(4):
        span = (j + 1) * size
        q = q_ref[pl.ds(starts[j], size), :]
        row = lax.broadcasted_iota(jnp.int32, (size, span), 0) + j * size
        seen = lax.broadcasted_iota(jnp.int32, (size, span), 1) <= row
        outs = []
        for head in range(2):
            lanes = first if head == 0 else ~first
            qh = jnp.where(lanes, q, jnp.zeros_like(q))
            s = mm_cols(qh, keys[:span]) * scale
            s = jnp.where(seen, s, NEG)
            p = jnp.exp(s - jnp.max(s, -1, keepdims=True))
            total = jnp.sum(p, -1, keepdims=True)
            outs.append(mm(p.astype(BF), values[:span]) / total)
        o_ref[pl.ds(starts[j], size), :] = jnp.where(first, outs[0], outs[1]).astype(BF)


def attn_fwd(z, qkv, scale):
    rows, width = qkv.shape
    pairs = width // 3 // 128
    return pl.pallas_call(
        functools.partial(attn_fwd_kernel, scale=scale),
        grid=(pairs,),
        out_shape=jax.ShapeDtypeStruct((rows, width // 3), BF),
        in_specs=[
            pl.BlockSpec(memory_space=pltpu.SMEM),
            pl.BlockSpec((rows, 128), lambda i: (0, i)),
            pl.BlockSpec((rows, 128), lambda i: (0, pairs + i)),
            pl.BlockSpec((rows, 128), lambda i: (0, 2 * pairs + i)),
        ],
        out_specs=pl.BlockSpec((rows, 128), lambda i: (0, i)),
        compiler_params=pltpu.CompilerParams(vmem_limit_bytes=32 * 2**20),
        cost_estimate=pl.CostEstimate(
            flops=4 * rows * rows * width // 3,
            bytes_accessed=rows * width * 3,
            transcendentals=rows * rows * pairs * 2,
        ),
    )(z, qkv, qkv, qkv)


def attn_bwd_kernel(z_ref, q_ref, k_ref, v_ref, g_ref, d_ref, dk_ref, dv_ref, *, scale, pairs):
    z = z_ref[0]
    at = pl.program_id(0)
    size = q_ref.shape[0] // 4
    starts = [pl.multiple_of((z ^ h) * size, size) for h in range(4)]
    keys = jnp.concatenate([k_ref[pl.ds(s, size), :] for s in starts], 0)
    values = jnp.concatenate([v_ref[pl.ds(s, size), :] for s in starts], 0)
    first = lax.broadcasted_iota(jnp.int32, (size, 128), 1) < 64
    dk_ref[...] = jnp.zeros_like(dk_ref)
    dv_ref[...] = jnp.zeros_like(dv_ref)
    for j in range(4):
        span = (j + 1) * size
        q = q_ref[pl.ds(starts[j], size), :]
        grad = g_ref[pl.ds(starts[j], size), :]
        row = lax.broadcasted_iota(jnp.int32, (size, span), 0) + j * size
        seen = lax.broadcasted_iota(jnp.int32, (size, span), 1) <= row
        outs = []
        for head in range(2):
            lanes = first if head == 0 else ~first
            qh = jnp.where(lanes, q, jnp.zeros_like(q))
            gh = jnp.where(lanes, grad, jnp.zeros_like(grad))
            s = mm_cols(qh, keys[:span]) * scale
            s = jnp.where(seen, s, NEG)
            p = jnp.exp(s - jnp.max(s, -1, keepdims=True))
            p = p / jnp.sum(p, -1, keepdims=True)
            dp = mm_cols(gh, values[:span])
            ds = (p * (dp - jnp.sum(p * dp, -1, keepdims=True))).astype(BF)
            dv_ref[0:span, :] += mm_rows(p.astype(BF), gh)
            dk_ref[0:span, :] += mm_rows(ds, qh)
            outs.append(mm(ds, keys[:span]))
        dq = jnp.where(first, outs[0], outs[1]) * scale
        d_ref[pl.ds(starts[j], size), pl.ds(pl.multiple_of(at * 128, 128), 128)] = dq.astype(BF)
    for j in range(4):
        rows = slice(j * size, (j + 1) * size)
        d_ref[pl.ds(starts[j], size), pl.ds(pl.multiple_of((at + pairs) * 128, 128), 128)] = (
            dk_ref[rows, :] * scale
        ).astype(BF)
        d_ref[pl.ds(starts[j], size), pl.ds(pl.multiple_of((at + 2 * pairs) * 128, 128), 128)] = (
            dv_ref[rows, :].astype(BF)
        )


def attn_bwd(z, qkv, grad, scale):
    rows, width = qkv.shape
    pairs = width // 3 // 128
    return pl.pallas_call(
        functools.partial(attn_bwd_kernel, scale=scale, pairs=pairs),
        grid=(pairs,),
        out_shape=jax.ShapeDtypeStruct((rows, width), BF),
        in_specs=[
            pl.BlockSpec(memory_space=pltpu.SMEM),
            pl.BlockSpec((rows, 128), lambda i: (0, i)),
            pl.BlockSpec((rows, 128), lambda i: (0, pairs + i)),
            pl.BlockSpec((rows, 128), lambda i: (0, 2 * pairs + i)),
            pl.BlockSpec((rows, 128), lambda i: (0, i)),
        ],
        out_specs=pl.BlockSpec((rows, width), lambda i: (0, 0)),
        scratch_shapes=[pltpu.VMEM((rows, 128), F32), pltpu.VMEM((rows, 128), F32)],
        compiler_params=pltpu.CompilerParams(vmem_limit_bytes=32 * 2**20),
        cost_estimate=pl.CostEstimate(
            flops=10 * rows * rows * width // 3,
            bytes_accessed=rows * width * 5,
            transcendentals=rows * rows * pairs * 2,
        ),
    )(z, qkv, qkv, qkv, grad)


def cross_probs(q, keys, lanes, seen, scale):
    qh = jnp.where(lanes, q, jnp.zeros_like(q))
    s = jnp.where(seen, mm_cols(qh, keys) * scale, NEG)
    p = jnp.where(seen, jnp.exp(s - jnp.max(s, -1, keepdims=True)), 0.0)
    return qh, p / jnp.sum(p, -1, keepdims=True)


def cross_fwd_kernel(cap_ref, seg_ref, q_ref, k_ref, v_ref, o_ref, *, scale):
    seen = seg_ref[...] == cap_ref[0]
    q, keys, values = q_ref[...], k_ref[...], v_ref[...]
    first = lax.broadcasted_iota(jnp.int32, q.shape, 1) < 64
    outs = []
    for head in range(2):
        _, p = cross_probs(q, keys, first if head == 0 else ~first, seen, scale)
        outs.append(mm(p.astype(BF), values))
    o_ref[...] = jnp.where(first, outs[0], outs[1]).astype(BF)


def cross_fwd(cap, seg, cq, ckv, scale):
    rows, width = cq.shape
    text = ckv.shape[0]
    pairs = width // 128
    return pl.pallas_call(
        functools.partial(cross_fwd_kernel, scale=scale),
        grid=(pairs,),
        out_shape=jax.ShapeDtypeStruct((rows, width), BF),
        in_specs=[
            pl.BlockSpec(memory_space=pltpu.SMEM),
            pl.BlockSpec((1, text), lambda i: (0, 0)),
            pl.BlockSpec((rows, 128), lambda i: (0, i)),
            pl.BlockSpec((text, 128), lambda i: (0, i)),
            pl.BlockSpec((text, 128), lambda i: (0, pairs + i)),
        ],
        out_specs=pl.BlockSpec((rows, 128), lambda i: (0, i)),
        compiler_params=pltpu.CompilerParams(vmem_limit_bytes=32 * 2**20),
        cost_estimate=pl.CostEstimate(
            flops=4 * rows * text * width,
            bytes_accessed=rows * width * 4,
            transcendentals=rows * text * pairs * 2,
        ),
    )(cap, seg, cq, ckv, ckv)


def cross_bwd_kernel(cap_ref, seg_ref, q_ref, k_ref, v_ref, g_ref, dq_ref, dk_ref, dv_ref, *, scale):
    seen = seg_ref[...] == cap_ref[0]
    q, keys, values, grad = q_ref[...], k_ref[...], v_ref[...], g_ref[...]
    first = lax.broadcasted_iota(jnp.int32, q.shape, 1) < 64
    outs = []
    for head in range(2):
        lanes = first if head == 0 else ~first
        qh, p = cross_probs(q, keys, lanes, seen, scale)
        gh = jnp.where(lanes, grad, jnp.zeros_like(grad))
        dp = mm_cols(gh, values)
        ds = (p * (dp - jnp.sum(p * dp, -1, keepdims=True))).astype(BF)
        dv = mm_rows(p.astype(BF), gh)
        dk = mm_rows(ds, qh) * scale
        if head == 0:
            dv_ref[...] = dv
            dk_ref[...] = dk
        else:
            dv_ref[...] += dv
            dk_ref[...] += dk
        outs.append(mm(ds, keys))
    dq_ref[...] = (jnp.where(first, outs[0], outs[1]) * scale).astype(BF)


def cross_bwd(cap, seg, cq, ckv, grad, scale):
    rows, width = cq.shape
    text = ckv.shape[0]
    pairs = width // 128
    return pl.pallas_call(
        functools.partial(cross_bwd_kernel, scale=scale),
        grid=(pairs,),
        out_shape=[
            jax.ShapeDtypeStruct((rows, width), BF),
            jax.ShapeDtypeStruct((text, width), F32),
            jax.ShapeDtypeStruct((text, width), F32),
        ],
        in_specs=[
            pl.BlockSpec(memory_space=pltpu.SMEM),
            pl.BlockSpec((1, text), lambda i: (0, 0)),
            pl.BlockSpec((rows, 128), lambda i: (0, i)),
            pl.BlockSpec((text, 128), lambda i: (0, i)),
            pl.BlockSpec((text, 128), lambda i: (0, pairs + i)),
            pl.BlockSpec((rows, 128), lambda i: (0, i)),
        ],
        out_specs=[
            pl.BlockSpec((rows, 128), lambda i: (0, i)),
            pl.BlockSpec((text, 128), lambda i: (0, i)),
            pl.BlockSpec((text, 128), lambda i: (0, i)),
        ],
        compiler_params=pltpu.CompilerParams(vmem_limit_bytes=32 * 2**20),
        cost_estimate=pl.CostEstimate(
            flops=10 * rows * text * width,
            bytes_accessed=rows * width * 6,
            transcendentals=rows * text * pairs * 2,
        ),
    )(cap, seg, cq, ckv, ckv, grad)


def long_masks(g, rows):
    slot = jnp.arange(rows, dtype=jnp.int32) // (2 * STRIPE)
    rest = jnp.arange(rows, dtype=jnp.int32) % (2 * STRIPE)

    def positions(r):
        return ((g.z ^ slot) * g.t + r) * (2 * STRIPE) + rest

    key_pos = jnp.concatenate([positions((g.r - q) % g.t) for q in range(g.t)])
    return key_pos[None, :] <= positions(g.r)[:, None]


def long_gather(g, value):
    return jnp.concatenate([value] + [g.over_r(value, q) for q in range(1, g.t)], 0)


def long_fwd(g, qkv, scale):
    rows, width = qkv.shape
    head = 64
    heads = width // 3 // head
    keyval = long_gather(g, qkv[:, width // 3 :])
    q = qkv[:, : width // 3].reshape(rows, heads, head)
    k = keyval[:, : width // 3].reshape(-1, heads, head)
    v = keyval[:, width // 3 :].reshape(-1, heads, head)
    seen = long_masks(g, rows)[None]
    s = jnp.einsum("qhd,khd->hqk", q, k, preferred_element_type=F32) * scale
    s = jnp.where(seen, s, NEG)
    p = jnp.exp(s - jnp.max(s, -1, keepdims=True))
    p = p / jnp.sum(p, -1, keepdims=True)
    out = jnp.einsum("hqk,khd->qhd", p.astype(BF), v, preferred_element_type=F32)
    return out.reshape(rows, width // 3).astype(BF), (q, k, v, p)


def long_bwd(g, saved, grad, scale):
    q, k, v, p = saved
    rows, heads, head = q.shape
    width = heads * head
    grad = grad.reshape(rows, heads, head)
    dv = jnp.einsum("hqk,qhd->khd", p.astype(BF), grad, preferred_element_type=F32)
    dp = jnp.einsum("qhd,khd->hqk", grad, v, preferred_element_type=F32)
    ds = (p * (dp - jnp.sum(p * dp, -1, keepdims=True))).astype(BF)
    dq = jnp.einsum("hqk,khd->qhd", ds, k, preferred_element_type=F32) * scale
    dk = jnp.einsum("hqk,qhd->khd", ds, q, preferred_element_type=F32) * scale
    both = jnp.concatenate([dk.reshape(-1, width), dv.reshape(-1, width)], 1)
    both = both.reshape(g.t, rows, 2 * width)
    total = both[0]
    for step in range(1, g.t):
        total = total + g.over_r(both[step], -step)
    return jnp.concatenate([dq.reshape(rows, width).astype(BF), total.astype(BF)], 1)


def normed(values):
    center = values - jnp.mean(values, -1, keepdims=True)
    spread = lax.rsqrt(jnp.mean(center * center, -1, keepdims=True) + EPS)
    return center * spread, spread


def norm_back(unit, spread, gain, grad):
    f = grad * gain
    added = spread * (
        f - jnp.mean(f, -1, keepdims=True) - unit * jnp.mean(f * unit, -1, keepdims=True)
    )
    return added, jnp.sum(grad * unit, 0), jnp.sum(grad, 0)


def column_halves(weight, groups, mine):
    rows, width = weight.shape
    parts = weight.reshape(rows, groups, 2, width // groups // 2)
    return (
        pick(parts, 2, mine).reshape(rows, width // 2),
        pick(parts, 2, 1 - mine).reshape(rows, width // 2),
    )


def two(g, mine, other, axis):
    first = jnp.where(g.c == 0, mine, other)
    second = jnp.where(g.c == 0, other, mine)
    return jnp.stack([first, second], axis)


def gather_fast(g, scal, weights, ids, tokens, cotangent):
    gains, shifts, w_qkv, w_out, w_cq, w_ckv, w_co, w_up, w_down = weights
    share, depth = w_co.shape
    tall = w_down.shape[0]
    small = jnp.concatenate([gains, shifts], 0).T
    small = jnp.pad(small, ((0, 0), (0, 128 - small.shape[1])))
    keep1, send1 = prep_weights(scal, [(w_qkv, 6), (small, 0), (w_cq, 2)])
    keep2, send2 = prep_weights(scal, [(w_ckv, 4)], w_out)
    keep3, send3 = prep_weights(scal, [(w_up, 2)])
    blocks = prep_tokens(scal, ids, tokens, cotangent)
    got1 = g.over_c(send1)
    got2 = g.over_c(jnp.concatenate([send2, send3], 1))

    def shape(kinds, rows, width):
        return (2, kinds, 4, 2, rows, width)

    n_qkv, n_cq, n_ckv, n_up = (w.shape[1] // 2 for w in (w_qkv, w_cq, w_ckv, w_up))
    groups = tall // share // 2
    low, high = (
        list(half.reshape(groups, share, depth))
        for half in (w_down[: tall // 2], w_down[tall // 2 :])
    )
    second = jnp.stack([keep2, jnp.concatenate([got2[:, :n_ckv], w_co], 1)])
    third = jnp.stack(
        [jnp.concatenate([keep3] + low, 1), jnp.concatenate([got2[:, n_ckv:]] + high, 1)]
    )
    first = after(jnp.stack([keep1, got1]), second, third)
    third_low, third_high = third[:1], third[1:]
    tok, cot = list(blocks[:4]), list(blocks[4:])

    near, far = g.gather_near, g.gather_far

    got_a = [first] + [g.xor_z(first, k) for k in (1, 2, 3)]
    tok[0], cot[0] = g.regroup(tok[0], 0), g.regroup(cot[0], 0)
    line_a = gather_line(scal, got_a)

    line_a, second, late = after((line_a, second, tok[3]), got_a, tok[0], cot[0])
    near_a = near(line_a)
    got_b = [second] + [g.xor_z(second, k) for k in (1, 2)]
    tok[3] = g.regroup(late, 3)

    near_a, second, third, third_low = after((near_a, second, third, third_low), got_b, tok[3])
    far_a = far(line_a, near_a)
    got_b.append(g.xor_z(second, 3))
    got_c1 = g.xor_z(third, 1)
    got_c2 = g.xor_z(third_low, 2)
    line_b = gather_line(scal, got_b)

    line_b, third_high, *late = after((line_b, third_high, *tok[1:3]), far_a, got_c1, got_c2)
    near_b = near(line_b)
    got_c2 = jnp.concatenate([got_c2, g.xor_z(third_high, 2)], 0)
    tok[1:3] = [g.regroup(late[k - 1], k) for k in (1, 2)]

    near_b, third, tok = after((near_b, third, tok), got_c2)
    far_b = far(line_b, near_b)
    got_c = [third, got_c1, got_c2, g.xor_z(third, 3)]
    resid = join_tokens(scal, tok, g.over_c(jnp.stack(tok)))
    line_c = gather_line(scal, got_c)

    line_c, *late = after((line_c, *cot[1:]), far_b)
    near_c = near(line_c)
    cot[1:] = [g.regroup(late[k - 1], k) for k in (1, 2, 3)]

    near_c, cot = after((near_c, cot))
    far_c = far(line_c, near_c)
    cot = join_tokens(scal, cot, g.over_c(jnp.stack(cot)))

    qkv, small, cq = gather_place(
        scal,
        *far_a,
        [shape(2, share, n_qkv), shape(2, share, 128), shape(2, share, n_cq)],
        [[(n_qkv, 0, None, 0), (128, 1, None, 0), (n_cq, 2, None, 0)]] * 2,
    )
    ckv, out, co = gather_place(
        scal,
        *far_b,
        [shape(2, share, n_ckv), shape(1, share, depth), shape(1, share, depth)],
        [[(n_ckv, 0, None, 0), (depth, 1 + half, 0, 0)] for half in range(2)],
    )

    def flat(array):
        return array.reshape(-1, array.shape[-1])

    def last(far_c):
        up, down = gather_place(
            scal,
            *far_c,
            [shape(2, share, n_up), shape(1, tall, depth)],
            [
                [(n_up, 0, None, 0)]
                + [(depth, 1, 0, (half * groups + i) * share) for i in range(groups)]
                for half in range(2)
            ],
        )
        return flat(up), flat(down)

    return (
        (resid, cot, far_c),
        last,
        flat(small)[:, :6].astype(F32).T,
    ) + tuple(flat(array) for array in (qkv, out, cq, ckv, co))


def gather_plain(g, weights):
    gains, shifts, w_qkv, w_out, w_cq, w_ckv, w_co, w_up, w_down = weights
    small = lax.all_gather(jnp.concatenate([gains, shifts], 0), AXES, axis=1, tiled=True)

    def columns(weight, groups):
        whole = lax.all_gather(weight, AXES, axis=0, tiled=True)
        return column_halves(whole, groups, g.c)[0]

    def rows(weight):
        whole = lax.all_gather(weight, AXES, axis=0, tiled=True)
        parts = whole.reshape(2, 2, whole.shape[0] // 4, whole.shape[1])
        return pick(parts, 1, g.c).reshape(whole.shape[0] // 2, whole.shape[1])

    return (
        small.astype(F32),
        columns(w_qkv, 6),
        rows(w_out),
        columns(w_cq, 2),
        columns(w_ckv, 4),
        rows(w_co),
        columns(w_up, 2),
        rows(w_down),
    )


def join_columns(g, keep, got, groups):
    rows, width = keep.shape
    block = width // groups
    parts = two(g, keep.reshape(rows, groups, block), got.reshape(rows, groups, block), 2)
    return parts.reshape(rows, 2 * width)


def scatter_columns_plain(g, grad, groups):
    rows, width = grad.shape
    whole = join_columns(g, grad, jnp.zeros_like(grad), groups)
    return lax.psum_scatter(whole, AXES, scatter_dimension=0, tiled=True)


def scatter_rows_plain(g, grad):
    rows, width = grad.shape
    parts = grad.reshape(2, rows // 2, width)
    whole = two(g, parts, jnp.zeros_like(parts), 1).reshape(2 * rows, width)
    return lax.psum_scatter(whole, AXES, scatter_dimension=0, tiled=True)


def both_cores(g, part):
    low = part.astype(BF)
    return low.astype(F32) + g.over_c(low).astype(F32)


def local(
    tokens,
    text_states,
    image_ids,
    text_segments,
    image_caption,
    norm_gains,
    norm_shifts,
    self_qkv,
    self_out,
    cross_query,
    cross_keyval,
    cross_out,
    mlp_up,
    mlp_down,
    cotangent,
    *,
    dp,
    seq,
):
    g = Grid(dp, seq)
    fast = g.t == 1
    depth = tokens.shape[-1]
    scale = (depth // H) ** (-0.5)
    weights = (
        norm_gains,
        norm_shifts,
        self_qkv,
        self_out,
        cross_query,
        cross_keyval,
        cross_out,
        mlp_up,
        mlp_down,
    )

    scal = jnp.stack([g.x, g.c, g.z, g.y]).astype(jnp.int32)
    start = image_ids[:, 0] & 1
    if fast:
        ((resid, cot, far_c), place_last, small, w_qkv, w_out, w_cq, w_ckv, w_co) = gather_fast(
            g, scal, weights, image_ids, tokens, cotangent
        )
    else:
        (small, w_qkv, w_out, w_cq, w_ckv, w_co, w_up, w_down) = gather_plain(g, weights)
        both = jnp.stack([tokens, cotangent], 2).reshape(4, STRIPE, 2 * depth)
        received = []
        for step in range(4):
            j = g.z ^ step
            half = (j & 1) ^ start[j >> 1]
            received.append(g.regroup(pick(both, 0, (j >> 1) * 2 + half), step))
        mine = jnp.stack(received)
        held = two(g, mine, g.over_c(mine), 1).reshape(8 * STRIPE, 2, depth)
        resid, cot = held[:, 0], held[:, 1]
    resid = resid.astype(F32)
    gain, shift = small[:3], small[3:]

    image = (g.x * 2 + g.y) * 2 + (g.z & 1)
    cap = image_caption[g.z >> 1, image].reshape(1)
    seg = text_segments.reshape(1, -1)
    slot = g.z.reshape(1).astype(jnp.int32)

    unit_one, spread_one = normed(resid)
    n_one = (unit_one * gain[0] + shift[0]).astype(BF)
    qkv = mm(n_one, w_qkv).astype(BF)
    if fast:
        attended = attn_fwd(slot, qkv, scale)
    else:
        attended, saved = long_fwd(g, qkv, scale)
    hidden_one = resid + both_cores(g, mm(attended, w_out))
    unit_two, spread_two = normed(hidden_one)
    n_two = (unit_two * gain[1] + shift[1]).astype(BF)
    cq = mm(n_two, w_cq).astype(BF)
    ckv = mm(text_states, w_ckv).astype(BF)
    crossed = cross_fwd(cap, seg, cq, ckv, scale)
    hidden_two = hidden_one + both_cores(g, mm(crossed, w_co))
    unit_three, spread_three = normed(hidden_two)
    n_three = (unit_three * gain[2] + shift[2]).astype(BF)
    if fast:
        w_up, w_down = place_last(far_c)
    up = mm(n_three, w_up)
    inner = jnp.tanh(GELU_C * (up + 0.044715 * up * up * up))
    act = (0.5 * up * (1.0 + inner)).astype(BF)

    def halves(value):
        parts = value.reshape(4, 2, STRIPE, value.shape[-1])
        return pick(parts, 1, g.c), pick(parts, 1, 1 - g.c)

    down = mm(act, w_down)
    keep, gone = halves(down)

    def finish(gone):
        return (halves(hidden_two)[0] + keep + g.over_c(gone).astype(F32)).astype(BF)

    grad_down = mm_rows(act, cot)
    slope = 0.5 * (1.0 + inner) + 0.5 * up * (1.0 - inner * inner) * GELU_C * (
        1.0 + 3 * 0.044715 * up * up
    )
    d_up = (mm_cols(cot, w_down) * slope).astype(BF)
    grad_up = mm_rows(n_three, d_up)
    share = depth // g.count
    if fast:
        mlp = by_rows(grad_down.astype(BF), share) + by_columns(grad_up.astype(BF), share)
        mlp_far, gone = after((fold_far(scal, share, mlp), gone.astype(BF)))
        mlp_far = g.over_y(mlp_far[0]), g.over_x(mlp_far[1])
        out = finish(gone)
        out_home = [g.regroup(out[k], k) for k in range(4)]
    else:
        out = finish(gone.astype(BF))
    added, gain_three, shift_three = norm_back(
        unit_three, spread_three, gain[2], both_cores(g, mm_cols(d_up, w_up))
    )
    g_two = cot.astype(F32) + added
    d_cross = g_two.astype(BF)
    grad_co = mm_rows(crossed, d_cross)
    d_crossed = mm_cols(d_cross, w_co).astype(BF)
    d_cq, d_ck, d_cv = cross_bwd(cap, seg, cq, ckv, d_crossed, scale)
    grad_cq = mm_rows(n_two, d_cq)
    if fast:
        cross = by_rows(grad_co.astype(BF), share) + by_columns(grad_cq.astype(BF), share)
        d_ckv = jnp.concatenate([d_ck, d_cv], 1).astype(BF)
    added, gain_two, shift_two = norm_back(
        unit_two, spread_two, gain[1], both_cores(g, mm_cols(d_cq, w_cq))
    )
    g_one = g_two + added
    d_self = g_one.astype(BF)
    grad_out = mm_rows(attended, d_self)
    d_att = mm_cols(d_self, w_out).astype(BF)
    if fast:
        near_ready, cross_far, swapped = after(
            (
                fold_near(scal, share, [(mlp, mlp_far)]),
                fold_far(scal, share, cross),
                d_ckv,
            ),
            mlp_far,
            out_home,
        )
        mlp_near = g.over_x(near_ready[0]), g.over_y(near_ready[1])
        cross_far = g.over_y(cross_far[0]), g.over_x(cross_far[1])
        d_ckv = swapped
        swapped = g.xor_z(swapped, 1)
        d_qkv = attn_bwd(slot, qkv, after(d_att, near_ready), scale)
        d_ckv = plus(d_ckv, swapped)
        mlp_line = fold_line(scal, share, [(mlp, mlp_far, mlp_near)])
        swapped = g.xor_z(d_ckv, 2)
    else:
        d_qkv = long_bwd(g, saved, d_att, scale)
    grad_qkv = mm_rows(n_one, d_qkv)
    added, gain_one, shift_one = norm_back(
        unit_one, spread_one, gain[0], both_cores(g, mm_cols(d_qkv, w_qkv))
    )
    grad_in = (g_one + added).astype(BF)

    norms = jnp.stack([gain_one, gain_two, gain_three, shift_one, shift_two, shift_three])
    back = halves(grad_in)[0]
    if fast:
        last = by_rows(grad_out.astype(BF), share) + by_columns(grad_qkv.astype(BF), share)
        d_ckv = plus(d_ckv, swapped)
        last_far, mlp_line = after(
            (fold_far(scal, share, last), mlp_line), cross_far, mlp_near, swapped
        )
        last_far = g.over_y(last_far[0]), g.over_x(last_far[1])
        mlp_terms = [mlp_line[0]] + [g.xor_z(mlp_line[k], k) for k in (1, 2)]

        near_last = fold_near(scal, share, [(last, last_far)])
        near_cross = fold_near(scal, share, [(cross, cross_far)])
        near_last, near_cross, mlp_line, d_ckv, norms = after(
            (near_last, near_cross, mlp_line, d_ckv, norms), last_far, mlp_terms[1:]
        )
        near_last = g.over_x(near_last[0]), g.over_y(near_last[1])
        near_cross = g.over_x(near_cross[0]), g.over_y(near_cross[1])
        mlp_terms.append(g.xor_z(mlp_line[3], 3))
        d_ckv = plus(d_ckv, g.over_x(d_ckv))
        norms = norms + g.over_y(norms)

        line = fold_line(
            scal, share, [(last, last_far, near_last), (cross, cross_far, near_cross)]
        )
        line, back, mlp_terms, d_ckv, norms = after((line, back, mlp_terms, d_ckv, norms))
        terms = [line[0]] + [g.xor_z(line[k], k) for k in (1, 2, 3)]
        back = [g.regroup(back[k], k) for k in range(4)]
        mlp_terms = after(mlp_terms, back)
        d_ckv = plus(d_ckv, g.over_y(d_ckv))
        norms = after(norms + g.over_x(norms), terms)
        norms = norms + g.xor_z(norms, 1)
        norms = norms + g.xor_z(norms, 2)
        norms = lax.dynamic_slice_in_dim(norms, g.me * share, share, 1)
        output, grad_tokens = place_home(scal, image_ids, out_home, back)
        d_ckv_whole = join_columns(g, d_ckv, g.over_c(d_ckv), 4)
    else:
        back = jnp.concatenate([out, back], 2)
        back = jnp.stack([g.regroup(back[step], step) for step in range(4)])
        order = []
        for block in range(4):
            j = (block & 2) + ((block & 1) ^ start[block >> 1])
            order.append(pick(back, 0, j ^ g.z))
        back = jnp.stack(order).reshape(2, 2 * STRIPE, 2 * depth)
        output, grad_tokens = back[:, :, :depth], back[:, :, depth:].astype(F32)
        d_ckv = jnp.concatenate([d_ck, d_cv], 1)
        whole = join_columns(g, d_ckv, jnp.zeros_like(d_ckv), 4)
        d_ckv_whole = lax.psum(whole, AXES).astype(BF)
        d_ckv = column_halves(d_ckv_whole, 4, g.c)[0]
        norms = lax.psum(norms, AXES) * 0.5
        norms = lax.dynamic_slice_in_dim(norms, g.me * (depth // g.count), depth // g.count, 1)
    part = mm_cols(d_ckv, w_ckv)
    grad_text = part + g.over_c(part)
    text_cols = lax.dynamic_slice_in_dim(text_states, g.me * share, share, 1)
    grad_ckv = mm_rows(text_cols, d_ckv_whole)
    if fast:
        tall = mlp_down.shape[0]

        def columns(terms, low, high, groups):
            got = g.over_c(plus(*[pick(term, 0, 1 - g.c)[:, low:high] for term in terms]))
            keep = sum(pick(term, 0, g.c)[:, low:high].astype(F32) for term in terms)
            return join_columns(g, keep, got.astype(F32), groups)

        n_down = tall // share // 2 * depth
        grad_down = summed(mlp_terms, ALL, ALL, slice(0, n_down))
        grad_down = grad_down.reshape(2, share, tall // share // 2, depth)
        grad_down = grad_down.transpose(0, 2, 1, 3).reshape(tall, depth)
        grad_up = columns(mlp_terms, n_down, None, 2)
        half = depth // 2
        to_qkv = half + grad_qkv.shape[1]

        def halves_of(start):
            total = summed(terms, ALL, ALL, slice(start, start + half))
            return jnp.concatenate([total[0], total[1]], 1)

        grad_out = halves_of(0)
        grad_qkv = columns(terms, half, to_qkv, 6)
        grad_co = halves_of(to_qkv)
        grad_cq = columns(terms, to_qkv + half, None, 2)
    else:
        grad_down = scatter_rows_plain(g, grad_down)
        grad_up = scatter_columns_plain(g, grad_up, 2)
        grad_co = scatter_rows_plain(g, grad_co)
        grad_cq = scatter_columns_plain(g, grad_cq, 2)
        grad_out = scatter_rows_plain(g, grad_out)
        grad_qkv = scatter_columns_plain(g, grad_qkv, 6)
    return (
        output,
        grad_tokens,
        grad_text,
        norms[:3],
        norms[3:5],
        grad_qkv,
        grad_out,
        grad_cq,
        grad_ckv,
        grad_co,
        grad_up,
        grad_down,
        norms[5],
    )


def solution(mesh):
    both = ("dp", "seq")
    rows = P(both, None)
    in_specs = (
        P(None, both, None),
        P(),
        P(None, both),
        P(),
        P(),
        P(None, both),
        P(None, both),
        rows,
        rows,
        rows,
        rows,
        rows,
        rows,
        rows,
        P(None, both, None),
    )
    out_specs = (
        P(None, both, None),
        P(None, both, None),
        P(),
        P(None, both),
        P(None, both),
        rows,
        rows,
        rows,
        rows,
        rows,
        rows,
        rows,
        P(both),
    )
    body = functools.partial(local, dp=mesh.shape["dp"], seq=mesh.shape["seq"])
    return jax.shard_map(body, mesh=mesh, in_specs=in_specs, out_specs=out_specs, check_vma=False)
```

```python
import functools

import jax
import jax.numpy as jnp
from jax import lax
from jax.experimental import pallas as pl
from jax.experimental.pallas import tpu as pltpu
from jax.sharding import PartitionSpec as P

H = 16
STRIPE = 64
EPS = 1e-05
NEG = -1e30
GELU_C = 0.7978845608028654
BF = jnp.bfloat16
F32 = jnp.float32
AXES = ("dp", "seq")


def mm(left, right):
    return jnp.dot(left, right, preferred_element_type=F32)


def mm_rows(left, right):
    return lax.dot_general(left, right, (((0,), (0,)), ((), ())), preferred_element_type=F32)


def mm_cols(left, right):
    return lax.dot_general(left, right, (((1,), (1,)), ((), ())), preferred_element_type=F32)


def pick(array, dim, index):
    return lax.dynamic_index_in_dim(array, index, dim, keepdims=False)


class Grid:
    def __init__(self, dp, seq):
        self.dp, self.seq, self.t = dp, seq, seq // 8
        self.count = dp * seq
        me = lax.axis_index(AXES)
        part = lax.rem(me, seq)
        self.me = me
        self.x = me // (2 * seq)
        self.c = lax.rem(me // seq, 2)
        self.z = part // (2 * self.t)
        self.r = lax.rem(part // 2, self.t)
        self.y = lax.rem(part, 2)

    def coords(self, d):
        part = d % self.seq
        return (
            d // (2 * self.seq),
            d // self.seq % 2,
            part // (2 * self.t),
            part // 2 % self.t,
            part % 2,
        )

    def index(self, x, c, z, r, y):
        return (x * 2 + c) * self.seq + (z * self.t + r) * 2 + y

    def send(self, value, move):
        perm = [(d, self.index(*move(*self.coords(d)))) for d in range(self.count)]
        return lax.ppermute(value, AXES, perm)

    def over_c(self, value):
        return self.send(value, lambda x, c, z, r, y: (x, 1 - c, z, r, y))

    def over_x(self, value):
        return self.send(value, lambda x, c, z, r, y: (1 - x, c, z, r, y))

    def over_y(self, value):
        return self.send(value, lambda x, c, z, r, y: (x, c, z, r, 1 - y))

    def xor_z(self, value, bits):
        return self.send(value, lambda x, c, z, r, y: (x, c, z ^ bits, r, y))

    def over_r(self, value, step):
        return self.send(value, lambda x, c, z, r, y: (x, c, z, (r + step) % self.t, y))

    def regroup(self, value, bits):
        return self.send(value, lambda x, c, z, r, y: (x, y, z ^ bits, r, c))

    def gather_near(self, lines):
        return self.over_x(lines[0]), self.over_y(lines[1])

    def gather_far(self, lines, got):
        pair_a, pair_b = jnp.stack([lines[0], got[0]]), jnp.stack([lines[1], got[1]])
        return pair_a, self.over_y(pair_a), pair_b, self.over_x(pair_b)

    def swap(self, value):
        return self.send(value, lambda x, c, z, r, y: (x, y, z, r, c))


def after(value, *others):
    return lax.optimization_barrier((value, others))[0]


def place(scalars, sources, shapes, copies):
    def kernel(s_ref, *refs):
        ins = refs[: len(sources)]
        outs = refs[len(sources) : len(sources) + len(shapes)]
        sems = refs[-1]
        started = []
        for i, (source, at, target, to) in enumerate(copies):
            copy = pltpu.make_async_copy(
                ins[source].at[at(s_ref)], outs[target].at[to(s_ref)], sems.at[i]
            )
            copy.start()
            started.append(copy)
        for copy in started:
            copy.wait()

    moved = sum(source.size * 2 for source in sources)
    return pl.pallas_call(
        kernel,
        out_shape=[jax.ShapeDtypeStruct(shape, BF) for shape in shapes],
        in_specs=[pl.BlockSpec(memory_space=pltpu.SMEM)]
        + [pl.BlockSpec(memory_space=pl.ANY)] * len(sources),
        out_specs=[pl.BlockSpec(memory_space=pltpu.VMEM)] * len(shapes),
        scratch_shapes=[pltpu.SemaphoreType.DMA((len(copies),))],
        compiler_params=pltpu.CompilerParams(vmem_limit_bytes=32 * 2**20),
        cost_estimate=pl.CostEstimate(flops=0, bytes_accessed=2 * moved, transcendentals=0),
    )(scalars, *sources)


ALL = slice(None)


def gather_line(scal, got):
    _, rows, width = got[0].shape
    return place(
        scal,
        got,
        [(4, rows, width)] * 2,
        [
            (k, lambda s, h=h: (h,), h, lambda s, k=k: (s[2] ^ k,))
            for k in range(4)
            for h in range(2)
        ],
    )


def gather_place(scal, pair_a, far_a, pair_b, far_b, shapes, targets):
    rows = pair_a.shape[2]
    copies = []
    for i, half in enumerate((0, 0, 1, 1)):
        far = i % 2
        for near in range(2):
            dx, dy = (near, far) if half == 0 else (far, near)
            start = 0
            for wide, out, kind, row in targets[half]:
                copies.append(
                    (
                        i,
                        lambda s, near=near, start=start, wide=wide: (
                            near,
                            ALL,
                            ALL,
                            pl.ds(start, wide),
                        ),
                        out,
                        lambda s, dx=dx, dy=dy, kind=kind, row=row, half=half: (
                            s[0] ^ dx,
                            s[1] ^ half if kind is None else kind,
                            ALL,
                            s[3] ^ dy,
                            pl.ds(row, rows),
                        ),
                    )
                )
                start += wide
    return place(scal, [pair_a, far_a, pair_b, far_b], shapes, copies)


def plus(*terms):
    total = terms[0].astype(F32)
    for term in terms[1:]:
        total = total + term.astype(F32)
    return total.astype(BF)


def by_columns(array, share):
    view = array.reshape(2, 2, 4, 2, share, array.shape[1])
    block = (None, None, None, None, share, array.shape[1])
    return [(view, block, lambda x, z, y, h, i: (x, h, z, y, 0, 0))]


def by_rows(array, share):
    groups, width = array.shape[0] // (16 * share), array.shape[1]
    if groups == 1:
        view = array.reshape(2, 4, 2, share, width)
        block = (None, None, None, share, width // 2)
        return [(view, block, lambda x, z, y, h, i: (x, z, y, 0, h))]
    view = array.reshape(2, 4, 2, groups, share, width)
    block = (None, None, None, None, share, width)
    return [
        (view, block, lambda x, z, y, h, i, j=j: (x, z, y, h * (groups // 2) + j, 0, 0))
        for j in range(groups // 2)
    ]


def by_steps(array):
    return [(array, (None, None) + array.shape[2:], lambda x, z, y, h, i: (i, h, 0, 0))]


def fold(scal, groups, steps, share, places, outs):
    arrays, specs, parts, width = [], [], [], 0
    for slots, received in groups:
        wide = sum(block[-1] for _, block, _ in slots)
        for h in range(2):
            extras, at = [], 0
            for array, at_step in received[h]:
                extras.append(len(arrays))
                arrays.append(array)
                specs.append(
                    pl.BlockSpec(
                        (None, share, wide),
                        lambda i, s, f=at_step: (f(i, s), 0, 0),
                    )
                )
            for view, block, index in slots:
                parts.append((h, len(arrays), extras, at, width + at, block[-1]))
                arrays.append(view)
                specs.append(
                    pl.BlockSpec(block, lambda i, s, h=h, f=index: f(*places[h](i, s), h, i))
                )
                at += block[-1]
        width += wide

    def kernel(s_ref, *refs):
        step = pl.program_id(0)
        ins, targets = refs[: len(arrays)], refs[len(arrays) :]
        for h, own, extras, at, to, wide in parts:
            value = ins[own][...]
            if extras:
                value = value.astype(F32)
                for extra in extras:
                    value = value + ins[extra][:, pl.ds(at, wide)].astype(F32)
                value = value.astype(BF)
            if outs is None:
                targets[h][:, pl.ds(to, wide)] = value
            else:
                for j in range(steps):

                    @pl.when(step == j)
                    def _():
                        targets[j][h, :, pl.ds(to, wide)] = value

    if outs is None:
        out_shape = [jax.ShapeDtypeStruct((steps, share, width), BF)] * 2
        out_specs = [pl.BlockSpec((None, share, width), lambda i, s: (i, 0, 0))] * 2
    else:
        out_shape = [jax.ShapeDtypeStruct((2, share, width), BF)] * steps
        out_specs = [pl.BlockSpec((2, share, width), lambda i, s: (0, 0, 0))] * steps
    return pl.pallas_call(
        kernel,
        grid_spec=pltpu.PrefetchScalarGridSpec(
            num_scalar_prefetch=1, grid=(steps,), in_specs=specs, out_specs=out_specs
        ),
        out_shape=out_shape,
        compiler_params=pltpu.CompilerParams(vmem_limit_bytes=32 * 2**20),
        cost_estimate=pl.CostEstimate(
            flops=0, bytes_accessed=2 * steps * share * width * 6, transcendentals=0
        ),
    )(scal, *arrays)


def fold_far(scal, share, slots):
    return fold(
        scal,
        [(slots, [[], []])],
        8,
        share,
        [
            lambda i, s: (i // 4, lax.rem(i, 4), 1 - s[3]),
            lambda i, s: (1 - s[0], i // 2, lax.rem(i, 2)),
        ],
        None,
    )


def fold_near(scal, share, chunks):
    return fold(
        scal,
        [
            (
                slots,
                [
                    [(far[0], lambda i, s: (1 - s[0]) * 4 + i)],
                    [(far[1], lambda i, s: i * 2 + 1 - s[3])],
                ],
            )
            for slots, far in chunks
        ],
        4,
        share,
        [lambda i, s: (1 - s[0], i, s[3]), lambda i, s: (s[0], i, 1 - s[3])],
        None,
    )


def fold_line(scal, share, chunks, more=()):
    groups = []
    for slots, far, near in chunks:
        groups.append(
            (
                slots,
                [
                    [
                        (far[0], lambda i, s: s[0] * 4 + (s[2] ^ i)),
                        (near[0], lambda i, s: s[2] ^ i),
                    ],
                    [
                        (far[1], lambda i, s: (s[2] ^ i) * 2 + s[3]),
                        (near[1], lambda i, s: s[2] ^ i),
                    ],
                ],
            )
        )
    if more:
        groups.append((list(more), [[], []]))
    return fold(
        scal, groups, 4, share, [lambda i, s: (s[0], s[2] ^ i, s[3])] * 2, True
    )


def summed(terms, *at):
    return sum(term[at].astype(F32) for term in terms)


def prep_weights(scal, sources, whole=None):
    share = sources[0][0].shape[0]
    more = 0 if whole is None else whole.shape[1]
    width = sum(array.shape[1] // (2 if groups else 1) for array, groups in sources)

    def kernel(s_ref, *refs):
        low = s_ref[1] == 0
        keep, send = refs[-2:]
        start = 0
        for ref, (_, groups) in zip(refs, sources):
            if groups == 0:
                keep[:, pl.ds(start, ref.shape[1])] = ref[...]
                send[:, pl.ds(start, ref.shape[1])] = ref[...]
                start += ref.shape[1]
                continue
            block = ref.shape[1] // groups // 2
            for i in range(groups):
                a = ref[:, pl.ds(2 * i * block, block)]
                b = ref[:, pl.ds((2 * i + 1) * block, block)]
                keep[:, pl.ds(start, block)] = jnp.where(low, a, b)
                send[:, pl.ds(start, block)] = jnp.where(low, b, a)
                start += block
        if whole is not None:
            keep[:, pl.ds(start, more)] = refs[len(sources)][...]

    vmem = pl.BlockSpec(memory_space=pltpu.VMEM)
    smem = pl.BlockSpec(memory_space=pltpu.SMEM)
    arrays = [array for array, _ in sources] + ([] if whole is None else [whole])
    return pl.pallas_call(
        kernel,
        in_specs=[smem] + [vmem] * len(arrays),
        out_specs=[vmem] * 2,
        out_shape=[
            jax.ShapeDtypeStruct((share, width + more), BF),
            jax.ShapeDtypeStruct((share, width), BF),
        ],
        compiler_params=pltpu.CompilerParams(vmem_limit_bytes=32 * 2**20),
    )(scal, *arrays)


def prep_tokens(scal, ids, tokens, cotangent):
    depth = tokens.shape[2]

    def kernel(s_ref, ids_ref, tok, cot, *blocks):
        for step in range(4):
            j = s_ref[2] ^ step
            b = j >> 1
            half = (j & 1) ^ (ids_ref[b, 0] & 1)
            rows = pl.ds(pl.multiple_of(half * STRIPE, STRIPE), STRIPE)
            blocks[step][...] = tok[b, rows, :]
            blocks[4 + step][...] = cot[b, rows, :]

    vmem = pl.BlockSpec(memory_space=pltpu.VMEM)
    smem = pl.BlockSpec(memory_space=pltpu.SMEM)
    return pl.pallas_call(
        kernel,
        in_specs=[smem, smem, vmem, vmem],
        out_specs=[vmem] * 8,
        out_shape=[jax.ShapeDtypeStruct((STRIPE, depth), BF)] * 8,
        compiler_params=pltpu.CompilerParams(vmem_limit_bytes=32 * 2**20),
    )(scal, ids, tokens, cotangent)


def join_tokens(scal, mine, other):
    _, rows, depth = other.shape

    def kernel(s_ref, a0, a1, a2, a3, o_ref, out):
        for step, ref in enumerate((a0, a1, a2, a3)):
            for part, core in ((ref, s_ref[1]), (o_ref.at[step], 1 - s_ref[1])):
                at = pl.ds(pl.multiple_of((2 * step + core) * rows, rows), rows)
                out[at, :] = part[...]

    vmem = pl.BlockSpec(memory_space=pltpu.VMEM)
    return pl.pallas_call(
        kernel,
        in_specs=[pl.BlockSpec(memory_space=pltpu.SMEM)] + [vmem] * 5,
        out_specs=vmem,
        out_shape=jax.ShapeDtypeStruct((8 * rows, depth), BF),
        compiler_params=pltpu.CompilerParams(vmem_limit_bytes=32 * 2**20),
    )(scal, *mine, other)


def place_home(scal, ids, outs, grads):
    rows, depth = outs[0].shape

    def kernel(s_ref, ids_ref, *refs):
        out, grad = refs[8:]
        for step in range(4):
            j = s_ref[2] ^ step
            b = j >> 1
            half = (j & 1) ^ (ids_ref[b, 0] & 1)
            at = pl.ds(pl.multiple_of(half * rows, rows), rows)
            out[b, at, :] = refs[step][...]
            grad[b, at, :] = refs[4 + step][...].astype(F32)

    vmem = pl.BlockSpec(memory_space=pltpu.VMEM)
    smem = pl.BlockSpec(memory_space=pltpu.SMEM)
    return pl.pallas_call(
        kernel,
        in_specs=[smem, smem] + [vmem] * 8,
        out_specs=[vmem] * 2,
        out_shape=[
            jax.ShapeDtypeStruct((2, 2 * rows, depth), BF),
            jax.ShapeDtypeStruct((2, 2 * rows, depth), F32),
        ],
        compiler_params=pltpu.CompilerParams(vmem_limit_bytes=32 * 2**20),
    )(scal, ids, *outs, *grads)


def attn_fwd_kernel(z_ref, q_ref, k_ref, v_ref, o_ref, *, scale):
    z = z_ref[0]
    size = q_ref.shape[0] // 4
    starts = [pl.multiple_of((z ^ h) * size, size) for h in range(4)]
    keys = jnp.concatenate([k_ref[pl.ds(s, size), :] for s in starts], 0)
    values = jnp.concatenate([v_ref[pl.ds(s, size), :] for s in starts], 0)
    first = lax.broadcasted_iota(jnp.int32, (size, 128), 1) < 64
    for j in range(4):
        span = (j + 1) * size
        q = q_ref[pl.ds(starts[j], size), :]
        row = lax.broadcasted_iota(jnp.int32, (size, span), 0) + j * size
        seen = lax.broadcasted_iota(jnp.int32, (size, span), 1) <= row
        outs = []
        for head in range(2):
            lanes = first if head == 0 else ~first
            qh = jnp.where(lanes, q, jnp.zeros_like(q))
            s = mm_cols(qh, keys[:span]) * scale
            s = jnp.where(seen, s, NEG)
            p = jnp.exp(s - jnp.max(s, -1, keepdims=True))
            total = jnp.sum(p, -1, keepdims=True)
            outs.append(mm(p.astype(BF), values[:span]) / total)
        o_ref[pl.ds(starts[j], size), :] = jnp.where(first, outs[0], outs[1]).astype(BF)


def attn_fwd(z, qkv, scale):
    rows, width = qkv.shape
    pairs = width // 3 // 128
    return pl.pallas_call(
        functools.partial(attn_fwd_kernel, scale=scale),
        grid=(pairs,),
        out_shape=jax.ShapeDtypeStruct((rows, width // 3), BF),
        in_specs=[
            pl.BlockSpec(memory_space=pltpu.SMEM),
            pl.BlockSpec((rows, 128), lambda i: (0, i)),
            pl.BlockSpec((rows, 128), lambda i: (0, pairs + i)),
            pl.BlockSpec((rows, 128), lambda i: (0, 2 * pairs + i)),
        ],
        out_specs=pl.BlockSpec((rows, 128), lambda i: (0, i)),
        compiler_params=pltpu.CompilerParams(vmem_limit_bytes=32 * 2**20),
        cost_estimate=pl.CostEstimate(
            flops=4 * rows * rows * width // 3,
            bytes_accessed=rows * width * 3,
            transcendentals=rows * rows * pairs * 2,
        ),
    )(z, qkv, qkv, qkv)


def attn_bwd_kernel(z_ref, q_ref, k_ref, v_ref, g_ref, d_ref, dk_ref, dv_ref, *, scale, pairs):
    z = z_ref[0]
    at = pl.program_id(0)
    size = q_ref.shape[0] // 4
    starts = [pl.multiple_of((z ^ h) * size, size) for h in range(4)]
    keys = jnp.concatenate([k_ref[pl.ds(s, size), :] for s in starts], 0)
    values = jnp.concatenate([v_ref[pl.ds(s, size), :] for s in starts], 0)
    first = lax.broadcasted_iota(jnp.int32, (size, 128), 1) < 64
    dk_ref[...] = jnp.zeros_like(dk_ref)
    dv_ref[...] = jnp.zeros_like(dv_ref)
    for j in range(4):
        span = (j + 1) * size
        q = q_ref[pl.ds(starts[j], size), :]
        grad = g_ref[pl.ds(starts[j], size), :]
        row = lax.broadcasted_iota(jnp.int32, (size, span), 0) + j * size
        seen = lax.broadcasted_iota(jnp.int32, (size, span), 1) <= row
        outs = []
        for head in range(2):
            lanes = first if head == 0 else ~first
            qh = jnp.where(lanes, q, jnp.zeros_like(q))
            gh = jnp.where(lanes, grad, jnp.zeros_like(grad))
            s = mm_cols(qh, keys[:span]) * scale
            s = jnp.where(seen, s, NEG)
            p = jnp.exp(s - jnp.max(s, -1, keepdims=True))
            p = p / jnp.sum(p, -1, keepdims=True)
            dp = mm_cols(gh, values[:span])
            ds = (p * (dp - jnp.sum(p * dp, -1, keepdims=True))).astype(BF)
            dv_ref[0:span, :] += mm_rows(p.astype(BF), gh)
            dk_ref[0:span, :] += mm_rows(ds, qh)
            outs.append(mm(ds, keys[:span]))
        dq = jnp.where(first, outs[0], outs[1]) * scale
        d_ref[pl.ds(starts[j], size), pl.ds(pl.multiple_of(at * 128, 128), 128)] = dq.astype(BF)
    for j in range(4):
        rows = slice(j * size, (j + 1) * size)
        d_ref[pl.ds(starts[j], size), pl.ds(pl.multiple_of((at + pairs) * 128, 128), 128)] = (
            dk_ref[rows, :] * scale
        ).astype(BF)
        d_ref[pl.ds(starts[j], size), pl.ds(pl.multiple_of((at + 2 * pairs) * 128, 128), 128)] = (
            dv_ref[rows, :].astype(BF)
        )


def attn_bwd(z, qkv, grad, scale):
    rows, width = qkv.shape
    pairs = width // 3 // 128
    return pl.pallas_call(
        functools.partial(attn_bwd_kernel, scale=scale, pairs=pairs),
        grid=(pairs,),
        out_shape=jax.ShapeDtypeStruct((rows, width), BF),
        in_specs=[
            pl.BlockSpec(memory_space=pltpu.SMEM),
            pl.BlockSpec((rows, 128), lambda i: (0, i)),
            pl.BlockSpec((rows, 128), lambda i: (0, pairs + i)),
            pl.BlockSpec((rows, 128), lambda i: (0, 2 * pairs + i)),
            pl.BlockSpec((rows, 128), lambda i: (0, i)),
        ],
        out_specs=pl.BlockSpec((rows, width), lambda i: (0, 0)),
        scratch_shapes=[pltpu.VMEM((rows, 128), F32), pltpu.VMEM((rows, 128), F32)],
        compiler_params=pltpu.CompilerParams(vmem_limit_bytes=32 * 2**20),
        cost_estimate=pl.CostEstimate(
            flops=10 * rows * rows * width // 3,
            bytes_accessed=rows * width * 5,
            transcendentals=rows * rows * pairs * 2,
        ),
    )(z, qkv, qkv, qkv, grad)


def cross_probs(q, keys, lanes, seen, scale):
    qh = jnp.where(lanes, q, jnp.zeros_like(q))
    s = jnp.where(seen, mm_cols(qh, keys) * scale, NEG)
    p = jnp.where(seen, jnp.exp(s - jnp.max(s, -1, keepdims=True)), 0.0)
    return qh, p / jnp.sum(p, -1, keepdims=True)


def cross_fwd_kernel(cap_ref, seg_ref, q_ref, k_ref, v_ref, o_ref, *, scale):
    seen = seg_ref[...] == cap_ref[0]
    q, keys, values = q_ref[...], k_ref[...], v_ref[...]
    first = lax.broadcasted_iota(jnp.int32, q.shape, 1) < 64
    outs = []
    for head in range(2):
        _, p = cross_probs(q, keys, first if head == 0 else ~first, seen, scale)
        outs.append(mm(p.astype(BF), values))
    o_ref[...] = jnp.where(first, outs[0], outs[1]).astype(BF)


def cross_fwd(cap, seg, cq, ckv, scale):
    rows, width = cq.shape
    text = ckv.shape[0]
    pairs = width // 128
    return pl.pallas_call(
        functools.partial(cross_fwd_kernel, scale=scale),
        grid=(pairs,),
        out_shape=jax.ShapeDtypeStruct((rows, width), BF),
        in_specs=[
            pl.BlockSpec(memory_space=pltpu.SMEM),
            pl.BlockSpec((1, text), lambda i: (0, 0)),
            pl.BlockSpec((rows, 128), lambda i: (0, i)),
            pl.BlockSpec((text, 128), lambda i: (0, i)),
            pl.BlockSpec((text, 128), lambda i: (0, pairs + i)),
        ],
        out_specs=pl.BlockSpec((rows, 128), lambda i: (0, i)),
        compiler_params=pltpu.CompilerParams(vmem_limit_bytes=32 * 2**20),
        cost_estimate=pl.CostEstimate(
            flops=4 * rows * text * width,
            bytes_accessed=rows * width * 4,
            transcendentals=rows * text * pairs * 2,
        ),
    )(cap, seg, cq, ckv, ckv)


def cross_bwd_kernel(cap_ref, seg_ref, q_ref, k_ref, v_ref, g_ref, dq_ref, dk_ref, dv_ref, *, scale):
    seen = seg_ref[...] == cap_ref[0]
    q, keys, values, grad = q_ref[...], k_ref[...], v_ref[...], g_ref[...]
    first = lax.broadcasted_iota(jnp.int32, q.shape, 1) < 64
    outs = []
    for head in range(2):
        lanes = first if head == 0 else ~first
        qh, p = cross_probs(q, keys, lanes, seen, scale)
        gh = jnp.where(lanes, grad, jnp.zeros_like(grad))
        dp = mm_cols(gh, values)
        ds = (p * (dp - jnp.sum(p * dp, -1, keepdims=True))).astype(BF)
        dv = mm_rows(p.astype(BF), gh)
        dk = mm_rows(ds, qh) * scale
        if head == 0:
            dv_ref[...] = dv
            dk_ref[...] = dk
        else:
            dv_ref[...] += dv
            dk_ref[...] += dk
        outs.append(mm(ds, keys))
    dq_ref[...] = (jnp.where(first, outs[0], outs[1]) * scale).astype(BF)


def cross_bwd(cap, seg, cq, ckv, grad, scale):
    rows, width = cq.shape
    text = ckv.shape[0]
    pairs = width // 128
    return pl.pallas_call(
        functools.partial(cross_bwd_kernel, scale=scale),
        grid=(pairs,),
        out_shape=[
            jax.ShapeDtypeStruct((rows, width), BF),
            jax.ShapeDtypeStruct((text, width), F32),
            jax.ShapeDtypeStruct((text, width), F32),
        ],
        in_specs=[
            pl.BlockSpec(memory_space=pltpu.SMEM),
            pl.BlockSpec((1, text), lambda i: (0, 0)),
            pl.BlockSpec((rows, 128), lambda i: (0, i)),
            pl.BlockSpec((text, 128), lambda i: (0, i)),
            pl.BlockSpec((text, 128), lambda i: (0, pairs + i)),
            pl.BlockSpec((rows, 128), lambda i: (0, i)),
        ],
        out_specs=[
            pl.BlockSpec((rows, 128), lambda i: (0, i)),
            pl.BlockSpec((text, 128), lambda i: (0, i)),
            pl.BlockSpec((text, 128), lambda i: (0, i)),
        ],
        compiler_params=pltpu.CompilerParams(vmem_limit_bytes=32 * 2**20),
        cost_estimate=pl.CostEstimate(
            flops=10 * rows * text * width,
            bytes_accessed=rows * width * 6,
            transcendentals=rows * text * pairs * 2,
        ),
    )(cap, seg, cq, ckv, ckv, grad)


def long_masks(g, rows):
    slot = jnp.arange(rows, dtype=jnp.int32) // (2 * STRIPE)
    rest = jnp.arange(rows, dtype=jnp.int32) % (2 * STRIPE)

    def positions(r):
        return ((g.z ^ slot) * g.t + r) * (2 * STRIPE) + rest

    key_pos = jnp.concatenate([positions((g.r - q) % g.t) for q in range(g.t)])
    return key_pos[None, :] <= positions(g.r)[:, None]


def long_gather(g, value):
    return jnp.concatenate([value] + [g.over_r(value, q) for q in range(1, g.t)], 0)


def long_fwd(g, qkv, scale):
    rows, width = qkv.shape
    head = 64
    heads = width // 3 // head
    keyval = long_gather(g, qkv[:, width // 3 :])
    q = qkv[:, : width // 3].reshape(rows, heads, head)
    k = keyval[:, : width // 3].reshape(-1, heads, head)
    v = keyval[:, width // 3 :].reshape(-1, heads, head)
    seen = long_masks(g, rows)[None]
    s = jnp.einsum("qhd,khd->hqk", q, k, preferred_element_type=F32) * scale
    s = jnp.where(seen, s, NEG)
    p = jnp.exp(s - jnp.max(s, -1, keepdims=True))
    p = p / jnp.sum(p, -1, keepdims=True)
    out = jnp.einsum("hqk,khd->qhd", p.astype(BF), v, preferred_element_type=F32)
    return out.reshape(rows, width // 3).astype(BF), (q, k, v, p)


def long_bwd(g, saved, grad, scale):
    q, k, v, p = saved
    rows, heads, head = q.shape
    width = heads * head
    grad = grad.reshape(rows, heads, head)
    dv = jnp.einsum("hqk,qhd->khd", p.astype(BF), grad, preferred_element_type=F32)
    dp = jnp.einsum("qhd,khd->hqk", grad, v, preferred_element_type=F32)
    ds = (p * (dp - jnp.sum(p * dp, -1, keepdims=True))).astype(BF)
    dq = jnp.einsum("hqk,khd->qhd", ds, k, preferred_element_type=F32) * scale
    dk = jnp.einsum("hqk,qhd->khd", ds, q, preferred_element_type=F32) * scale
    both = jnp.concatenate([dk.reshape(-1, width), dv.reshape(-1, width)], 1)
    both = both.reshape(g.t, rows, 2 * width)
    total = both[0]
    for step in range(1, g.t):
        total = total + g.over_r(both[step], -step)
    return jnp.concatenate([dq.reshape(rows, width).astype(BF), total.astype(BF)], 1)


def normed(values):
    center = values - jnp.mean(values, -1, keepdims=True)
    spread = lax.rsqrt(jnp.mean(center * center, -1, keepdims=True) + EPS)
    return center * spread, spread


def norm_back(unit, spread, gain, grad):
    f = grad * gain
    added = spread * (
        f - jnp.mean(f, -1, keepdims=True) - unit * jnp.mean(f * unit, -1, keepdims=True)
    )
    return added, jnp.sum(grad * unit, 0), jnp.sum(grad, 0)


def column_halves(weight, groups, mine):
    rows, width = weight.shape
    parts = weight.reshape(rows, groups, 2, width // groups // 2)
    return (
        pick(parts, 2, mine).reshape(rows, width // 2),
        pick(parts, 2, 1 - mine).reshape(rows, width // 2),
    )


def two(g, mine, other, axis):
    first = jnp.where(g.c == 0, mine, other)
    second = jnp.where(g.c == 0, other, mine)
    return jnp.stack([first, second], axis)


def gather_fast(g, scal, weights, ids, tokens, cotangent):
    gains, shifts, w_qkv, w_out, w_cq, w_ckv, w_co, w_up, w_down = weights
    share, depth = w_co.shape
    tall = w_down.shape[0]
    small = jnp.concatenate([gains, shifts], 0).T
    small = jnp.pad(small, ((0, 0), (0, 128 - small.shape[1])))
    keep1, send1 = prep_weights(scal, [(w_qkv, 6), (small, 0), (w_cq, 2)])
    keep2, send2 = prep_weights(scal, [(w_ckv, 4)], w_out)
    keep3, send3 = prep_weights(scal, [(w_up, 2)])
    blocks = prep_tokens(scal, ids, tokens, cotangent)
    got1 = g.over_c(send1)
    got2 = g.over_c(jnp.concatenate([send2, send3], 1))

    def shape(kinds, rows, width):
        return (2, kinds, 4, 2, rows, width)

    n_qkv, n_cq, n_ckv, n_up = (w.shape[1] // 2 for w in (w_qkv, w_cq, w_ckv, w_up))
    groups = tall // share // 2
    low, high = (
        list(half.reshape(groups, share, depth))
        for half in (w_down[: tall // 2], w_down[tall // 2 :])
    )
    second = jnp.stack([keep2, jnp.concatenate([got2[:, :n_ckv], w_co], 1)])
    third = jnp.stack(
        [jnp.concatenate([keep3] + low, 1), jnp.concatenate([got2[:, n_ckv:]] + high, 1)]
    )
    first = after(jnp.stack([keep1, got1]), second, third)
    third_low, third_high = third[:1], third[1:]
    tok, cot = list(blocks[:4]), list(blocks[4:])

    near, far = g.gather_near, g.gather_far

    got_a = [first] + [g.xor_z(first, k) for k in (1, 2, 3)]
    tok[0], cot[0] = g.regroup(tok[0], 0), g.regroup(cot[0], 0)
    line_a = gather_line(scal, got_a)

    line_a, second, late = after((line_a, second, tok[3]), got_a, tok[0], cot[0])
    near_a = near(line_a)
    got_b = [second] + [g.xor_z(second, k) for k in (1, 2)]
    tok[3] = g.regroup(late, 3)

    near_a, second, third, third_low = after((near_a, second, third, third_low), got_b, tok[3])
    far_a = far(line_a, near_a)
    got_b.append(g.xor_z(second, 3))
    got_c1 = g.xor_z(third, 1)
    got_c2 = g.xor_z(third_low, 2)
    line_b = gather_line(scal, got_b)

    line_b, third_high, *late = after((line_b, third_high, *tok[1:3]), far_a, got_c1, got_c2)
    near_b = near(line_b)
    got_c2 = jnp.concatenate([got_c2, g.xor_z(third_high, 2)], 0)
    tok[1:3] = [g.regroup(late[k - 1], k) for k in (1, 2)]

    near_b, third, tok = after((near_b, third, tok), got_c2)
    far_b = far(line_b, near_b)
    got_c = [third, got_c1, got_c2, g.xor_z(third, 3)]
    resid = join_tokens(scal, tok, g.over_c(jnp.stack(tok)))
    line_c = gather_line(scal, got_c)

    line_c, *late = after((line_c, *cot[1:]), far_b)
    near_c = near(line_c)
    cot[1:] = [g.regroup(late[k - 1], k) for k in (1, 2, 3)]

    near_c, cot = after((near_c, cot))
    far_c = far(line_c, near_c)
    cot = join_tokens(scal, cot, g.over_c(jnp.stack(cot)))

    qkv, small, cq = gather_place(
        scal,
        *far_a,
        [shape(2, share, n_qkv), shape(2, share, 128), shape(2, share, n_cq)],
        [[(n_qkv, 0, None, 0), (128, 1, None, 0), (n_cq, 2, None, 0)]] * 2,
    )
    ckv, out, co = gather_place(
        scal,
        *far_b,
        [shape(2, share, n_ckv), shape(1, share, depth), shape(1, share, depth)],
        [[(n_ckv, 0, None, 0), (depth, 1 + half, 0, 0)] for half in range(2)],
    )

    def flat(array):
        return array.reshape(-1, array.shape[-1])

    def last(far_c):
        up, down = gather_place(
            scal,
            *far_c,
            [shape(2, share, n_up), shape(1, tall, depth)],
            [
                [(n_up, 0, None, 0)]
                + [(depth, 1, 0, (half * groups + i) * share) for i in range(groups)]
                for half in range(2)
            ],
        )
        return flat(up), flat(down)

    return (
        (resid, cot, far_c),
        last,
        flat(small)[:, :6].astype(F32).T,
    ) + tuple(flat(array) for array in (qkv, out, cq, ckv, co))


def gather_plain(g, weights):
    gains, shifts, w_qkv, w_out, w_cq, w_ckv, w_co, w_up, w_down = weights
    small = lax.all_gather(jnp.concatenate([gains, shifts], 0), AXES, axis=1, tiled=True)

    def columns(weight, groups):
        whole = lax.all_gather(weight, AXES, axis=0, tiled=True)
        return column_halves(whole, groups, g.c)[0]

    def rows(weight):
        whole = lax.all_gather(weight, AXES, axis=0, tiled=True)
        parts = whole.reshape(2, 2, whole.shape[0] // 4, whole.shape[1])
        return pick(parts, 1, g.c).reshape(whole.shape[0] // 2, whole.shape[1])

    return (
        small.astype(F32),
        columns(w_qkv, 6),
        rows(w_out),
        columns(w_cq, 2),
        columns(w_ckv, 4),
        rows(w_co),
        columns(w_up, 2),
        rows(w_down),
    )


def join_columns(g, keep, got, groups):
    rows, width = keep.shape
    block = width // groups
    parts = two(g, keep.reshape(rows, groups, block), got.reshape(rows, groups, block), 2)
    return parts.reshape(rows, 2 * width)


def scatter_columns_plain(g, grad, groups):
    rows, width = grad.shape
    whole = join_columns(g, grad, jnp.zeros_like(grad), groups)
    return lax.psum_scatter(whole, AXES, scatter_dimension=0, tiled=True)


def scatter_rows_plain(g, grad):
    rows, width = grad.shape
    parts = grad.reshape(2, rows // 2, width)
    whole = two(g, parts, jnp.zeros_like(parts), 1).reshape(2 * rows, width)
    return lax.psum_scatter(whole, AXES, scatter_dimension=0, tiled=True)


def both_cores(g, part):
    low = part.astype(BF)
    return low.astype(F32) + g.over_c(low).astype(F32)


def local(
    tokens,
    text_states,
    image_ids,
    text_segments,
    image_caption,
    norm_gains,
    norm_shifts,
    self_qkv,
    self_out,
    cross_query,
    cross_keyval,
    cross_out,
    mlp_up,
    mlp_down,
    cotangent,
    *,
    dp,
    seq,
):
    g = Grid(dp, seq)
    fast = g.t == 1
    depth = tokens.shape[-1]
    scale = (depth // H) ** (-0.5)
    weights = (
        norm_gains,
        norm_shifts,
        self_qkv,
        self_out,
        cross_query,
        cross_keyval,
        cross_out,
        mlp_up,
        mlp_down,
    )

    scal = jnp.stack([g.x, g.c, g.z, g.y]).astype(jnp.int32)
    start = image_ids[:, 0] & 1
    if fast:
        ((resid, cot, far_c), place_last, small, w_qkv, w_out, w_cq, w_ckv, w_co) = gather_fast(
            g, scal, weights, image_ids, tokens, cotangent
        )
    else:
        (small, w_qkv, w_out, w_cq, w_ckv, w_co, w_up, w_down) = gather_plain(g, weights)
        both = jnp.stack([tokens, cotangent], 2).reshape(4, STRIPE, 2 * depth)
        received = []
        for step in range(4):
            j = g.z ^ step
            half = (j & 1) ^ start[j >> 1]
            received.append(g.regroup(pick(both, 0, (j >> 1) * 2 + half), step))
        mine = jnp.stack(received)
        held = two(g, mine, g.over_c(mine), 1).reshape(8 * STRIPE, 2, depth)
        resid, cot = held[:, 0], held[:, 1]
    resid = resid.astype(F32)
    gain, shift = small[:3], small[3:]

    image = (g.x * 2 + g.y) * 2 + (g.z & 1)
    cap = image_caption[g.z >> 1, image].reshape(1)
    seg = text_segments.reshape(1, -1)
    slot = g.z.reshape(1).astype(jnp.int32)

    unit_one, spread_one = normed(resid)
    n_one = (unit_one * gain[0] + shift[0]).astype(BF)
    qkv = mm(n_one, w_qkv).astype(BF)
    if fast:
        attended = attn_fwd(slot, qkv, scale)
    else:
        attended, saved = long_fwd(g, qkv, scale)
    hidden_one = resid + both_cores(g, mm(attended, w_out))
    unit_two, spread_two = normed(hidden_one)
    n_two = (unit_two * gain[1] + shift[1]).astype(BF)
    cq = mm(n_two, w_cq).astype(BF)
    ckv = mm(text_states, w_ckv).astype(BF)
    crossed = cross_fwd(cap, seg, cq, ckv, scale)
    hidden_two = hidden_one + both_cores(g, mm(crossed, w_co))
    unit_three, spread_three = normed(hidden_two)
    n_three = (unit_three * gain[2] + shift[2]).astype(BF)
    if fast:
        w_up, w_down = place_last(far_c)
    up = mm(n_three, w_up)
    inner = jnp.tanh(GELU_C * (up + 0.044715 * up * up * up))
    act = (0.5 * up * (1.0 + inner)).astype(BF)

    def halves(value):
        parts = value.reshape(4, 2, STRIPE, value.shape[-1])
        return pick(parts, 1, g.c), pick(parts, 1, 1 - g.c)

    down = mm(act, w_down)
    keep, gone = halves(down)

    def finish(gone):
        return (halves(hidden_two)[0] + keep + g.over_c(gone).astype(F32)).astype(BF)

    grad_down = mm_rows(act, cot)
    slope = 0.5 * (1.0 + inner) + 0.5 * up * (1.0 - inner * inner) * GELU_C * (
        1.0 + 3 * 0.044715 * up * up
    )
    d_up = (mm_cols(cot, w_down) * slope).astype(BF)
    grad_up = mm_rows(n_three, d_up)
    share = depth // g.count
    if fast:
        mlp = by_rows(grad_down.astype(BF), share) + by_columns(grad_up.astype(BF), share)
        mlp_far, gone = after((fold_far(scal, share, mlp), gone.astype(BF)))
        mlp_far = g.over_y(mlp_far[0]), g.over_x(mlp_far[1])
        out = finish(gone)
        out_home = [g.regroup(out[k], k) for k in range(4)]
    else:
        out = finish(gone.astype(BF))
    added, gain_three, shift_three = norm_back(
        unit_three, spread_three, gain[2], both_cores(g, mm_cols(d_up, w_up))
    )
    g_two = cot.astype(F32) + added
    d_cross = g_two.astype(BF)
    grad_co = mm_rows(crossed, d_cross)
    d_crossed = mm_cols(d_cross, w_co).astype(BF)
    d_cq, d_ck, d_cv = cross_bwd(cap, seg, cq, ckv, d_crossed, scale)
    grad_cq = mm_rows(n_two, d_cq)
    if fast:
        cross = by_rows(grad_co.astype(BF), share) + by_columns(grad_cq.astype(BF), share)
        d_ckv = jnp.concatenate([d_ck, d_cv], 1).astype(BF)
    added, gain_two, shift_two = norm_back(
        unit_two, spread_two, gain[1], both_cores(g, mm_cols(d_cq, w_cq))
    )
    g_one = g_two + added
    d_self = g_one.astype(BF)
    grad_out = mm_rows(attended, d_self)
    d_att = mm_cols(d_self, w_out).astype(BF)
    if fast:
        near_ready, cross_far, swapped = after(
            (
                fold_near(scal, share, [(mlp, mlp_far)]),
                fold_far(scal, share, cross),
                d_ckv,
            ),
            mlp_far,
            out_home,
        )
        mlp_near = g.over_x(near_ready[0]), g.over_y(near_ready[1])
        cross_far = g.over_y(cross_far[0]), g.over_x(cross_far[1])
        d_ckv = swapped
        swapped = g.xor_z(swapped, 1)
        d_qkv = attn_bwd(slot, qkv, after(d_att, near_ready), scale)
        d_ckv = plus(d_ckv, swapped)
        mlp_line = fold_line(scal, share, [(mlp, mlp_far, mlp_near)])
        swapped = g.xor_z(d_ckv, 2)
        d_qkv = after(d_qkv, cross_far)
    else:
        d_qkv = long_bwd(g, saved, d_att, scale)
    grad_qkv = mm_rows(n_one, d_qkv)
    added, gain_one, shift_one = norm_back(
        unit_one, spread_one, gain[0], both_cores(g, mm_cols(d_qkv, w_qkv))
    )
    grad_in = (g_one + added).astype(BF)

    norms = jnp.stack([gain_one, gain_two, gain_three, shift_one, shift_two, shift_three])
    back = halves(grad_in)[0]
    if fast:
        last = by_rows(grad_out.astype(BF), share) + by_columns(grad_qkv.astype(BF), share)
        d_ckv = plus(d_ckv, swapped)
        last_far, mlp_line = after(
            (fold_far(scal, share, last), mlp_line), cross_far, mlp_near, swapped
        )
        last_far = g.over_y(last_far[0]), g.over_x(last_far[1])
        mlp_terms = [mlp_line[0]] + [g.xor_z(mlp_line[k], k) for k in (1, 2)]

        near_last = fold_near(scal, share, [(last, last_far)])
        near_cross = fold_near(scal, share, [(cross, cross_far)])
        near_last, near_cross, mlp_line, d_ckv, norms = after(
            (near_last, near_cross, mlp_line, d_ckv, norms), last_far, mlp_terms[1:]
        )
        near_last = g.over_x(near_last[0]), g.over_y(near_last[1])
        near_cross = g.over_x(near_cross[0]), g.over_y(near_cross[1])
        mlp_terms.append(g.xor_z(mlp_line[3], 3))
        d_ckv = plus(d_ckv, g.over_x(d_ckv))
        norms = norms + g.over_y(norms)

        line = fold_line(
            scal, share, [(last, last_far, near_last), (cross, cross_far, near_cross)]
        )
        line, back, mlp_terms, d_ckv, norms = after((line, back, mlp_terms, d_ckv, norms))
        terms = [line[0]] + [g.xor_z(line[k], k) for k in (1, 2, 3)]
        back = [g.regroup(back[k], k) for k in range(4)]
        mlp_terms = after(mlp_terms, back)
        d_ckv = plus(d_ckv, g.over_y(d_ckv))
        norms = after(norms + g.over_x(norms), terms)
        norms = norms + g.xor_z(norms, 1)
        norms = norms + g.xor_z(norms, 2)
        norms = lax.dynamic_slice_in_dim(norms, g.me * share, share, 1)
        output, grad_tokens = place_home(scal, image_ids, out_home, back)
        d_ckv_whole = join_columns(g, d_ckv, g.over_c(d_ckv), 4)
    else:
        back = jnp.concatenate([out, back], 2)
        back = jnp.stack([g.regroup(back[step], step) for step in range(4)])
        order = []
        for block in range(4):
            j = (block & 2) + ((block & 1) ^ start[block >> 1])
            order.append(pick(back, 0, j ^ g.z))
        back = jnp.stack(order).reshape(2, 2 * STRIPE, 2 * depth)
        output, grad_tokens = back[:, :, :depth], back[:, :, depth:].astype(F32)
        d_ckv = jnp.concatenate([d_ck, d_cv], 1)
        whole = join_columns(g, d_ckv, jnp.zeros_like(d_ckv), 4)
        d_ckv_whole = lax.psum(whole, AXES).astype(BF)
        d_ckv = column_halves(d_ckv_whole, 4, g.c)[0]
        norms = lax.psum(norms, AXES) * 0.5
        norms = lax.dynamic_slice_in_dim(norms, g.me * (depth // g.count), depth // g.count, 1)
    part = mm_cols(d_ckv, w_ckv)
    grad_text = part + g.over_c(part)
    text_cols = lax.dynamic_slice_in_dim(text_states, g.me * share, share, 1)
    grad_ckv = mm_rows(text_cols, d_ckv_whole)
    if fast:
        tall = mlp_down.shape[0]

        def columns(terms, low, high, groups):
            got = g.over_c(plus(*[pick(term, 0, 1 - g.c)[:, low:high] for term in terms]))
            keep = sum(pick(term, 0, g.c)[:, low:high].astype(F32) for term in terms)
            return join_columns(g, keep, got.astype(F32), groups)

        n_down = tall // share // 2 * depth
        grad_down = summed(mlp_terms, ALL, ALL, slice(0, n_down))
        grad_down = grad_down.reshape(2, share, tall // share // 2, depth)
        grad_down = grad_down.transpose(0, 2, 1, 3).reshape(tall, depth)
        grad_up = columns(mlp_terms, n_down, None, 2)
        half = depth // 2
        to_qkv = half + grad_qkv.shape[1]

        def halves_of(start):
            total = summed(terms, ALL, ALL, slice(start, start + half))
            return jnp.concatenate([total[0], total[1]], 1)

        grad_out = halves_of(0)
        grad_qkv = columns(terms, half, to_qkv, 6)
        grad_co = halves_of(to_qkv)
        grad_cq = columns(terms, to_qkv + half, None, 2)
    else:
        grad_down = scatter_rows_plain(g, grad_down)
        grad_up = scatter_columns_plain(g, grad_up, 2)
        grad_co = scatter_rows_plain(g, grad_co)
        grad_cq = scatter_columns_plain(g, grad_cq, 2)
        grad_out = scatter_rows_plain(g, grad_out)
        grad_qkv = scatter_columns_plain(g, grad_qkv, 6)
    return (
        output,
        grad_tokens,
        grad_text,
        norms[:3],
        norms[3:5],
        grad_qkv,
        grad_out,
        grad_cq,
        grad_ckv,
        grad_co,
        grad_up,
        grad_down,
        norms[5],
    )


def solution(mesh):
    both = ("dp", "seq")
    rows = P(both, None)
    in_specs = (
        P(None, both, None),
        P(),
        P(None, both),
        P(),
        P(),
        P(None, both),
        P(None, both),
        rows,
        rows,
        rows,
        rows,
        rows,
        rows,
        rows,
        P(None, both, None),
    )
    out_specs = (
        P(None, both, None),
        P(None, both, None),
        P(),
        P(None, both),
        P(None, both),
        rows,
        rows,
        rows,
        rows,
        rows,
        rows,
        rows,
        P(both),
    )
    body = functools.partial(local, dp=mesh.shape["dp"], seq=mesh.shape["seq"])
    return jax.shard_map(body, mesh=mesh, in_specs=in_specs, out_specs=out_specs, check_vma=False)
```
